32 devices in a mesh: dp: 4 (over y, x), tensor: 8 (over z, core).
Axes of the slice: x: 2, y: 2, z: 4, core: 2. Of those that a mesh axis runs over, the one named last changes fastest.
Arguments:
- features: bfloat16 [1024, 18432], P('tensor', 'dp'), may hold values from -6 to 6
- slot_live: int32 [32], P('dp'), may hold values 0 or 1
- position: float32 [24, 24, 1024], P(None, None, 'tensor'), may hold values from -3 to 3
- gain_outer: float32 [1024], P('tensor'), may hold values from 0.1 to 1.9
- reduce_weight: bfloat16 [1024, 256], P(None, 'tensor'), may hold values from -0.1875 to 0.1875
- gain_middle: float32 [256], P('tensor'), may hold values from 0.1 to 1.9
- conv_weight: bfloat16 [3, 3, 256, 256], P(None, None, None, 'tensor'), may hold values from -0.125 to 0.125
- gain_inner: float32 [256], P('tensor'), may hold values from 0.1 to 1.9
- expand_weight: bfloat16 [256, 1024], P('tensor'), may hold values from -0.5 to 0.5
- readout_weight: bfloat16 [4096, 1024], P('tensor'), may hold values from -0.25 to 0.25
- cotangent: bfloat16 [4096, 4608], P('tensor', 'dp'), may hold values from -6 to 6
Outputs:
- readout: bfloat16 [4096, 4608], P('tensor', 'dp')
- grad_features: float32 [1024, 18432], P('tensor', 'dp')
- grad_position: float32 [24, 24, 1024], P(None, None, 'tensor')
- grad_gain_outer: float32 [1024], P('tensor')
- grad_reduce: float32 [1024, 256], P(None, 'tensor')
- grad_gain_middle: float32 [256], P('tensor')
- grad_conv: float32 [3, 3, 256, 256], P(None, None, None, 'tensor')
- grad_gain_inner: float32 [256], P('tensor')
- grad_expand: float32 [256, 1024], P('tensor')
- grad_readout: float32 [4096, 1024], P('tensor')
The draws below stay inside these ranges and needn't reach their ends.
All inputs are finite; a program needn't handle non-finite values. No bound on the sum of `slot_live` on one device may be relied on, other than what follows from the above.
Results may differ from the reference program's by a relative error of at most 0.015.
Values may be sent and summed in bfloat16 or wider, within the bound.
A program may use at most 192 MiB of HBM per device.

```python
import jax
import jax.numpy as jnp
from jax import lax

C = 1024
H = 256
RO = 4096
GRID = 24
POOL = 12
IMAGES = 32


def set_ends(entries, rng, low, largest):
    longest = entries.shape.index(max(entries.shape))
    spots = []
    for shift in (0, 1):
        where = [jax.random.randint(jax.random.fold_in(rng, axis), (), 0, length) for axis, length in enumerate(entries.shape)]
        where[longest] = (where[longest] + shift) % entries.shape[longest]
        spots.append(tuple(where))
    return entries.at[spots[0]].set(low).at[spots[1]].set(largest)


def steps_of(own_key, shape, pieces, least, top_value):
    loudness = 1.0
    for axis_at, parts in pieces:
        steps = jax.random.uniform(jax.random.fold_in(jax.random.fold_in(own_key, 6), axis_at), (parts,), jnp.float32, least / len(pieces), top_value / len(pieces))
        loudness = loudness * jnp.repeat(jnp.exp(steps), shape[axis_at] // parts).reshape((-1,) + (1,) * (len(shape) - 1 - axis_at))
    return loudness


def centred(own_key, shape, width, limit, pieces=(), dtype=jnp.bfloat16):
    array = jax.random.normal(own_key, shape, jnp.float32) * width
    if len(pieces) > 0:
        array = steps_of(own_key, shape, pieces, -0.22, 0.18) * array
    return jnp.clip(array, min=-limit, max=limit).astype(dtype)


def setup_inputs(seed: int = 0) -> dict:
    streams_of = jax.random.split(jax.random.key(seed), 12)
    return {
        "features": centred(streams_of[0], (C, IMAGES * GRID * GRID), 1.0, 6.0, ((0, 8), (1, 4))),
        "slot_live": set_ends((jax.random.randint(streams_of[1], (IMAGES,), 0, 4) < 3).astype(jnp.int32), jax.random.fold_in(streams_of[1], 1), 0, 1),
        "position": centred(streams_of[2], (GRID, GRID, C), 0.5, 3.0, ((2, 8),), jnp.float32),
        "gain_outer": jnp.clip(1.0 + 0.18 * jax.random.normal(streams_of[3], (C,), jnp.float32), 0.1, 1.9),
        "reduce_weight": centred(streams_of[4], (C, H), C ** -0.5, 0.1875, ((1, 8),)),
        "gain_middle": jnp.clip(1.0 + 0.18 * jax.random.normal(streams_of[5], (H,), jnp.float32), 0.1, 1.9),
        "conv_weight": centred(streams_of[6], (3, 3, H, H), (9 * H) ** -0.5, 0.125, ((3, 8),)),
        "gain_inner": jnp.clip(1.0 + 0.18 * jax.random.normal(streams_of[7], (H,), jnp.float32), 0.1, 1.9),
        "expand_weight": centred(streams_of[8], (H, C), (H // 2) ** -0.5, 0.5, ((0, 8),)),
        "readout_weight": centred(streams_of[9], (RO, C), (C // 2) ** -0.5, 0.25, ((0, 8),)),
        "cotangent": centred(streams_of[10], (RO, IMAGES * POOL * POOL), 1.0, 6.0, ((0, 8), (1, 4))),
    }


epsilon = 1e-05

@jax.custom_vjp
def low(v):
    return lax.optimization_barrier(v.astype(jnp.bfloat16)).astype(jnp.float32)

@jax.custom_vjp
def low_back(v):
    return v

def low_keep(v):
    return (low(v), None)

def low_pass(kept, grad):
    return (grad,)

def back_keep(v):
    return (v, None)

def back_low(kept, grad):
    return (low(grad),)
low.defvjp(low_keep, low_pass)
low_back.defvjp(back_keep, back_low)

def norm_rows(values, norm_gain):
    center = lax.optimization_barrier(jnp.mean(values, axis=-1, keepdims=True))
    shifted = values - center
    spread = lax.optimization_barrier(jnp.mean(shifted * shifted, axis=-1, keepdims=True))
    return shifted * lax.rsqrt(spread + epsilon) * norm_gain

def reference(features, slot_live, position, gain_outer, reduce_weight, gain_middle, conv_weight, gain_inner, expand_weight, readout_weight, cotangent):
    highest = lax.Precision.HIGHEST
    live_mask = slot_live.astype(jnp.float32)[:, None, None, None]

    def forward(inputs, embed, gain_one, reduce_matrix, gain_two, conv_kernel, gain_three, expand_matrix, out_matrix):
        breadth = inputs.shape[0]
        count = inputs.shape[1] // (GRID * GRID)
        placed = inputs.T.reshape(count, GRID, GRID, breadth) + embed[None]
        reduce_in = low(norm_rows(placed, gain_one))
        reduced = low_back(jnp.einsum('nhwc,cd->nhwd', reduce_in, reduce_matrix, precision=highest))
        hidden = low(jax.nn.silu(norm_rows(reduced, gain_two)))
        convolved = low_back(lax.conv_general_dilated(hidden, conv_kernel, (1, 1), 'SAME', dimension_numbers=('NHWC', 'HWIO', 'NHWC'), precision=highest))
        activated = low(jax.nn.silu(norm_rows(convolved, gain_three)))
        expanded = low_back(jnp.einsum('nhwd,dc->nhwc', activated, expand_matrix, precision=highest))
        mixed = placed + live_mask * expanded
        half = GRID // 2
        pooled = low(lax.optimization_barrier(jnp.mean(mixed.reshape(count, half, 2, half, 2, breadth), axis=(2, 4))))
        before = low_back(jnp.einsum('nhwc,oc->nhwo', pooled, out_matrix, precision=highest))
        result = jax.nn.gelu(before, approximate=False)
        return result.reshape(count * half * half, out_matrix.shape[0]).T
    primals = (features.astype(jnp.float32), position, gain_outer, reduce_weight.astype(jnp.float32), gain_middle, conv_weight.astype(jnp.float32), gain_inner, expand_weight.astype(jnp.float32), readout_weight.astype(jnp.float32))
    output, pullback = jax.vjp(forward, *primals)
    grads = pullback(cotangent.astype(jnp.float32))
    return (output.astype(jnp.bfloat16), grads[0], grads[1], grads[2], grads[3], grads[4], grads[5], grads[6], grads[7], grads[8])
```

```python
import jax
import jax.numpy as jnp
from jax import lax
from jax.sharding import PartitionSpec as P

epsilon = 1e-05
bf16 = jnp.bfloat16
f32 = jnp.float32


def silu_grad(inputs):
    gate_value = jax.nn.sigmoid(inputs)
    return gate_value * (1.0 + inputs * (1.0 - gate_value))


def gelu_grad(inputs):
    below = 0.5 * (1.0 + lax.erf(inputs * 0.7071067811865476))
    density = jnp.exp(-0.5 * inputs * inputs) * 0.3989422804014327
    return below + inputs * density


def dot(a, b, ca, cb):
    return lax.dot_general(a, b, (((ca,), (cb,)), ((), ())), preferred_element_type=f32)


def shifted(grid_values, a, b, side):
    padded = jnp.pad(grid_values, ((1, 1), (1, 1), (0, 0)))
    return padded[a : a + side, b : b + side].reshape(side * side, -1)


def gather(x, axis):
    return lax.all_gather(x, "tensor", axis=axis, tiled=True)


def local_by_image(features, slot_live, position, gain_outer, reduce_weight, gain_middle, conv_weight, gain_inner, expand_weight, readout_weight, cotangent):
    side = position.shape[0]
    half = side // 2
    cells = half * half
    spots = side * side
    share = features.shape[0]
    rows = features.shape[1]
    images = rows // spots
    parts = lax.axis_size("tensor")
    me = lax.axis_index("tensor")
    channels = share * parts
    hs = reduce_weight.shape[1]
    hidden_width = hs * parts
    live = slot_live.astype(f32)

    w_mine = lax.all_to_all(reduce_weight, "tensor", split_axis=0, concat_axis=1, tiled=True)
    conv_full = gather(conv_weight, 3).reshape(9, hidden_width, hidden_width)
    expand_full = gather(expand_weight, 0)
    gm = gather(gain_middle, 0)
    gi = gather(gain_inner, 0)
    go = gain_outer[:, None]

    placed = (features.astype(f32).reshape(share, images, spots) + position.reshape(spots, share).T[:, None, :]).reshape(share, rows)
    m_mine = jnp.mean(placed, axis=0)
    centred = placed - m_mine
    q_mine = jnp.sum(centred * centred, axis=0)
    part = dot((centred * go).astype(bf16), w_mine, 0, 0)
    reduced0 = lax.psum_scatter(part.astype(bf16), "tensor", scatter_dimension=0, tiled=True).astype(f32)
    stats = lax.all_to_all(jnp.stack([m_mine, q_mine]), "tensor", split_axis=1, concat_axis=0, tiled=True).reshape(parts, 2, spots)
    m_t, q_t = stats[:, 0], stats[:, 1]
    colsum = gather(jnp.sum(w_mine.astype(f32) * go, axis=0)[None], 0)
    mean = jnp.mean(m_t, axis=0)
    dm = m_t - mean
    var = (jnp.sum(q_t, axis=0) + share * jnp.sum(dm * dm, axis=0)) / channels
    rstd = lax.rsqrt(var + epsilon)
    corr = lax.dot_general(dm, colsum, (((0,), (0,)), ((), ())), precision=lax.Precision.HIGHEST, preferred_element_type=f32)
    reduced = rstd[:, None] * (reduced0 + corr)

    def norm(v, g):
        c = jnp.mean(v, axis=1, keepdims=True)
        s = v - c
        r = lax.rsqrt(jnp.mean(s * s, axis=1, keepdims=True) + epsilon)
        return s * r, r, s * r * g

    xm, rm, zm = norm(reduced, gm)
    hidden = jax.nn.silu(zm).astype(bf16)
    hidden_grid = hidden.reshape(side, side, hidden_width)
    convolved = sum(dot(shifted(hidden_grid, t // 3, t % 3, side), conv_full[t], 1, 0) for t in range(9))
    xi, ri, zi = norm(convolved, gi)
    activated = jax.nn.silu(zi).astype(bf16)
    act_cells = jnp.mean(activated.astype(f32).reshape(half, 2, half, 2, hidden_width), axis=(1, 3)).reshape(cells, hidden_width)
    act_all = gather(act_cells.astype(bf16), 0)
    act_live = (act_all.astype(f32) * jnp.repeat(live, cells)[:, None]).astype(bf16)

    placed_cells = jnp.mean(placed.reshape(share, images, half, 2, half, 2), axis=(3, 5)).reshape(share, images * cells).T
    placed_pool = gather(placed_cells.astype(bf16), 1)
    pooled = (placed_pool.astype(f32) + dot(act_live, expand_full, 1, 0)).astype(bf16)
    before = dot(pooled, readout_weight, 1, 1)
    readout = jax.nn.gelu(before, approximate=False).astype(bf16).T
    grad_before = (cotangent.T.astype(f32) * gelu_grad(before)).astype(bf16)
    grad_readout = dot(grad_before, pooled, 0, 0)
    terms = dot(grad_before, readout_weight, 1, 0)
    act_terms = dot(terms.astype(bf16), expand_full, 1, 1)
    grad_act = lax.psum_scatter(act_terms.astype(bf16), "tensor", scatter_dimension=0, tiled=True).astype(f32)
    grad_act = grad_act * (0.25 * live[me])
    grad_pooled = lax.psum_scatter(terms.astype(bf16), "tensor", scatter_dimension=1, tiled=True)
    grad_expand = 1.0 * dot(act_live, grad_pooled, 0, 0)
    grad_expand = lax.all_to_all(grad_expand.astype(bf16), "tensor", split_axis=0, concat_axis=1, tiled=True)

    def norm_back(dy, xhat, r, g):
        dx = dy * g
        return r * (dx - jnp.mean(dx, axis=1, keepdims=True) - xhat * jnp.mean(dx * xhat, axis=1, keepdims=True)), jnp.sum(dy * xhat, axis=0)

    ga_rows = jnp.broadcast_to(grad_act.reshape(half, 1, half, 1, hidden_width), (half, 2, half, 2, hidden_width)).reshape(spots, hidden_width)
    gc, g_gi = norm_back(ga_rows * silu_grad(zi), xi, ri, gi)
    gc = gc.astype(bf16)
    gc_grid = gc.reshape(side, side, hidden_width)
    grad_conv = jnp.stack([dot(shifted(hidden_grid, t // 3, t % 3, side), gc, 0, 0) for t in range(9)])
    grad_hidden = sum(dot(shifted(gc_grid, 2 - t // 3, 2 - t % 3, side), conv_full[t], 1, 1) for t in range(9))
    gr, g_gm = norm_back(grad_hidden * silu_grad(zm), xm, rm, gm)
    gr = gr.astype(bf16)

    wg = jnp.sum(colsum, axis=0)
    s1 = dot(gr.astype(f32), wg[:, None], 1, 0)[:, 0] / channels
    s2 = jnp.sum(gr.astype(f32) * reduced, axis=1) / channels
    gr_all = gather(gr, 0)
    row_stats = gather(jnp.stack([mean, rstd, s1, s2]), 1)
    xhat = (placed - row_stats[0]) * row_stats[1]
    gn = dot(w_mine, gr_all, 1, 1)
    grad_in = row_stats[1] * (gn * go - row_stats[2] - xhat * row_stats[3])
    g_go = jnp.sum(gn * xhat, axis=1)
    grad_reduce = dot((xhat * go).astype(bf16), gr_all, 1, 0)
    grad_reduce = lax.all_to_all(grad_reduce.astype(bf16), "tensor", split_axis=1, concat_axis=0, tiled=True)
    spread = (0.25 * grad_pooled.astype(f32)).T.reshape(share, images, half, 1, half, 1)
    grad_features = jnp.broadcast_to(spread, (share, images, half, 2, half, 2)).reshape(share, rows) + grad_in
    grad_position = jnp.sum(grad_features.reshape(share, images, spots), axis=1).T.reshape(side, side, share)
    g_conv = lax.psum_scatter(grad_conv.astype(bf16), "tensor", scatter_dimension=2, tiled=True).reshape(conv_weight.shape)
    g_gm = lax.psum_scatter(g_gm.astype(f32), "tensor", scatter_dimension=0, tiled=True)
    g_gi = lax.psum_scatter(g_gi.astype(f32), "tensor", scatter_dimension=0, tiled=True)
    out = [grad_position, g_go, grad_reduce, g_gm, g_conv, g_gi, grad_expand, grad_readout]
    out = [lax.psum(o.astype(bf16), "dp").astype(f32) for o in out]
    return (readout, grad_features, *out)


def row_totals(leading, trailing):
    return lax.psum((leading, trailing), "tensor")


def norm_forward(values, norm_gain, breadth):
    totals, squares = row_totals(jnp.sum(values, axis=1), jnp.sum(values * values, axis=1))
    center = totals / breadth
    spread = squares / breadth - center * center
    scaled = lax.rsqrt(spread + epsilon)[:, None]
    normed = (values - center[:, None]) * scaled
    return (normed, scaled, normed * norm_gain)


def norm_backward(grad_out, normed, scaled, norm_gain, breadth):
    grad_normed = grad_out * norm_gain
    gain_grad = jnp.sum(grad_out * normed, axis=0)
    leading, trailing = row_totals(
        jnp.sum(grad_normed, axis=1), jnp.sum(grad_normed * normed, axis=1)
    )
    grad_in = scaled * (
        grad_normed - leading[:, None] / breadth - normed * (trailing[:, None] / breadth)
    )
    return (grad_in, gain_grad)


def silu_slope(inputs):
    gate_value = jax.nn.sigmoid(inputs)
    return gate_value * (1.0 + inputs * (1.0 - gate_value))


def gelu_slope(inputs):
    below = 0.5 * (1.0 + lax.erf(inputs * 0.7071067811865476))
    density = jnp.exp(-0.5 * inputs * inputs) * 0.3989422804014327
    return below + inputs * density


def contract_rows(left_side, right_side):
    return lax.dot_general(
        left_side, right_side, (((0,), (0,)), ((), ())), preferred_element_type=jnp.float32
    )


def window_of(padded, shift_down, shift_across, grid_side):
    images = padded.shape[0]
    breadth = padded.shape[3]
    return padded[
        :, shift_down : shift_down + grid_side, shift_across : shift_across + grid_side, :
    ].reshape(images * grid_side * grid_side, breadth)


def local_by_hidden(
    features,
    slot_live,
    position,
    gain_outer,
    reduce_weight,
    gain_middle,
    conv_weight,
    gain_inner,
    expand_weight,
    readout_weight,
    cotangent,
):
    grid_side = position.shape[0]
    half_side = grid_side // 2
    channel_share = features.shape[0]
    row_count = features.shape[1]
    images = row_count // (grid_side * grid_side)
    tensor_size = lax.axis_size("tensor")
    channels = channel_share * tensor_size
    hidden_share = reduce_weight.shape[1]
    hidden_width = hidden_share * tensor_size
    pooled_count = images * half_side * half_side
    placed = (
        features.T.astype(jnp.float32).reshape(images, grid_side * grid_side, channel_share)
        + position.reshape(1, grid_side * grid_side, channel_share)
    ).reshape(row_count, channel_share)
    live_rows = jnp.repeat(slot_live.astype(jnp.float32), grid_side * grid_side)[:, None]
    normed_outer, scaled_outer, shaped_outer = norm_forward(placed, gain_outer, channels)
    reduce_in = shaped_outer.astype(jnp.bfloat16)
    reduce_full = lax.all_gather(reduce_in, "tensor", axis=1, tiled=True)
    reduced = jnp.dot(reduce_full, reduce_weight, preferred_element_type=jnp.float32)
    normed_middle, scaled_middle, shaped_middle = norm_forward(reduced, gain_middle, hidden_width)
    hidden = jax.nn.silu(shaped_middle).astype(jnp.bfloat16)
    hidden_full = lax.all_gather(hidden, "tensor", axis=1, tiled=True)
    padded_hidden = jnp.pad(
        hidden_full.reshape(images, grid_side, grid_side, hidden_width),
        ((0, 0), (1, 1), (1, 1), (0, 0)),
    )
    convolved = jnp.zeros((row_count, hidden_share), jnp.float32)
    for offset_tap in range(9):
        shift_down = offset_tap // 3
        shift_across = offset_tap % 3
        convolved = convolved + jnp.dot(
            window_of(padded_hidden, shift_down, shift_across, grid_side),
            conv_weight[shift_down, shift_across],
            preferred_element_type=jnp.float32,
        )
    normed_inner, scaled_inner, shaped_inner = norm_forward(convolved, gain_inner, hidden_width)
    activated = jax.nn.silu(shaped_inner).astype(jnp.bfloat16)
    expand_terms = jnp.dot(activated, expand_weight, preferred_element_type=jnp.float32)
    expanded = lax.psum_scatter(expand_terms, "tensor", scatter_dimension=1, tiled=True)
    mixed = placed + live_rows * expanded
    pooled = jnp.mean(mixed.reshape(images, half_side, 2, half_side, 2, channel_share), axis=(2, 4))
    pooled_low = pooled.reshape(pooled_count, channel_share).astype(jnp.bfloat16)
    pooled_full = lax.all_gather(pooled_low, "tensor", axis=1, tiled=True)
    before = lax.dot_general(
        pooled_full, readout_weight, (((1,), (1,)), ((), ())), preferred_element_type=jnp.float32
    )
    readout = jax.nn.gelu(before, approximate=False).astype(jnp.bfloat16).T
    grad_before = (cotangent.T.astype(jnp.float32) * gelu_slope(before)).astype(jnp.bfloat16)
    grad_readout = contract_rows(grad_before, pooled_full)
    pooled_terms = jnp.dot(grad_before, readout_weight, preferred_element_type=jnp.float32)
    grad_pooled = lax.psum_scatter(pooled_terms, "tensor", scatter_dimension=1, tiled=True)
    spread_grad = jnp.broadcast_to(
        (0.25 * grad_pooled).reshape(images, half_side, 1, half_side, 1, channel_share),
        (images, half_side, 2, half_side, 2, channel_share),
    )
    grad_mixed = spread_grad.reshape(row_count, channel_share)
    grad_branch = (live_rows * grad_mixed).astype(jnp.bfloat16)
    grad_full = lax.all_gather(grad_branch, "tensor", axis=1, tiled=True)
    grad_expand = contract_rows(activated, grad_full)
    grad_activated = jnp.dot(grad_full, expand_weight.T, preferred_element_type=jnp.float32)
    grad_convolved, grad_gain_inner = norm_backward(
        grad_activated * silu_slope(shaped_inner),
        normed_inner,
        scaled_inner,
        gain_inner,
        hidden_width,
    )
    grad_conv_low = grad_convolved.astype(jnp.bfloat16)
    tap_grads = []
    grad_padded = jnp.zeros((images, grid_side + 2, grid_side + 2, hidden_width), jnp.float32)
    for offset_tap in range(9):
        shift_down = offset_tap // 3
        shift_across = offset_tap % 3
        tap_grads.append(
            contract_rows(
                window_of(padded_hidden, shift_down, shift_across, grid_side), grad_conv_low
            )
        )
        tap_back = jnp.dot(
            grad_conv_low,
            conv_weight[shift_down, shift_across].T,
            preferred_element_type=jnp.float32,
        )
        grad_padded = grad_padded + jnp.pad(
            tap_back.reshape(images, grid_side, grid_side, hidden_width),
            ((0, 0), (shift_down, 2 - shift_down), (shift_across, 2 - shift_across), (0, 0)),
        )
    grad_conv = jnp.stack(tap_grads, axis=0).reshape(conv_weight.shape)
    grad_window = grad_padded[:, 1 : grid_side + 1, 1 : grid_side + 1, :].reshape(
        row_count, hidden_width
    )
    grad_hidden = lax.psum_scatter(grad_window, "tensor", scatter_dimension=1, tiled=True)
    grad_reduced, grad_gain_middle = norm_backward(
        grad_hidden * silu_slope(shaped_middle),
        normed_middle,
        scaled_middle,
        gain_middle,
        hidden_width,
    )
    grad_reduced_low = grad_reduced.astype(jnp.bfloat16)
    grad_reduce = contract_rows(reduce_full, grad_reduced_low)
    outer_terms = jnp.dot(grad_reduced_low, reduce_weight.T, preferred_element_type=jnp.float32)
    grad_shaped_outer = lax.psum_scatter(outer_terms, "tensor", scatter_dimension=1, tiled=True)
    grad_inputs, grad_gain_outer = norm_backward(
        grad_shaped_outer, normed_outer, scaled_outer, gain_outer, channels
    )
    grad_rows = grad_mixed + grad_inputs
    grad_place = jnp.sum(grad_rows.reshape(images, grid_side, grid_side, channel_share), axis=0)
    grad_total = grad_rows.T
    summed = (
        lax.psum(grad_place.astype(jnp.bfloat16), "dp").astype(jnp.float32),
        lax.psum(grad_gain_outer.astype(jnp.bfloat16), "dp").astype(jnp.float32),
        lax.psum(grad_reduce.astype(jnp.bfloat16), "dp").astype(jnp.float32),
        lax.psum(grad_gain_middle.astype(jnp.bfloat16), "dp").astype(jnp.float32),
        lax.psum(grad_conv.astype(jnp.bfloat16), "dp").astype(jnp.float32),
        lax.psum(grad_gain_inner.astype(jnp.bfloat16), "dp").astype(jnp.float32),
        lax.psum(grad_expand.astype(jnp.bfloat16), "dp").astype(jnp.float32),
        lax.psum(grad_readout.astype(jnp.bfloat16), "dp").astype(jnp.float32),
    )
    return (
        readout,
        grad_total,
        summed[0],
        summed[1],
        summed[2],
        summed[3],
        summed[4],
        summed[5],
        summed[6],
        summed[7],
    )


def solution(mesh):
    parts, groups = mesh.shape["tensor"], mesh.shape["dp"]
    specs = (P("tensor", "dp"), P("dp"), P(None, None, "tensor"), P("tensor"), P(None, "tensor"), P("tensor"), P(None, None, None, "tensor"), P("tensor"), P("tensor", None), P("tensor", None), P("tensor", "dp"))

    def whole(*arrays):
        by_image = arrays[1].shape[0] == parts * groups
        return jax.shard_map(
            local_by_image if by_image else local_by_hidden, mesh=mesh, in_specs=specs,
            out_specs=(P("tensor", "dp"), P("tensor", "dp"), *specs[2:10]), check_vma=False,
        )(*arrays)

    return whole
```

```python
import jax
import jax.numpy as jnp
from jax import lax
from jax.experimental import pallas as pl
from jax.experimental.pallas import tpu as pltpu
from jax.sharding import PartitionSpec as P

epsilon = 1e-05
bf16 = jnp.bfloat16
f32 = jnp.float32
COPIES = 112

MESH = pl.DeviceIdType.MESH
HIGHEST = lax.Precision.HIGHEST


def mm(a, b, ca, cb, precision=None):
    return lax.dot_general(a, b, (((ca,), (cb,)), ((), ())), precision=precision, preferred_element_type=f32)


def split(x):
    high = x.astype(bf16)
    return high, (x - high.astype(f32)).astype(bf16)


def eye(n, dtype=bf16):
    return (lax.broadcasted_iota(jnp.int32, (n, n), 0) == lax.broadcasted_iota(jnp.int32, (n, n), 1)).astype(f32).astype(dtype)


def pool_wide():
    spot = lax.broadcasted_iota(jnp.int32, (144, 768), 1)
    cell = lax.broadcasted_iota(jnp.int32, (144, 768), 0)
    i, j = spot >> 5, spot & 31
    return jnp.where(((i >> 1) * 12 + (j >> 1) == cell) & (j < 24), 0.25, 0.0).astype(bf16)


def pool_pair():
    spot = lax.broadcasted_iota(jnp.int32, (288, 1152), 1)
    cell = lax.broadcasted_iota(jnp.int32, (288, 1152), 0)
    i = (spot * 2731) >> 16
    j = spot - i * 24
    return jnp.where((i >> 1) * 12 + (j >> 1) == cell, 0.25, 0.0).astype(bf16)


def norm_rows(v):
    s = v - jnp.mean(v, axis=1, keepdims=True)
    r = lax.rsqrt(jnp.mean(s * s, axis=1, keepdims=True) + epsilon)
    return s * r, r


def norm_rows_back(dx, xhat, r):
    return r * (dx - jnp.mean(dx, axis=1, keepdims=True) - xhat * jnp.mean(dx * xhat, axis=1, keepdims=True))


def kernel(
    features, slot_live, position, gain_outer, reduce_weight, gain_middle, conv_weight, gain_inner, expand_weight, readout_weight, cotangent,
    readout_o, gfeat_o, gpos_o, gexp_o, gred_o, gconv_o, gread_o,
    WBLK, WT, WC, CB, WQ, WB, WF, MT, POOL, PLC, XW, XK, ST, SR, QF, QS, QO, QR, RED, HB, GB,
    XM, ZM, RM, XI, ZI, RI, ACT, ACL, PP, POOLED, BEF, GBT, TE, TR, ES, ER, GP, AT, AR, AS, AZ,
    GW, GA, RS, FT, TA, PM, CG, CGR, CGS, CGD, CGT, CGZ, CGF, GR, GRR, GRF, ssem, rsem,
):
    d = lax.axis_index("dp")
    t = lax.axis_index("tensor")
    z = t // 2
    c = t % 2
    sib = 2 * z + 1 - c
    count = [0]
    pending = []

    def send(src, dst, dd, tt):
        i = count[0]
        count[0] += 1
        cp = pltpu.make_async_remote_copy(
            src_ref=src, dst_ref=dst, send_sem=ssem.at[i], recv_sem=rsem.at[i], device_id=(dd, tt), device_id_type=MESH
        )
        cp.start()
        pending.append(cp)
        return cp

    def zpeer(k):
        return 2 * ((z + k) % 4) + c

    def dpeer(k):
        return (d + k) % 4

    barrier = pltpu.get_barrier_semaphore()
    for k in range(1, 8):
        pl.semaphore_signal(barrier, 1, device_id=(d, (t + k) % 8), device_id_type=MESH)
    for k in range(1, 4):
        pl.semaphore_signal(barrier, 1, device_id=(dpeer(k), t), device_id_type=MESH)

    WBLK[...] = mm(eye(32), reduce_weight[...], 1, 1).astype(bf16)
    CB[:, 0:2304] = mm(eye(32), conv_weight[...], 1, 1).astype(bf16)
    CB[:, 2304:3328] = expand_weight[...]
    eighth = jnp.full((8, 128), 0.125, f32)
    lane = lax.broadcasted_iota(jnp.int32, (32, 128), 1)
    packed = jnp.zeros((32, 128), f32)
    for n, gain in enumerate((gain_middle, gain_inner)):
        column = mm(jnp.broadcast_to(gain[...], (8, 32)), eighth, 0, 0, HIGHEST)
        high, rest = split(column)
        rest = column - high.astype(f32)
        mid, low = split(rest)
        for m, part in enumerate((high, mid, low)):
            packed = jnp.where(lane == 3 * n + m, part.astype(f32), packed)
    CB[:, 3328:3456] = packed.astype(bf16)
    CB[:, 3456:3584] = jnp.zeros((32, 128), bf16)
    pl.semaphore_wait(barrier, 10)

    w_cp = []
    for k in range(1, 8):
        s = (t + k) % 8
        w_cp.append(send(WBLK.at[:, pl.ds(pl.multiple_of(256 * (s // 2), 256), 256)], WT.at[pl.ds(pl.multiple_of(32 * t, 32), 32)], d, s))
    WT[pl.ds(pl.multiple_of(32 * t, 32), 32), :] = WBLK[:, pl.ds(pl.multiple_of(256 * z, 256), 256)]
    quarter = CB.at[:, pl.ds(pl.multiple_of(896 * d, 128), 896)]
    wq_cp = [send(quarter, WQ.at[z], d, zpeer(k)) for k in range(1, 4)]
    WQ[z] = quarter[...]

    go_rows = jnp.broadcast_to(gain_outer[...], (8, 128))
    go = mm(go_rows, eighth, 0, 0, HIGHEST)[:, 0:1]
    pos = position[...]
    pos_pair = mm(eye(128, f32), jnp.concatenate([pos, pos], axis=0), 1, 1, HIGHEST)
    x_cp = []
    for k in (1, 2, 3, 0):
        p = (z + k) % 4
        cols = pl.ds(pl.multiple_of(1152 * p, 128), 1152)
        x = features[:, cols].astype(f32) + pos_pair
        PLC[:, cols] = x
        m = jnp.mean(x, axis=0, keepdims=True)
        x = x - m
        q = jnp.sum(x * x, axis=0, keepdims=True)
        x = (x * go).astype(bf16)
        for par, lo in ((0, 0), (1, 512)):
            XW[par, p] = x[:, lo : lo + 640]
            ST[2 * p + par, 0:1, :] = m[:, lo : lo + 640]
            ST[2 * p + par, 1:2, :] = q[:, lo : lo + 640]
        x_cp.append(send(XW.at[1 - c, p], XK.at[p, pl.ds(pl.multiple_of(128 * c, 128), 128)], d, sib))
        XK[p, pl.ds(pl.multiple_of(128 * c, 128), 128), :] = XW[c, p]

    for cp in w_cp:
        cp.wait_recv()
    WC[...] = mm(eye(256), WT[...], 1, 1).astype(bf16)
    mine = WC[pl.ds(pl.multiple_of(128 * c, 128), 128), :].astype(f32)
    colsum = mm(go_rows, mine, 1, 0, HIGHEST)[0:1]
    for n in range(8):
        ST[n, 2:3, 0:256] = colsum
    q_cp = []
    for n, k in enumerate((1, 2, 3, 0)):
        p = (z + k) % 4
        x_cp[n].wait_recv()
        QF[...] = mm(XK[p], WC[...], 0, 0)
        part = QF[pl.ds(pl.multiple_of(64 * c, 64), 576), :]
        if k == 0:
            QO[...] = part
        else:
            QS[k - 1] = part.astype(bf16)
            q_cp.append(send(QS.at[k - 1], QR.at[k - 1], d, zpeer(k)))
    st_cp = [send(ST.at[(t + k) % 8], SR.at[t], d, (t + k) % 8) for k in range(1, 8)]
    SR[t] = ST[t]

    POOL[...] = pool_pair()
    for p in range(4):
        high, low = split(PLC[:, 1152 * p : 1152 * (p + 1)])
        PP[t, 288 * p : 288 * (p + 1), :] = (mm(POOL[...], high, 1, 1) + mm(POOL[...], low, 1, 1)).astype(bf16)
    pp_cp = [send(PP.at[t], PP.at[t], d, zpeer(k)) for k in range(1, 4)]
    pps_cp = [send(PP.at[t], PP.at[t], d, sib)]

    for cp in wq_cp:
        cp.wait_recv()
    wb_cp = [send(WQ, WB.at[c, d], dpeer(k), t) for k in range(1, 4)]
    WB[c, d] = WQ[...]
    for cp in wb_cp:
        cp.wait_recv()
    ws_cp = send(WB.at[c], WB.at[c], d, sib)
    ws_cp.wait_recv()
    for cc in range(2):
        for zz in range(4):
            for dd in range(4):
                WF[32 * (2 * zz + cc) : 32 * (2 * zz + cc + 1), 896 * dd : 896 * (dd + 1)] = WB[cc, dd, zz]
    lane = lax.broadcasted_iota(jnp.int32, (8, 128), 1)
    row = lax.broadcasted_iota(jnp.int32, (8, 128), 0)
    pick = jnp.where((lane >= 3 * row) & (lane < 3 * row + 3) & (row < 2), 1.0, 0.0).astype(bf16)
    gains = mm(pick, WF[:, 3328:3456], 1, 1)
    gm, gi = gains[0:1], gains[1:2]
    MT[...] = mm(readout_weight[...], WF[:, 2304:3328], 1, 1).astype(bf16)

    for cp in st_cp:
        cp.wait_recv()
    m_t = SR[:, 0, :]
    q_t = SR[:, 1, :]
    sums = SR[:, 2, 0:256]
    mean = jnp.mean(m_t, axis=0, keepdims=True)
    dm = m_t - mean
    var = (jnp.sum(q_t, axis=0, keepdims=True) + 128.0 * jnp.sum(dm * dm, axis=0, keepdims=True)) * (1.0 / 1024.0)
    rstd = lax.rsqrt(var + epsilon)
    valid = pl.ds(pl.multiple_of(64 * c, 64), 576)
    QF[...] = mm(dm, sums, 0, 0, HIGHEST)
    total = QO[...] + QF[valid, :]
    QF[...] = mm(jnp.broadcast_to(rstd, (8, 640)), jnp.full((8, 256), 0.125, f32), 0, 0, HIGHEST)
    scale = QF[valid, :]
    for cp in q_cp:
        cp.wait_recv()
    for k in range(3):
        total += QR[k].astype(f32)
    RED[...] = jnp.zeros((24, 32, 256), f32)
    RED[:, 0:24, :] = (total * scale).reshape(24, 24, 256)

    xm, rm = norm_rows(RED[...].reshape(768, 256))
    zm = xm * gm
    hidden = zm * jax.nn.sigmoid(zm)
    XM[...], ZM[...], RM[...] = xm, zm, jnp.broadcast_to(rm, (768, 128))
    HB[0:32, :] = jnp.zeros((32, 768), bf16)
    HB[800:832, :] = jnp.zeros((32, 768), bf16)
    HB[32:800, 0:256] = pltpu.roll(hidden, 1, 0).astype(bf16)
    HB[32:800, 256:512] = hidden.astype(bf16)
    HB[32:800, 512:768] = pltpu.roll(hidden, 767, 0).astype(bf16)
    conv = mm(HB[0:768, :], WF[:, 0:768], 1, 1)
    conv += mm(HB[32:800, :], WF[:, 768:1536], 1, 1)
    conv += mm(HB[64:832, :], WF[:, 1536:2304], 1, 1)
    xi, ri = norm_rows(conv)
    zi = xi * gi
    activated = (zi * jax.nn.sigmoid(zi)).astype(bf16)
    XI[...], ZI[...], RI[...] = xi, zi, jnp.broadcast_to(ri, (768, 128))
    pool = pool_wide()
    ACT[t] = mm(pool, activated, 1, 0).astype(bf16)
    a_cp = [send(ACT.at[t], ACT.at[t], d, zpeer(k)) for k in range(1, 4)]
    as_cp = [send(ACT.at[t], ACT.at[t], d, sib)]

    for k in range(1, 4):
        pp_cp[k - 1].wait_recv()
        slot = 2 * ((z + 4 - k) % 4) + c
        pps_cp.append(send(PP.at[slot], PP.at[slot], d, sib))
    for cp in pps_cp:
        cp.wait_recv()
    before = jnp.zeros((512, 1152), f32)
    for q in range(4):
        both = jnp.concatenate([PP[2 * q], PP[2 * q + 1]], axis=1)
        before += mm(readout_weight[:, 256 * q : 256 * (q + 1)], both, 1, 1)
    BEF[...] = before

    for k in range(1, 4):
        a_cp[k - 1].wait_recv()
        slot = 2 * ((z + 4 - k) % 4) + c
        as_cp.append(send(ACT.at[slot], ACT.at[slot], d, sib))
    for cp in as_cp:
        cp.wait_recv()
    for n in range(8):
        ACL[n] = (ACT[n].astype(f32) * slot_live[n].astype(f32)).astype(bf16)
    act_live = ACL[...].reshape(1152, 256)
    BEF[...] += mm(MT[...], act_live, 1, 1)

    @pl.loop(0, 16)
    def _(u):
        rows = pl.ds(pl.multiple_of(32 * u, 32), 32)
        b = BEF[rows, :]
        below = 0.5 * (1.0 + lax.erf(b * 0.7071067811865476))
        density = jnp.exp(-0.5 * b * b) * 0.3989422804014327
        readout_o[rows, :] = (b * below).astype(bf16)
        GBT[rows, :] = (cotangent[rows, :].astype(f32) * (below + b * density)).astype(bf16)

    terms = mm(GBT[...], MT[...], 0, 0).astype(bf16).reshape(8, 144, 256)
    for n in range(8):
        AT[n % 2, n // 2] = terms[n]
    at_cp = send(AT.at[1 - c], AR, d, sib)
    for q in range(4):
        block = mm(GBT[...], readout_weight[:, 256 * q : 256 * (q + 1)], 0, 0).astype(bf16)
        TE[0, q] = block[:, 0:128]
        TE[1, q] = block[:, 128:256]
    at_cp.wait_recv()
    az_cp = []
    for k in (1, 2, 3):
        p = (z + k) % 4
        AS[k - 1] = (AT[c, p].astype(f32) + AR[p].astype(f32)).astype(bf16)
        az_cp.append(send(AS.at[k - 1], AZ.at[k - 1], d, zpeer(k)))
    te_cp = send(TE.at[1 - c], TR, d, sib)
    grad_act = AT[c, z].astype(f32) + AR[z].astype(f32)
    for q in range(4):
        both = jnp.concatenate([PP[2 * q], PP[2 * q + 1]], axis=1).astype(f32)
        POOLED[:, 256 * q : 256 * (q + 1)] = (both + mm(act_live, WF[:, 2304 + 256 * q : 2560 + 256 * q], 1, 0)).astype(bf16)
    for q in range(4):
        GR[q] = mm(GBT[128 * q : 128 * (q + 1), :], POOLED[...], 1, 0).astype(bf16)
    gr_cp = [send(GR.at[(d + k) % 4], GRR.at[d], dpeer(k), t) for k in range(1, 4)]
    GRR[d] = GR[d]
    te_cp.wait_recv()
    es_cp = []
    for k in (1, 2, 3):
        p = (z + k) % 4
        ES[k - 1] = (TE[c, p].astype(f32) + TR[p].astype(f32)).astype(bf16)
        es_cp.append(send(ES.at[k - 1], ER.at[k - 1], d, zpeer(k)))
    GP[...] = TE[c, z].astype(f32) + TR[z].astype(f32)

    for cp in az_cp:
        cp.wait_recv()
    for k in range(3):
        grad_act += AZ[k].astype(f32)
    high, low = split(grad_act * slot_live[t].astype(f32))
    grad_rows = mm(pool, high, 0, 0) + mm(pool, low, 0, 0)
    zi = ZI[...]
    gate = jax.nn.sigmoid(zi)
    dy = grad_rows * (gate * (1.0 + zi * (1.0 - gate)))
    xi = XI[...]
    dyx_inner = dy * xi
    gc = norm_rows_back(dy * gi, xi, RI[:, 0:1]).astype(bf16)
    GB[0:32, :] = jnp.zeros((32, 256), bf16)
    GB[800:832, :] = jnp.zeros((32, 256), bf16)
    GB[32:800, :] = gc
    back = mm(GB[64:832, :], WF[:, 0:768], 1, 0)
    back += mm(GB[32:800, :], WF[:, 768:1536], 1, 0)
    back += mm(GB[0:768, :], WF[:, 1536:2304], 1, 0)
    grad_hidden = pltpu.roll(back[:, 0:256], 767, 0) + back[:, 256:512] + pltpu.roll(back[:, 512:768], 1, 0)
    zm = ZM[...]
    gate = jax.nn.sigmoid(zm)
    inside = (lax.broadcasted_iota(jnp.int32, (768, 256), 0) & 31) < 24
    dy = jnp.where(inside, grad_hidden * (gate * (1.0 + zm * (1.0 - gate))), 0.0)
    xm = XM[...]
    dyx_middle = dy * xm
    gr = norm_rows_back(dy * gm, xm, RM[:, 0:1]).reshape(24, 32, 256)[:, 0:24, :].reshape(576, 256).astype(bf16)
    GA[t] = gr
    ga_cp = [send(GA.at[t], GA.at[t], d, zpeer(k)) for k in range(1, 4)]
    gas_cp = [send(GA.at[t], GA.at[t], d, sib)]
    QF[...] = jnp.zeros((640, 256), f32)
    QF[valid, :] = gr.astype(f32)
    wg = jnp.sum(sums, axis=0, keepdims=True)
    s1 = mm(jnp.broadcast_to(wg, (8, 256)), QF[...], 1, 1, HIGHEST)[0:1]
    QF[valid, :] = gr.astype(f32) * RED[:, 0:24, :].reshape(576, 256)
    s2 = mm(jnp.ones((8, 256), f32), QF[...], 1, 1, HIGHEST)[0:1]
    RS[t, 0:1, :] = mean
    RS[t, 1:2, :] = rstd
    RS[t, 2:3, :] = s1 * (1.0 / 1024.0)
    RS[t, 3:4, :] = s2 * (1.0 / 1024.0)
    rs_cp = [send(RS.at[t], RS.at[t], d, (t + k) % 8) for k in range(1, 8)]

    def put(lo, value):
        value = value.astype(bf16)
        for n in range(8):
            CG[n % 2, n // 2, :, lo : lo + value.shape[1]] = value[32 * n : 32 * (n + 1)]

    for a in range(3):
        put(768 * a, mm(gc, HB[32 * a : 32 * a + 768, :], 0, 0))
    ones = jnp.ones((768, 128), bf16)
    for lo, value in ((2304, dyx_inner), (2432, dyx_middle)):
        high, low = split(value)
        put(lo, mm(high, ones, 0, 0) + mm(low, ones, 0, 0))
    cg_cp = send(CG.at[1 - c], CGR, d, sib)

    for cp in gr_cp:
        cp.wait_recv()
    total = GRR[0].astype(f32)
    for n in range(1, 4):
        total += GRR[n].astype(f32)
    GRF[d] = total.astype(bf16)
    grf_cp = [send(GRF.at[d], GRF.at[d], dpeer(k), t) for k in range(1, 4)]

    cg_cp.wait_recv()
    CGS[...] = (CG[c].astype(f32) + CGR[...].astype(f32)).astype(bf16)
    cgd_cp = []
    for k in range(1, 4):
        dd = dpeer(k)
        cgd_cp.append(send(CGS.at[:, :, pl.ds(pl.multiple_of(640 * dd, 128), 640)], CGD.at[d], dd, t))
    CGD[d] = CGS[:, :, pl.ds(pl.multiple_of(640 * d, 128), 640)]

    for k in range(1, 4):
        ga_cp[k - 1].wait_recv()
        slot = 2 * ((z + 4 - k) % 4) + c
        gas_cp.append(send(GA.at[slot], GA.at[slot], d, sib))
    for cp in cgd_cp:
        cp.wait_recv()
    total = CGD[0].astype(f32)
    for n in range(1, 4):
        total += CGD[n].astype(f32)
    CGT[...] = total.astype(bf16)
    cgz_cp = [send(CGT.at[(z + k) % 4], CGZ.at[z], d, zpeer(k)) for k in range(1, 4)]
    CGZ[z] = CGT[z]
    for cp in es_cp:
        cp.wait_recv()
    gp = GP[...]
    for k in range(3):
        gp += ER[k].astype(f32)
    gp_high, gp_low = split(gp)
    FT[0] = mm(act_live, gp_high, 0, 0).astype(bf16)
    for cp in cgz_cp:
        cp.wait_recv()
    total = CGZ[0].astype(f32)
    for n in range(1, 4):
        total += CGZ[n].astype(f32)
    CGF[d] = total.astype(bf16)
    cgf_cp = [send(CGF.at[d], CGF.at[d], dpeer(k), t) for k in range(1, 4)]
    for cp in rs_cp:
        cp.wait_recv()
    for cp in gas_cp:
        cp.wait_recv()
    w_own = WC[pl.ds(pl.multiple_of(128 * c, 128), 128), :]
    lane = lax.broadcasted_iota(jnp.int32, (4, 128), 1)
    place_sum = jnp.zeros((128, 1152), f32)
    gain_sum = jnp.zeros((128, 1), f32)
    grad_reduce = jnp.zeros((128, 256), f32)
    for p in range(4):
        cols = slice(1152 * p, 1152 * (p + 1))
        even, odd = RS[2 * p], RS[2 * p + 1]
        stats = jnp.concatenate([even[:, 0:512], jnp.where(lane < 64, even[:, 512:640], odd[:, 0:128]), odd[:, 128:640]], axis=1)
        g = GA[2 * p : 2 * p + 2].reshape(1152, 256)
        gn = mm(w_own, g, 1, 1)
        xhat = (PLC[:, cols] - stats[0:1]) * stats[1:2]
        gain_sum += jnp.sum(gn * xhat, axis=1, keepdims=True)
        grad_reduce += mm((xhat * go).astype(bf16), g, 1, 0)
        spread = mm(gp_high[288 * p : 288 * (p + 1)], POOL[...], 0, 0) + mm(gp_low[288 * p : 288 * (p + 1)], POOL[...], 0, 0)
        out = spread + stats[1:2] * (gn * go - stats[2:3] - xhat * stats[3:4])
        gfeat_o[:, cols] = out
        place_sum += out
    FT[1] = jnp.transpose(grad_reduce).astype(bf16)
    ft_cp = []
    for k in range(1, 8):
        s = (t + k) % 8
        ft_cp.append(send(FT.at[:, pl.ds(pl.multiple_of(32 * s, 32), 32)], TA.at[d, t], d, s))
    TA[d, t] = FT[:, pl.ds(pl.multiple_of(32 * t, 32), 32), :]
    odd = pltpu.roll(place_sum, 576, 1)
    lane = lax.broadcasted_iota(jnp.int32, (128, 640), 1)
    PM[d] = jnp.where(lane < 576, place_sum[:, 0:640] + odd[:, 0:640], jnp.broadcast_to(gain_sum, (128, 640))).astype(bf16)
    pm_cp = [send(PM.at[d], PM.at[d], dpeer(k), t) for k in range(1, 4)]
    for cp in ft_cp:
        cp.wait_recv()
    ta_cp = [send(TA.at[d], TA.at[d], dpeer(k), t) for k in range(1, 4)]

    for cp in grf_cp:
        cp.wait_recv()
    for q in range(4):
        gread_o[128 * q : 128 * (q + 1), :] = GRF[q].astype(f32)
    for cp in cgf_cp:
        cp.wait_recv()
    for q in range(4):
        gconv_o[:, 640 * q : 640 * (q + 1)] = CGF[q].astype(f32)
    for cp in pm_cp:
        cp.wait_recv()
    total = PM[0].astype(f32)
    for n in range(1, 4):
        total += PM[n].astype(f32)
    gpos_o[...] = jnp.transpose(total)
    for cp in ta_cp:
        cp.wait_recv()
    for s in range(8):
        total = TA[0, s].astype(f32)
        for n in range(1, 4):
            total += TA[n, s].astype(f32)
        gexp_o[:, 128 * s : 128 * (s + 1)] = total[0]
        gred_o[:, 128 * s : 128 * (s + 1)] = total[1]
    for cp in pending:
        cp.wait_send()


SCRATCH = (
    ("WBLK", (32, 1024), bf16), ("WT", (256, 256), bf16), ("WC", (256, 256), bf16), ("CB", (32, 3584), bf16),
    ("WQ", (4, 32, 896), bf16), ("WB", (2, 4, 4, 32, 896), bf16), ("WF", (256, 3584), bf16), ("MT", (512, 256), bf16),
    ("POOL", (288, 1152), bf16), ("PLC", (128, 4608), f32), ("XW", (2, 4, 128, 640), bf16), ("XK", (4, 256, 640), bf16),
    ("ST", (8, 4, 640), f32), ("SR", (8, 4, 640), f32), ("QF", (640, 256), f32), ("QS", (3, 576, 256), bf16),
    ("QO", (576, 256), f32), ("QR", (3, 576, 256), bf16), ("RED", (24, 32, 256), f32), ("HB", (832, 768), bf16),
    ("GB", (832, 256), bf16), ("XM", (768, 256), f32), ("ZM", (768, 256), f32), ("RM", (768, 128), f32),
    ("XI", (768, 256), f32), ("ZI", (768, 256), f32), ("RI", (768, 128), f32), ("ACT", (8, 144, 256), bf16), ("ACL", (8, 144, 256), bf16),
    ("PP", (8, 1152, 128), bf16), ("POOLED", (1152, 1024), bf16), ("BEF", (512, 1152), f32), ("GBT", (512, 1152), bf16),
    ("TE", (2, 4, 1152, 128), bf16), ("TR", (4, 1152, 128), bf16), ("ES", (3, 1152, 128), bf16), ("ER", (3, 1152, 128), bf16),
    ("GP", (1152, 128), f32), ("AT", (2, 4, 144, 256), bf16), ("AR", (4, 144, 256), bf16), ("AS", (3, 144, 256), bf16),
    ("AZ", (3, 144, 256), bf16), ("GW", (8, 128), f32), ("GA", (8, 576, 256), bf16), ("RS", (8, 4, 640), f32),
    ("FT", (2, 256, 128), bf16), ("TA", (4, 8, 2, 32, 128), bf16), ("PM", (4, 128, 640), bf16),
    ("CG", (2, 4, 32, 2560), bf16), ("CGR", (4, 32, 2560), bf16), ("CGS", (4, 32, 2560), bf16), ("CGD", (4, 4, 32, 640), bf16),
    ("CGT", (4, 32, 640), bf16), ("CGZ", (4, 32, 640), bf16), ("CGF", (4, 32, 640), bf16), ("GR", (4, 128, 1024), bf16), ("GRR", (4, 128, 1024), bf16),
    ("GRF", (4, 128, 1024), bf16),
)


def local_by_image(features, slot_live, position, gain_outer, reduce_weight, gain_middle, conv_weight, gain_inner, expand_weight, readout_weight, cotangent):
    vmem = pl.BlockSpec(memory_space=pltpu.VMEM)
    smem = pl.BlockSpec(memory_space=pltpu.SMEM)
    readout, gfeat, gpos, gexp, gred, gconv, gread = pl.pallas_call(
        kernel,
        out_shape=(
            jax.ShapeDtypeStruct((512, 1152), bf16), jax.ShapeDtypeStruct((128, 4608), f32), jax.ShapeDtypeStruct((640, 128), f32),
            jax.ShapeDtypeStruct((32, 1024), f32), jax.ShapeDtypeStruct((32, 1024), f32), jax.ShapeDtypeStruct((32, 2560), f32),
            jax.ShapeDtypeStruct((512, 1024), f32),
        ),
        in_specs=[vmem, smem] + [vmem] * 9,
        out_specs=[vmem] * 7,
        scratch_shapes=[pltpu.VMEM(shape, dtype) for _, shape, dtype in SCRATCH]
        + [pltpu.SemaphoreType.DMA((COPIES,)), pltpu.SemaphoreType.DMA((COPIES,))],
        compiler_params=pltpu.CompilerParams(collective_id=0, has_side_effects=True, vmem_limit_bytes=63 * 2**20),
    )(
        features, slot_live, position.reshape(576, 128), gain_outer.reshape(1, 128), reduce_weight, gain_middle.reshape(1, 32),
        conv_weight.reshape(2304, 32), gain_inner.reshape(1, 32), expand_weight, readout_weight, cotangent,
    )
    return (
        readout, gfeat, gpos[0:576].reshape(24, 24, 128), gpos[576], gred.T, gconv[:, 2432],
        gconv[:, 0:2304].T.reshape(3, 3, 256, 32), gconv[:, 2304], gexp, gread,
    )


def row_totals(leading, trailing):
    return lax.psum((leading, trailing), "tensor")


def norm_forward(values, norm_gain, breadth):
    totals, squares = row_totals(jnp.sum(values, axis=1), jnp.sum(values * values, axis=1))
    center = totals / breadth
    spread = squares / breadth - center * center
    scaled = lax.rsqrt(spread + epsilon)[:, None]
    normed = (values - center[:, None]) * scaled
    return (normed, scaled, normed * norm_gain)


def norm_backward(grad_out, normed, scaled, norm_gain, breadth):
    grad_normed = grad_out * norm_gain
    gain_grad = jnp.sum(grad_out * normed, axis=0)
    leading, trailing = row_totals(
        jnp.sum(grad_normed, axis=1), jnp.sum(grad_normed * normed, axis=1)
    )
    grad_in = scaled * (
        grad_normed - leading[:, None] / breadth - normed * (trailing[:, None] / breadth)
    )
    return (grad_in, gain_grad)


def silu_grad(inputs):
    gate_value = jax.nn.sigmoid(inputs)
    return gate_value * (1.0 + inputs * (1.0 - gate_value))


def gelu_grad(inputs):
    below = 0.5 * (1.0 + lax.erf(inputs * 0.7071067811865476))
    density = jnp.exp(-0.5 * inputs * inputs) * 0.3989422804014327
    return below + inputs * density


def contract_rows(left_side, right_side):
    return lax.dot_general(
        left_side, right_side, (((0,), (0,)), ((), ())), preferred_element_type=jnp.float32
    )


def window_of(padded, shift_down, shift_across, grid_side):
    images = padded.shape[0]
    breadth = padded.shape[3]
    return padded[
        :, shift_down : shift_down + grid_side, shift_across : shift_across + grid_side, :
    ].reshape(images * grid_side * grid_side, breadth)


def local_by_hidden(
    features,
    slot_live,
    position,
    gain_outer,
    reduce_weight,
    gain_middle,
    conv_weight,
    gain_inner,
    expand_weight,
    readout_weight,
    cotangent,
):
    grid_side = position.shape[0]
    half_side = grid_side // 2
    channel_share = features.shape[0]
    row_count = features.shape[1]
    images = row_count // (grid_side * grid_side)
    tensor_size = lax.axis_size("tensor")
    channels = channel_share * tensor_size
    hidden_share = reduce_weight.shape[1]
    hidden_width = hidden_share * tensor_size
    pooled_count = images * half_side * half_side
    placed = (
        features.T.astype(jnp.float32).reshape(images, grid_side * grid_side, channel_share)
        + position.reshape(1, grid_side * grid_side, channel_share)
    ).reshape(row_count, channel_share)
    live_rows = jnp.repeat(slot_live.astype(jnp.float32), grid_side * grid_side)[:, None]
    normed_outer, scaled_outer, shaped_outer = norm_forward(placed, gain_outer, channels)
    reduce_in = shaped_outer.astype(jnp.bfloat16)
    reduce_full = lax.all_gather(reduce_in, "tensor", axis=1, tiled=True)
    reduced = jnp.dot(reduce_full, reduce_weight, preferred_element_type=jnp.float32)
    normed_middle, scaled_middle, shaped_middle = norm_forward(reduced, gain_middle, hidden_width)
    hidden = jax.nn.silu(shaped_middle).astype(jnp.bfloat16)
    hidden_full = lax.all_gather(hidden, "tensor", axis=1, tiled=True)
    padded_hidden = jnp.pad(
        hidden_full.reshape(images, grid_side, grid_side, hidden_width),
        ((0, 0), (1, 1), (1, 1), (0, 0)),
    )
    convolved = jnp.zeros((row_count, hidden_share), jnp.float32)
    for offset_tap in range(9):
        shift_down = offset_tap // 3
        shift_across = offset_tap % 3
        convolved = convolved + jnp.dot(
            window_of(padded_hidden, shift_down, shift_across, grid_side),
            conv_weight[shift_down, shift_across],
            preferred_element_type=jnp.float32,
        )
    normed_inner, scaled_inner, shaped_inner = norm_forward(convolved, gain_inner, hidden_width)
    activated = jax.nn.silu(shaped_inner).astype(jnp.bfloat16)
    expand_terms = jnp.dot(activated, expand_weight, preferred_element_type=jnp.float32)
    expanded = lax.psum_scatter(expand_terms, "tensor", scatter_dimension=1, tiled=True)
    mixed = placed + live_rows * expanded
    pooled = jnp.mean(mixed.reshape(images, half_side, 2, half_side, 2, channel_share), axis=(2, 4))
    pooled_low = pooled.reshape(pooled_count, channel_share).astype(jnp.bfloat16)
    pooled_full = lax.all_gather(pooled_low, "tensor", axis=1, tiled=True)
    before = lax.dot_general(
        pooled_full, readout_weight, (((1,), (1,)), ((), ())), preferred_element_type=jnp.float32
    )
    readout = jax.nn.gelu(before, approximate=False).astype(jnp.bfloat16).T
    grad_before = (cotangent.T.astype(jnp.float32) * gelu_grad(before)).astype(jnp.bfloat16)
    grad_readout = contract_rows(grad_before, pooled_full)
    pooled_terms = jnp.dot(grad_before, readout_weight, preferred_element_type=jnp.float32)
    grad_pooled = lax.psum_scatter(pooled_terms, "tensor", scatter_dimension=1, tiled=True)
    spread_grad = jnp.broadcast_to(
        (0.25 * grad_pooled).reshape(images, half_side, 1, half_side, 1, channel_share),
        (images, half_side, 2, half_side, 2, channel_share),
    )
    grad_mixed = spread_grad.reshape(row_count, channel_share)
    grad_branch = (live_rows * grad_mixed).astype(jnp.bfloat16)
    grad_full = lax.all_gather(grad_branch, "tensor", axis=1, tiled=True)
    grad_expand = contract_rows(activated, grad_full)
    grad_activated = jnp.dot(grad_full, expand_weight.T, preferred_element_type=jnp.float32)
    grad_convolved, grad_gain_inner = norm_backward(
        grad_activated * silu_grad(shaped_inner),
        normed_inner,
        scaled_inner,
        gain_inner,
        hidden_width,
    )
    grad_conv_low = grad_convolved.astype(jnp.bfloat16)
    tap_grads = []
    grad_padded = jnp.zeros((images, grid_side + 2, grid_side + 2, hidden_width), jnp.float32)
    for offset_tap in range(9):
        shift_down = offset_tap // 3
        shift_across = offset_tap % 3
        tap_grads.append(
            contract_rows(
                window_of(padded_hidden, shift_down, shift_across, grid_side), grad_conv_low
            )
        )
        tap_back = jnp.dot(
            grad_conv_low,
            conv_weight[shift_down, shift_across].T,
            preferred_element_type=jnp.float32,
        )
        grad_padded = grad_padded + jnp.pad(
            tap_back.reshape(images, grid_side, grid_side, hidden_width),
            ((0, 0), (shift_down, 2 - shift_down), (shift_across, 2 - shift_across), (0, 0)),
        )
    grad_conv = jnp.stack(tap_grads, axis=0).reshape(conv_weight.shape)
    grad_window = grad_padded[:, 1 : grid_side + 1, 1 : grid_side + 1, :].reshape(
        row_count, hidden_width
    )
    grad_hidden = lax.psum_scatter(grad_window, "tensor", scatter_dimension=1, tiled=True)
    grad_reduced, grad_gain_middle = norm_backward(
        grad_hidden * silu_grad(shaped_middle),
        normed_middle,
        scaled_middle,
        gain_middle,
        hidden_width,
    )
    grad_reduced_low = grad_reduced.astype(jnp.bfloat16)
    grad_reduce = contract_rows(reduce_full, grad_reduced_low)
    outer_terms = jnp.dot(grad_reduced_low, reduce_weight.T, preferred_element_type=jnp.float32)
    grad_shaped_outer = lax.psum_scatter(outer_terms, "tensor", scatter_dimension=1, tiled=True)
    grad_inputs, grad_gain_outer = norm_backward(
        grad_shaped_outer, normed_outer, scaled_outer, gain_outer, channels
    )
    grad_rows = grad_mixed + grad_inputs
    grad_place = jnp.sum(grad_rows.reshape(images, grid_side, grid_side, channel_share), axis=0)
    grad_total = grad_rows.T
    summed = (
        lax.psum(grad_place.astype(jnp.bfloat16), "dp").astype(jnp.float32),
        lax.psum(grad_gain_outer.astype(jnp.bfloat16), "dp").astype(jnp.float32),
        lax.psum(grad_reduce.astype(jnp.bfloat16), "dp").astype(jnp.float32),
        lax.psum(grad_gain_middle.astype(jnp.bfloat16), "dp").astype(jnp.float32),
        lax.psum(grad_conv.astype(jnp.bfloat16), "dp").astype(jnp.float32),
        lax.psum(grad_gain_inner.astype(jnp.bfloat16), "dp").astype(jnp.float32),
        lax.psum(grad_expand.astype(jnp.bfloat16), "dp").astype(jnp.float32),
        lax.psum(grad_readout.astype(jnp.bfloat16), "dp").astype(jnp.float32),
    )
    return (
        readout,
        grad_total,
        summed[0],
        summed[1],
        summed[2],
        summed[3],
        summed[4],
        summed[5],
        summed[6],
        summed[7],
    )


def solution(mesh):
    parts, groups = mesh.shape["tensor"], mesh.shape["dp"]
    specs = (P("tensor", "dp"), P("dp"), P(None, None, "tensor"), P("tensor"), P(None, "tensor"), P("tensor"), P(None, None, None, "tensor"), P("tensor"), P("tensor", None), P("tensor", None), P("tensor", "dp"))

    def whole(*arrays):
        by_image = (parts, groups) == (8, 4) and arrays[1].shape[0] == parts * groups
        return jax.shard_map(
            local_by_image if by_image else local_by_hidden, mesh=mesh, in_specs=specs,
            out_specs=(P("tensor", "dp"), P("tensor", "dp"), *specs[2:10]), check_vma=False,
        )(*arrays)

    return whole
```

```python
import jax
import jax.numpy as jnp
from jax import lax
from jax.experimental import pallas as pl
from jax.experimental.pallas import tpu as pltpu
from jax.sharding import PartitionSpec as P

epsilon = 1e-05
bf16 = jnp.bfloat16
f32 = jnp.float32
COPIES = 160

MESH = pl.DeviceIdType.MESH
HIGHEST = lax.Precision.HIGHEST


def mm(a, b, ca, cb, precision=None):
    return lax.dot_general(a, b, (((ca,), (cb,)), ((), ())), precision=precision, preferred_element_type=f32)


def split(x):
    high = x.astype(bf16)
    return high, (x - high.astype(f32)).astype(bf16)


def eye(n, dtype=bf16):
    return (lax.broadcasted_iota(jnp.int32, (n, n), 0) == lax.broadcasted_iota(jnp.int32, (n, n), 1)).astype(f32).astype(dtype)


def pool_wide():
    spot = lax.broadcasted_iota(jnp.int32, (144, 768), 1)
    cell = lax.broadcasted_iota(jnp.int32, (144, 768), 0)
    i, j = spot >> 5, spot & 31
    return jnp.where(((i >> 1) * 12 + (j >> 1) == cell) & (j < 24), 0.25, 0.0).astype(bf16)


def pool_pair():
    spot = lax.broadcasted_iota(jnp.int32, (288, 1152), 1)
    cell = lax.broadcasted_iota(jnp.int32, (288, 1152), 0)
    i = (spot * 2731) >> 16
    j = spot - i * 24
    return jnp.where((i >> 1) * 12 + (j >> 1) == cell, 0.25, 0.0).astype(bf16)


def norm_rows(v):
    s = v - jnp.mean(v, axis=1, keepdims=True)
    r = lax.rsqrt(jnp.mean(s * s, axis=1, keepdims=True) + epsilon)
    return s * r, r


def norm_rows_back(dx, xhat, r):
    return r * (dx - jnp.mean(dx, axis=1, keepdims=True) - xhat * jnp.mean(dx * xhat, axis=1, keepdims=True))


def kernel(
    features, slot_live, position, gain_outer, reduce_weight, gain_middle, conv_weight, gain_inner, expand_weight, readout_weight, cotangent,
    readout_o, gfeat_o, gpos_o, gexp_o, gred_o, gconv_o, gread_o,
    WBLK, WT, WC, CB, WQ, WB, WF, MT, POOL, PLC, XW, XK, ST, SR, QF, QS, QO, QR, RED, HB, GB,
    XM, ZM, RM, XI, ZI, RI, ACT, ACL, PP, POOLED, BEF, GBT, TE, TR, ES, ER, GP, AT, AR, AS, AZ,
    GW, GA, RS, FT, TA, PM, CG, CGR, CGS, CGD, CGT, CGZ, CGF, GR, GRR, GRF, ssem, rsem,
):
    d = lax.axis_index("dp")
    t = lax.axis_index("tensor")
    z = t // 2
    c = t % 2
    sib = 2 * z + 1 - c
    side = z // 2
    is_mid = ((z + 1) // 2) % 2
    near_end, near_mid, far_end, far_mid = 3 * side, 1 + side, 3 - 3 * side, 2 - side
    partner = z + 1 - 2 * (z % 2)
    sends, arrivals = [0], [0]
    pending = []

    def copy(src, dst, dd, tt, arrival):
        cp = pltpu.make_async_remote_copy(
            src_ref=src, dst_ref=dst, send_sem=ssem.at[sends[0]], recv_sem=rsem.at[arrival], device_id=(dd, tt), device_id_type=MESH
        )
        sends[0] += 1
        return cp

    def take(n):
        arrivals[0] += n
        return arrivals[0] - n

    def send(src, dst, dd, tt):
        cp = copy(src, dst, dd, tt, take(1))
        cp.start()
        pending.append(cp)
        return cp

    class Gather:
        def __init__(self, buf, parts):
            self.buf, self.parts, self.rows = buf, parts, buf.shape[1] // parts
            self.base = take(4 * parts)
            self.forwards = []

        def view(self, zz, h):
            return self.buf.at[2 * zz + c, pl.ds(h * self.rows, self.rows)]

        def to(self, block, zz, h):
            return copy(self.view(block, h), self.view(block, h), d, 2 * zz + c, self.base + 4 * h + block)

        def start(self):
            for zz in (far_mid, partner):
                for h in range(self.parts):
                    cp = self.to(z, zz, h)
                    cp.start()
                    pending.append(cp)
            self.siblings = [send(self.buf.at[t], self.buf.at[t], d, sib)]

        def arrived(self, block, h):
            view = self.view(block, h)
            pltpu.make_async_remote_copy(
                src_ref=view, dst_ref=view, send_sem=ssem.at[0], recv_sem=rsem.at[self.base + 4 * h + block],
                device_id=(d, sib), device_id_type=MESH,
            ).wait_recv()

        def forward(self, block, h):
            cp = self.to(block, near_end, h)
            self.forwards.append(cp)

            @pl.when(is_mid == 1)
            def _():
                self.arrived(block, h)
                cp.start()

        def finish(self):
            for h in range(self.parts):

                @pl.when(is_mid == 0)
                def _(h=h):
                    self.arrived(far_mid, h)
                    self.arrived(far_end, h)

                self.arrived(partner, h)
            for zz in (far_mid, far_end, partner):
                self.siblings.append(send(self.buf.at[2 * zz + c], self.buf.at[2 * zz + c], d, sib))
            for cp in self.siblings:
                cp.wait_recv()

        def drain(self):
            @pl.when(is_mid == 1)
            def _():
                for cp in self.forwards:
                    cp.wait_send()

    order = (
        far_end + is_mid * (near_end - far_end),
        far_mid + is_mid * (far_end - far_mid),
        near_mid + is_mid * (far_mid - near_mid),
    )

    class Summed:
        def __init__(self, out, arrive):
            self.out, self.arrive = out, arrive
            self.base = take(4)
            to = (partner, near_mid + is_mid * (far_end - near_mid), near_mid + is_mid * (far_mid - near_mid))
            slot = (2 * is_mid, 1 + 2 * is_mid, 2 + is_mid)
            self.cps = [copy(out.at[n], arrive.at[slot[n]], d, 2 * to[n] + c, self.base + slot[n]) for n in range(3)]
            pending.extend(self.cps)

        def wait(self, n):
            view = self.arrive.at[n]
            pltpu.make_async_remote_copy(
                src_ref=view, dst_ref=view, send_sem=ssem.at[0], recv_sem=rsem.at[self.base + n], device_id=(d, sib), device_id_type=MESH
            ).wait_recv()

        def start(self):
            self.cps[0].start()

            @pl.when(is_mid == 0)
            def _():
                self.cps[1].start()
                self.cps[2].start()

        def add(self, n):
            @pl.when(is_mid == 1)
            def _():
                self.wait(n)
                self.out[n + 1] = (self.out[n + 1].astype(f32) + self.arrive[n].astype(f32)).astype(bf16)
                self.cps[n + 1].start()

        def result(self, own):
            self.wait(2)
            self.wait(3)
            return own + self.arrive[2].astype(f32) + self.arrive[3].astype(f32)

    def zpeer(k):
        return 2 * ((z + k) % 4) + c

    def dpeer(k):
        return (d + k) % 4

    barrier = pltpu.get_barrier_semaphore()
    for k in range(1, 8):
        pl.semaphore_signal(barrier, 1, device_id=(d, (t + k) % 8), device_id_type=MESH)
    for k in range(1, 4):
        pl.semaphore_signal(barrier, 1, device_id=(dpeer(k), t), device_id_type=MESH)

    WBLK[...] = mm(eye(32), reduce_weight[...], 1, 1).astype(bf16)
    CB[:, 0:2304] = mm(eye(32), conv_weight[...], 1, 1).astype(bf16)
    CB[:, 2304:3328] = expand_weight[...]
    eighth = jnp.full((8, 128), 0.125, f32)
    lane = lax.broadcasted_iota(jnp.int32, (32, 128), 1)
    packed = jnp.zeros((32, 128), f32)
    for n, gain in enumerate((gain_middle, gain_inner)):
        column = mm(jnp.broadcast_to(gain[...], (8, 32)), eighth, 0, 0, HIGHEST)
        high, rest = split(column)
        rest = column - high.astype(f32)
        mid, low = split(rest)
        for m, part in enumerate((high, mid, low)):
            packed = jnp.where(lane == 3 * n + m, part.astype(f32), packed)
    CB[:, 3328:3456] = packed.astype(bf16)
    CB[:, 3456:3584] = jnp.zeros((32, 128), bf16)
    pl.semaphore_wait(barrier, 10)

    w_cp = []
    for k in range(1, 8):
        s = (t + k) % 8
        w_cp.append(send(WBLK.at[:, pl.ds(pl.multiple_of(256 * (s // 2), 256), 256)], WT.at[pl.ds(pl.multiple_of(32 * t, 32), 32)], d, s))
    WT[pl.ds(pl.multiple_of(32 * t, 32), 32), :] = WBLK[:, pl.ds(pl.multiple_of(256 * z, 256), 256)]
    quarter = CB.at[:, pl.ds(pl.multiple_of(896 * d, 128), 896)]
    wq_cp = [send(quarter, WQ.at[z], d, zpeer(k)) for k in range(1, 4)]
    WQ[z] = quarter[...]

    go_rows = jnp.broadcast_to(gain_outer[...], (8, 128))
    go = mm(go_rows, eighth, 0, 0, HIGHEST)[:, 0:1]
    pos = position[...]
    pos_pair = mm(eye(128, f32), jnp.concatenate([pos, pos], axis=0), 1, 1, HIGHEST)
    x_cp = []
    for p in (*order, z):
        cols = pl.ds(pl.multiple_of(1152 * p, 128), 1152)
        x = features[:, cols].astype(f32) + pos_pair
        PLC[:, cols] = x
        m = jnp.mean(x, axis=0, keepdims=True)
        x = x - m
        q = jnp.sum(x * x, axis=0, keepdims=True)
        x = (x * go).astype(bf16)
        for par, lo in ((0, 0), (1, 512)):
            XW[par, p] = x[:, lo : lo + 640]
            ST[2 * p + par, 0:1, :] = m[:, lo : lo + 640]
            ST[2 * p + par, 1:2, :] = q[:, lo : lo + 640]
        x_cp.append(send(XW.at[1 - c, p], XK.at[p, pl.ds(pl.multiple_of(128 * c, 128), 128)], d, sib))
        XK[p, pl.ds(pl.multiple_of(128 * c, 128), 128), :] = XW[c, p]

    for cp in w_cp:
        cp.wait_recv()
    WC[...] = mm(eye(256), WT[...], 1, 1).astype(bf16)
    mine = WC[pl.ds(pl.multiple_of(128 * c, 128), 128), :].astype(f32)
    colsum = mm(go_rows, mine, 1, 0, HIGHEST)[0:1]
    for n in range(8):
        ST[n, 2:3, 0:256] = colsum
    st_cp = [send(ST.at[(t + k) % 8], SR.at[t], d, (t + k) % 8) for k in range(1, 8)]
    SR[t] = ST[t]
    for n, p in enumerate((*order, z)):
        x_cp[n].wait_recv()
        QF[...] = mm(XK[p], WC[...], 0, 0)
        part = QF[pl.ds(pl.multiple_of(64 * c, 64), 576), :]
        if n == 3:
            QO[...] = part
        else:
            QS[n] = part.astype(bf16)
    reduced_sum = Summed(QS, QR)
    reduced_sum.start()

    POOL[...] = pool_pair()
    for p in range(4):
        high, low = split(PLC[:, 1152 * p : 1152 * (p + 1)])
        PP[t, 288 * p : 288 * (p + 1), :] = (mm(POOL[...], high, 1, 1) + mm(POOL[...], low, 1, 1)).astype(bf16)
    placed_gather = Gather(PP, 1)
    placed_gather.start()

    for cp in wq_cp:
        cp.wait_recv()
    wb_cp = [send(WQ, WB.at[c, d], dpeer(k), t) for k in range(1, 4)]
    WB[c, d] = WQ[...]
    reduced_sum.add(0)
    placed_gather.forward(far_mid, 0)
    reduced_sum.add(1)
    for cp in wb_cp:
        cp.wait_recv()
    ws_cp = send(WB.at[c], WB.at[c], d, sib)
    ws_cp.wait_recv()
    for cc in range(2):
        for zz in range(4):
            for dd in range(4):
                WF[32 * (2 * zz + cc) : 32 * (2 * zz + cc + 1), 896 * dd : 896 * (dd + 1)] = WB[cc, dd, zz]
    lane = lax.broadcasted_iota(jnp.int32, (8, 128), 1)
    row = lax.broadcasted_iota(jnp.int32, (8, 128), 0)
    pick = jnp.where((lane >= 3 * row) & (lane < 3 * row + 3) & (row < 2), 1.0, 0.0).astype(bf16)
    gains = mm(pick, WF[:, 3328:3456], 1, 1)
    gm, gi = gains[0:1], gains[1:2]
    MT[...] = mm(readout_weight[...], WF[:, 2304:3328], 1, 1).astype(bf16)

    for cp in st_cp:
        cp.wait_recv()
    m_t = SR[:, 0, :]
    q_t = SR[:, 1, :]
    sums = SR[:, 2, 0:256]
    mean = jnp.mean(m_t, axis=0, keepdims=True)
    dm = m_t - mean
    var = (jnp.sum(q_t, axis=0, keepdims=True) + 128.0 * jnp.sum(dm * dm, axis=0, keepdims=True)) * (1.0 / 1024.0)
    rstd = lax.rsqrt(var + epsilon)
    valid = pl.ds(pl.multiple_of(64 * c, 64), 576)
    QF[...] = mm(dm, sums, 0, 0, HIGHEST)
    total = QO[...] + QF[valid, :]
    QF[...] = mm(jnp.broadcast_to(rstd, (8, 640)), jnp.full((8, 256), 0.125, f32), 0, 0, HIGHEST)
    scale = QF[valid, :]
    total = reduced_sum.result(total)
    RED[...] = jnp.zeros((24, 32, 256), f32)
    RED[:, 0:24, :] = (total * scale).reshape(24, 24, 256)

    xm, rm = norm_rows(RED[...].reshape(768, 256))
    zm = xm * gm
    hidden = zm * jax.nn.sigmoid(zm)
    XM[...], ZM[...], RM[...] = xm, zm, jnp.broadcast_to(rm, (768, 128))
    HB[0:32, :] = jnp.zeros((32, 768), bf16)
    HB[800:832, :] = jnp.zeros((32, 768), bf16)
    HB[32:800, 0:256] = pltpu.roll(hidden, 1, 0).astype(bf16)
    HB[32:800, 256:512] = hidden.astype(bf16)
    HB[32:800, 512:768] = pltpu.roll(hidden, 767, 0).astype(bf16)
    conv = mm(HB[0:768, :], WF[:, 0:768], 1, 1)
    conv += mm(HB[32:800, :], WF[:, 768:1536], 1, 1)
    conv += mm(HB[64:832, :], WF[:, 1536:2304], 1, 1)
    xi, ri = norm_rows(conv)
    zi = xi * gi
    activated = (zi * jax.nn.sigmoid(zi)).astype(bf16)
    XI[...], ZI[...], RI[...] = xi, zi, jnp.broadcast_to(ri, (768, 128))
    pool = pool_wide()
    ACT[t] = mm(pool, activated, 1, 0).astype(bf16)
    a_cp = [send(ACT.at[t], ACT.at[t], d, zpeer(k)) for k in range(1, 4)]
    as_cp = [send(ACT.at[t], ACT.at[t], d, sib)]

    placed_gather.forward(far_end, 0)
    placed_gather.finish()
    before = jnp.zeros((512, 1152), f32)
    for q in range(4):
        both = jnp.concatenate([PP[2 * q], PP[2 * q + 1]], axis=1)
        before += mm(readout_weight[:, 256 * q : 256 * (q + 1)], both, 1, 1)
    BEF[...] = before

    for k in range(1, 4):
        a_cp[k - 1].wait_recv()
        slot = 2 * ((z + 4 - k) % 4) + c
        as_cp.append(send(ACT.at[slot], ACT.at[slot], d, sib))
    for cp in as_cp:
        cp.wait_recv()
    for n in range(8):
        ACL[n] = (ACT[n].astype(f32) * slot_live[n].astype(f32)).astype(bf16)
    act_live = ACL[...].reshape(1152, 256)
    BEF[...] += mm(MT[...], act_live, 1, 1)

    @pl.loop(0, 16)
    def _(u):
        rows = pl.ds(pl.multiple_of(32 * u, 32), 32)
        b = BEF[rows, :]
        below = 0.5 * (1.0 + lax.erf(b * 0.7071067811865476))
        density = jnp.exp(-0.5 * b * b) * 0.3989422804014327
        readout_o[rows, :] = (b * below).astype(bf16)
        GBT[rows, :] = (cotangent[rows, :].astype(f32) * (below + b * density)).astype(bf16)

    terms = mm(GBT[...], MT[...], 0, 0).astype(bf16).reshape(8, 144, 256)
    for n in range(8):
        AT[n % 2, n // 2] = terms[n]
    at_cp = send(AT.at[1 - c], AR, d, sib)
    for q in range(4):
        block = mm(GBT[...], readout_weight[:, 256 * q : 256 * (q + 1)], 0, 0).astype(bf16)
        TE[0, q] = block[:, 0:128]
        TE[1, q] = block[:, 128:256]
    at_cp.wait_recv()
    az_cp = []
    for k in (1, 2, 3):
        p = (z + k) % 4
        AS[k - 1] = (AT[c, p].astype(f32) + AR[p].astype(f32)).astype(bf16)
        az_cp.append(send(AS.at[k - 1], AZ.at[k - 1], d, zpeer(k)))
    te_cp = send(TE.at[1 - c], TR, d, sib)
    grad_act = AT[c, z].astype(f32) + AR[z].astype(f32)
    for q in range(4):
        both = jnp.concatenate([PP[2 * q], PP[2 * q + 1]], axis=1).astype(f32)
        POOLED[:, 256 * q : 256 * (q + 1)] = (both + mm(act_live, WF[:, 2304 + 256 * q : 2560 + 256 * q], 1, 0)).astype(bf16)
    for q in range(4):
        GR[q] = mm(GBT[128 * q : 128 * (q + 1), :], POOLED[...], 1, 0).astype(bf16)
    gr_cp = [send(GR.at[(d + k) % 4], GRR.at[d], dpeer(k), t) for k in range(1, 4)]
    GRR[d] = GR[d]
    te_cp.wait_recv()
    for n, p in enumerate(order):
        ES[n] = (TE[c, p].astype(f32) + TR[p].astype(f32)).astype(bf16)
    pooled_sum = Summed(ES, ER)
    pooled_sum.start()
    GP[...] = TE[c, z].astype(f32) + TR[z].astype(f32)

    for cp in az_cp:
        cp.wait_recv()
    for k in range(3):
        grad_act += AZ[k].astype(f32)
    pooled_sum.add(0)
    high, low = split(grad_act * slot_live[t].astype(f32))
    grad_rows = mm(pool, high, 0, 0) + mm(pool, low, 0, 0)
    zi = ZI[...]
    gate = jax.nn.sigmoid(zi)
    dy = grad_rows * (gate * (1.0 + zi * (1.0 - gate)))
    xi = XI[...]
    dyx_inner = dy * xi
    gc = norm_rows_back(dy * gi, xi, RI[:, 0:1]).astype(bf16)
    GB[0:32, :] = jnp.zeros((32, 256), bf16)
    GB[800:832, :] = jnp.zeros((32, 256), bf16)
    GB[32:800, :] = gc
    back = mm(GB[64:832, :], WF[:, 0:768], 1, 0)
    back += mm(GB[32:800, :], WF[:, 768:1536], 1, 0)
    back += mm(GB[0:768, :], WF[:, 1536:2304], 1, 0)
    grad_hidden = pltpu.roll(back[:, 0:256], 767, 0) + back[:, 256:512] + pltpu.roll(back[:, 512:768], 1, 0)
    zm = ZM[...]
    gate = jax.nn.sigmoid(zm)
    inside = (lax.broadcasted_iota(jnp.int32, (768, 256), 0) & 31) < 24
    dy = jnp.where(inside, grad_hidden * (gate * (1.0 + zm * (1.0 - gate))), 0.0)
    xm = XM[...]
    dyx_middle = dy * xm
    gr = norm_rows_back(dy * gm, xm, RM[:, 0:1]).reshape(24, 32, 256)[:, 0:24, :].reshape(576, 256).astype(bf16)
    GA[t] = gr
    grad_gather = Gather(GA, 2)
    grad_gather.start()
    pooled_sum.add(1)
    QF[...] = jnp.zeros((640, 256), f32)
    QF[valid, :] = gr.astype(f32)
    wg = jnp.sum(sums, axis=0, keepdims=True)
    s1 = mm(jnp.broadcast_to(wg, (8, 256)), QF[...], 1, 1, HIGHEST)[0:1]
    QF[valid, :] = gr.astype(f32) * RED[:, 0:24, :].reshape(576, 256)
    s2 = mm(jnp.ones((8, 256), f32), QF[...], 1, 1, HIGHEST)[0:1]
    RS[t, 0:1, :] = mean
    RS[t, 1:2, :] = rstd
    RS[t, 2:3, :] = s1 * (1.0 / 1024.0)
    RS[t, 3:4, :] = s2 * (1.0 / 1024.0)
    rs_cp = [send(RS.at[t], RS.at[t], d, (t + k) % 8) for k in range(1, 8)]

    def put(lo, value):
        value = value.astype(bf16)
        for n in range(8):
            CG[n % 2, n // 2, :, lo : lo + value.shape[1]] = value[32 * n : 32 * (n + 1)]

    for a in range(3):
        put(768 * a, mm(gc, HB[32 * a : 32 * a + 768, :], 0, 0))
    ones = jnp.ones((768, 128), bf16)
    for lo, value in ((2304, dyx_inner), (2432, dyx_middle)):
        high, low = split(value)
        put(lo, mm(high, ones, 0, 0) + mm(low, ones, 0, 0))
    cg_cp = send(CG.at[1 - c], CGR, d, sib)

    for cp in gr_cp:
        cp.wait_recv()
    total = GRR[0].astype(f32)
    for n in range(1, 4):
        total += GRR[n].astype(f32)
    GRF[d] = total.astype(bf16)
    grf_cp = [send(GRF.at[d], GRF.at[d], dpeer(k), t) for k in range(1, 4)]

    cg_cp.wait_recv()
    CGS[...] = (CG[c].astype(f32) + CGR[...].astype(f32)).astype(bf16)
    cgd_cp = []
    for k in range(1, 4):
        dd = dpeer(k)
        cgd_cp.append(send(CGS.at[:, :, pl.ds(pl.multiple_of(640 * dd, 128), 640)], CGD.at[d], dd, t))
    CGD[d] = CGS[:, :, pl.ds(pl.multiple_of(640 * d, 128), 640)]

    for h in range(2):
        grad_gather.forward(far_mid, h)
    for h in range(2):
        grad_gather.forward(far_end, h)
    for cp in cgd_cp:
        cp.wait_recv()
    total = CGD[0].astype(f32)
    for n in range(1, 4):
        total += CGD[n].astype(f32)
    CGT[...] = total.astype(bf16)
    cgz_cp = [send(CGT.at[(z + k) % 4], CGZ.at[z], d, zpeer(k)) for k in range(1, 4)]
    CGZ[z] = CGT[z]
    gp = pooled_sum.result(GP[...])
    gp_high, gp_low = split(gp)
    FT[0] = mm(act_live, gp_high, 0, 0).astype(bf16)
    for cp in cgz_cp:
        cp.wait_recv()
    total = CGZ[0].astype(f32)
    for n in range(1, 4):
        total += CGZ[n].astype(f32)
    CGF[d] = total.astype(bf16)
    cgf_cp = [send(CGF.at[d], CGF.at[d], dpeer(k), t) for k in range(1, 4)]
    for cp in rs_cp:
        cp.wait_recv()
    grad_gather.finish()
    w_own = WC[pl.ds(pl.multiple_of(128 * c, 128), 128), :]
    lane = lax.broadcasted_iota(jnp.int32, (4, 128), 1)
    place_sum = jnp.zeros((128, 1152), f32)
    gain_sum = jnp.zeros((128, 1), f32)
    grad_reduce = jnp.zeros((128, 256), f32)
    for p in range(4):
        cols = slice(1152 * p, 1152 * (p + 1))
        even, odd = RS[2 * p], RS[2 * p + 1]
        stats = jnp.concatenate([even[:, 0:512], jnp.where(lane < 64, even[:, 512:640], odd[:, 0:128]), odd[:, 128:640]], axis=1)
        g = GA[2 * p : 2 * p + 2].reshape(1152, 256)
        gn = mm(w_own, g, 1, 1)
        xhat = (PLC[:, cols] - stats[0:1]) * stats[1:2]
        gain_sum += jnp.sum(gn * xhat, axis=1, keepdims=True)
        grad_reduce += mm((xhat * go).astype(bf16), g, 1, 0)
        spread = mm(gp_high[288 * p : 288 * (p + 1)], POOL[...], 0, 0) + mm(gp_low[288 * p : 288 * (p + 1)], POOL[...], 0, 0)
        out = spread + stats[1:2] * (gn * go - stats[2:3] - xhat * stats[3:4])
        gfeat_o[:, cols] = out
        place_sum += out
    FT[1] = jnp.transpose(grad_reduce).astype(bf16)
    ft_cp = []
    for k in range(1, 8):
        s = (t + k) % 8
        ft_cp.append(send(FT.at[:, pl.ds(pl.multiple_of(32 * s, 32), 32)], TA.at[d, t], d, s))
    TA[d, t] = FT[:, pl.ds(pl.multiple_of(32 * t, 32), 32), :]
    odd = pltpu.roll(place_sum, 576, 1)
    lane = lax.broadcasted_iota(jnp.int32, (128, 640), 1)
    PM[d] = jnp.where(lane < 576, place_sum[:, 0:640] + odd[:, 0:640], jnp.broadcast_to(gain_sum, (128, 640))).astype(bf16)
    pm_cp = [send(PM.at[d], PM.at[d], dpeer(k), t) for k in range(1, 4)]
    for cp in ft_cp:
        cp.wait_recv()
    ta_cp = [send(TA.at[d], TA.at[d], dpeer(k), t) for k in range(1, 4)]

    for cp in grf_cp:
        cp.wait_recv()
    for q in range(4):
        gread_o[128 * q : 128 * (q + 1), :] = GRF[q].astype(f32)
    for cp in cgf_cp:
        cp.wait_recv()
    for q in range(4):
        gconv_o[:, 640 * q : 640 * (q + 1)] = CGF[q].astype(f32)
    for cp in pm_cp:
        cp.wait_recv()
    total = PM[0].astype(f32)
    for n in range(1, 4):
        total += PM[n].astype(f32)
    gpos_o[...] = jnp.transpose(total)
    for cp in ta_cp:
        cp.wait_recv()
    for s in range(8):
        total = TA[0, s].astype(f32)
        for n in range(1, 4):
            total += TA[n, s].astype(f32)
        gexp_o[:, 128 * s : 128 * (s + 1)] = total[0]
        gred_o[:, 128 * s : 128 * (s + 1)] = total[1]
    for cp in pending:
        cp.wait_send()
    placed_gather.drain()
    grad_gather.drain()


SCRATCH = (
    ("WBLK", (32, 1024), bf16), ("WT", (256, 256), bf16), ("WC", (256, 256), bf16), ("CB", (32, 3584), bf16),
    ("WQ", (4, 32, 896), bf16), ("WB", (2, 4, 4, 32, 896), bf16), ("WF", (256, 3584), bf16), ("MT", (512, 256), bf16),
    ("POOL", (288, 1152), bf16), ("PLC", (128, 4608), f32), ("XW", (2, 4, 128, 640), bf16), ("XK", (4, 256, 640), bf16),
    ("ST", (8, 4, 640), f32), ("SR", (8, 4, 640), f32), ("QF", (640, 256), f32), ("QS", (3, 576, 256), bf16),
    ("QO", (576, 256), f32), ("QR", (4, 576, 256), bf16), ("RED", (24, 32, 256), f32), ("HB", (832, 768), bf16),
    ("GB", (832, 256), bf16), ("XM", (768, 256), f32), ("ZM", (768, 256), f32), ("RM", (768, 128), f32),
    ("XI", (768, 256), f32), ("ZI", (768, 256), f32), ("RI", (768, 128), f32), ("ACT", (8, 144, 256), bf16), ("ACL", (8, 144, 256), bf16),
    ("PP", (8, 1152, 128), bf16), ("POOLED", (1152, 1024), bf16), ("BEF", (512, 1152), f32), ("GBT", (512, 1152), bf16),
    ("TE", (2, 4, 1152, 128), bf16), ("TR", (4, 1152, 128), bf16), ("ES", (3, 1152, 128), bf16), ("ER", (4, 1152, 128), bf16),
    ("GP", (1152, 128), f32), ("AT", (2, 4, 144, 256), bf16), ("AR", (4, 144, 256), bf16), ("AS", (3, 144, 256), bf16),
    ("AZ", (3, 144, 256), bf16), ("GW", (8, 128), f32), ("GA", (8, 576, 256), bf16), ("RS", (8, 4, 640), f32),
    ("FT", (2, 256, 128), bf16), ("TA", (4, 8, 2, 32, 128), bf16), ("PM", (4, 128, 640), bf16),
    ("CG", (2, 4, 32, 2560), bf16), ("CGR", (4, 32, 2560), bf16), ("CGS", (4, 32, 2560), bf16), ("CGD", (4, 4, 32, 640), bf16),
    ("CGT", (4, 32, 640), bf16), ("CGZ", (4, 32, 640), bf16), ("CGF", (4, 32, 640), bf16), ("GR", (4, 128, 1024), bf16), ("GRR", (4, 128, 1024), bf16),
    ("GRF", (4, 128, 1024), bf16),
)


def local_by_image(features, slot_live, position, gain_outer, reduce_weight, gain_middle, conv_weight, gain_inner, expand_weight, readout_weight, cotangent):
    vmem = pl.BlockSpec(memory_space=pltpu.VMEM)
    smem = pl.BlockSpec(memory_space=pltpu.SMEM)
    readout, gfeat, gpos, gexp, gred, gconv, gread = pl.pallas_call(
        kernel,
        out_shape=(
            jax.ShapeDtypeStruct((512, 1152), bf16), jax.ShapeDtypeStruct((128, 4608), f32), jax.ShapeDtypeStruct((640, 128), f32),
            jax.ShapeDtypeStruct((32, 1024), f32), jax.ShapeDtypeStruct((32, 1024), f32), jax.ShapeDtypeStruct((32, 2560), f32),
            jax.ShapeDtypeStruct((512, 1024), f32),
        ),
        in_specs=[vmem, smem] + [vmem] * 9,
        out_specs=[vmem] * 7,
        scratch_shapes=[pltpu.VMEM(shape, dtype) for _, shape, dtype in SCRATCH]
        + [pltpu.SemaphoreType.DMA((COPIES,)), pltpu.SemaphoreType.DMA((COPIES,))],
        compiler_params=pltpu.CompilerParams(collective_id=0, has_side_effects=True, vmem_limit_bytes=63 * 2**20),
    )(
        features, slot_live, position.reshape(576, 128), gain_outer.reshape(1, 128), reduce_weight, gain_middle.reshape(1, 32),
        conv_weight.reshape(2304, 32), gain_inner.reshape(1, 32), expand_weight, readout_weight, cotangent,
    )
    return (
        readout, gfeat, gpos[0:576].reshape(24, 24, 128), gpos[576], gred.T, gconv[:, 2432],
        gconv[:, 0:2304].T.reshape(3, 3, 256, 32), gconv[:, 2304], gexp, gread,
    )


def row_totals(leading, trailing):
    return lax.psum((leading, trailing), "tensor")


def norm_forward(values, norm_gain, breadth):
    totals, squares = row_totals(jnp.sum(values, axis=1), jnp.sum(values * values, axis=1))
    center = totals / breadth
    spread = squares / breadth - center * center
    scaled = lax.rsqrt(spread + epsilon)[:, None]
    normed = (values - center[:, None]) * scaled
    return (normed, scaled, normed * norm_gain)


def norm_backward(grad_out, normed, scaled, norm_gain, breadth):
    grad_normed = grad_out * norm_gain
    gain_grad = jnp.sum(grad_out * normed, axis=0)
    leading, trailing = row_totals(
        jnp.sum(grad_normed, axis=1), jnp.sum(grad_normed * normed, axis=1)
    )
    grad_in = scaled * (
        grad_normed - leading[:, None] / breadth - normed * (trailing[:, None] / breadth)
    )
    return (grad_in, gain_grad)


def silu_grad(inputs):
    gate_value = jax.nn.sigmoid(inputs)
    return gate_value * (1.0 + inputs * (1.0 - gate_value))


def gelu_grad(inputs):
    below = 0.5 * (1.0 + lax.erf(inputs * 0.7071067811865476))
    density = jnp.exp(-0.5 * inputs * inputs) * 0.3989422804014327
    return below + inputs * density


def contract_rows(left_side, right_side):
    return lax.dot_general(
        left_side, right_side, (((0,), (0,)), ((), ())), preferred_element_type=jnp.float32
    )


def window_of(padded, shift_down, shift_across, grid_side):
    images = padded.shape[0]
    breadth = padded.shape[3]
    return padded[
        :, shift_down : shift_down + grid_side, shift_across : shift_across + grid_side, :
    ].reshape(images * grid_side * grid_side, breadth)


def local_by_hidden(
    features,
    slot_live,
    position,
    gain_outer,
    reduce_weight,
    gain_middle,
    conv_weight,
    gain_inner,
    expand_weight,
    readout_weight,
    cotangent,
):
    grid_side = position.shape[0]
    half_side = grid_side // 2
    channel_share = features.shape[0]
    row_count = features.shape[1]
    images = row_count // (grid_side * grid_side)
    tensor_size = lax.axis_size("tensor")
    channels = channel_share * tensor_size
    hidden_share = reduce_weight.shape[1]
    hidden_width = hidden_share * tensor_size
    pooled_count = images * half_side * half_side
    placed = (
        features.T.astype(jnp.float32).reshape(images, grid_side * grid_side, channel_share)
        + position.reshape(1, grid_side * grid_side, channel_share)
    ).reshape(row_count, channel_share)
    live_rows = jnp.repeat(slot_live.astype(jnp.float32), grid_side * grid_side)[:, None]
    normed_outer, scaled_outer, shaped_outer = norm_forward(placed, gain_outer, channels)
    reduce_in = shaped_outer.astype(jnp.bfloat16)
    reduce_full = lax.all_gather(reduce_in, "tensor", axis=1, tiled=True)
    reduced = jnp.dot(reduce_full, reduce_weight, preferred_element_type=jnp.float32)
    normed_middle, scaled_middle, shaped_middle = norm_forward(reduced, gain_middle, hidden_width)
    hidden = jax.nn.silu(shaped_middle).astype(jnp.bfloat16)
    hidden_full = lax.all_gather(hidden, "tensor", axis=1, tiled=True)
    padded_hidden = jnp.pad(
        hidden_full.reshape(images, grid_side, grid_side, hidden_width),
        ((0, 0), (1, 1), (1, 1), (0, 0)),
    )
    convolved = jnp.zeros((row_count, hidden_share), jnp.float32)
    for offset_tap in range(9):
        shift_down = offset_tap // 3
        shift_across = offset_tap % 3
        convolved = convolved + jnp.dot(
            window_of(padded_hidden, shift_down, shift_across, grid_side),
            conv_weight[shift_down, shift_across],
            preferred_element_type=jnp.float32,
        )
    normed_inner, scaled_inner, shaped_inner = norm_forward(convolved, gain_inner, hidden_width)
    activated = jax.nn.silu(shaped_inner).astype(jnp.bfloat16)
    expand_terms = jnp.dot(activated, expand_weight, preferred_element_type=jnp.float32)
    expanded = lax.psum_scatter(expand_terms, "tensor", scatter_dimension=1, tiled=True)
    mixed = placed + live_rows * expanded
    pooled = jnp.mean(mixed.reshape(images, half_side, 2, half_side, 2, channel_share), axis=(2, 4))
    pooled_low = pooled.reshape(pooled_count, channel_share).astype(jnp.bfloat16)
    pooled_full = lax.all_gather(pooled_low, "tensor", axis=1, tiled=True)
    before = lax.dot_general(
        pooled_full, readout_weight, (((1,), (1,)), ((), ())), preferred_element_type=jnp.float32
    )
    readout = jax.nn.gelu(before, approximate=False).astype(jnp.bfloat16).T
    grad_before = (cotangent.T.astype(jnp.float32) * gelu_grad(before)).astype(jnp.bfloat16)
    grad_readout = contract_rows(grad_before, pooled_full)
    pooled_terms = jnp.dot(grad_before, readout_weight, preferred_element_type=jnp.float32)
    grad_pooled = lax.psum_scatter(pooled_terms, "tensor", scatter_dimension=1, tiled=True)
    spread_grad = jnp.broadcast_to(
        (0.25 * grad_pooled).reshape(images, half_side, 1, half_side, 1, channel_share),
        (images, half_side, 2, half_side, 2, channel_share),
    )
    grad_mixed = spread_grad.reshape(row_count, channel_share)
    grad_branch = (live_rows * grad_mixed).astype(jnp.bfloat16)
    grad_full = lax.all_gather(grad_branch, "tensor", axis=1, tiled=True)
    grad_expand = contract_rows(activated, grad_full)
    grad_activated = jnp.dot(grad_full, expand_weight.T, preferred_element_type=jnp.float32)
    grad_convolved, grad_gain_inner = norm_backward(
        grad_activated * silu_grad(shaped_inner),
        normed_inner,
        scaled_inner,
        gain_inner,
        hidden_width,
    )
    grad_conv_low = grad_convolved.astype(jnp.bfloat16)
    tap_grads = []
    grad_padded = jnp.zeros((images, grid_side + 2, grid_side + 2, hidden_width), jnp.float32)
    for offset_tap in range(9):
        shift_down = offset_tap // 3
        shift_across = offset_tap % 3
        tap_grads.append(
            contract_rows(
                window_of(padded_hidden, shift_down, shift_across, grid_side), grad_conv_low
            )
        )
        tap_back = jnp.dot(
            grad_conv_low,
            conv_weight[shift_down, shift_across].T,
            preferred_element_type=jnp.float32,
        )
        grad_padded = grad_padded + jnp.pad(
            tap_back.reshape(images, grid_side, grid_side, hidden_width),
            ((0, 0), (shift_down, 2 - shift_down), (shift_across, 2 - shift_across), (0, 0)),
        )
    grad_conv = jnp.stack(tap_grads, axis=0).reshape(conv_weight.shape)
    grad_window = grad_padded[:, 1 : grid_side + 1, 1 : grid_side + 1, :].reshape(
        row_count, hidden_width
    )
    grad_hidden = lax.psum_scatter(grad_window, "tensor", scatter_dimension=1, tiled=True)
    grad_reduced, grad_gain_middle = norm_backward(
        grad_hidden * silu_grad(shaped_middle),
        normed_middle,
        scaled_middle,
        gain_middle,
        hidden_width,
    )
    grad_reduced_low = grad_reduced.astype(jnp.bfloat16)
    grad_reduce = contract_rows(reduce_full, grad_reduced_low)
    outer_terms = jnp.dot(grad_reduced_low, reduce_weight.T, preferred_element_type=jnp.float32)
    grad_shaped_outer = lax.psum_scatter(outer_terms, "tensor", scatter_dimension=1, tiled=True)
    grad_inputs, grad_gain_outer = norm_backward(
        grad_shaped_outer, normed_outer, scaled_outer, gain_outer, channels
    )
    grad_rows = grad_mixed + grad_inputs
    grad_place = jnp.sum(grad_rows.reshape(images, grid_side, grid_side, channel_share), axis=0)
    grad_total = grad_rows.T
    summed = (
        lax.psum(grad_place.astype(jnp.bfloat16), "dp").astype(jnp.float32),
        lax.psum(grad_gain_outer.astype(jnp.bfloat16), "dp").astype(jnp.float32),
        lax.psum(grad_reduce.astype(jnp.bfloat16), "dp").astype(jnp.float32),
        lax.psum(grad_gain_middle.astype(jnp.bfloat16), "dp").astype(jnp.float32),
        lax.psum(grad_conv.astype(jnp.bfloat16), "dp").astype(jnp.float32),
        lax.psum(grad_gain_inner.astype(jnp.bfloat16), "dp").astype(jnp.float32),
        lax.psum(grad_expand.astype(jnp.bfloat16), "dp").astype(jnp.float32),
        lax.psum(grad_readout.astype(jnp.bfloat16), "dp").astype(jnp.float32),
    )
    return (
        readout,
        grad_total,
        summed[0],
        summed[1],
        summed[2],
        summed[3],
        summed[4],
        summed[5],
        summed[6],
        summed[7],
    )


def solution(mesh):
    parts, groups = mesh.shape["tensor"], mesh.shape["dp"]
    specs = (P("tensor", "dp"), P("dp"), P(None, None, "tensor"), P("tensor"), P(None, "tensor"), P("tensor"), P(None, None, None, "tensor"), P("tensor"), P("tensor", None), P("tensor", None), P("tensor", "dp"))

    def whole(*arrays):
        by_image = (parts, groups) == (8, 4) and arrays[1].shape[0] == parts * groups
        return jax.shard_map(
            local_by_image if by_image else local_by_hidden, mesh=mesh, in_specs=specs,
            out_specs=(P("tensor", "dp"), P("tensor", "dp"), *specs[2:10]), check_vma=False,
        )(*arrays)

    return whole
```

```python
import jax
import jax.numpy as jnp
from jax import lax
from jax.experimental import pallas as pl
from jax.experimental.pallas import tpu as pltpu
from jax.sharding import PartitionSpec as P

epsilon = 1e-05
bf16 = jnp.bfloat16
f32 = jnp.float32
COPIES = 160

MESH = pl.DeviceIdType.MESH
HIGHEST = lax.Precision.HIGHEST


def mm(a, b, ca, cb, precision=None):
    return lax.dot_general(a, b, (((ca,), (cb,)), ((), ())), precision=precision, preferred_element_type=f32)


def split(x):
    high = x.astype(bf16)
    return high, (x - high.astype(f32)).astype(bf16)


def eye(n, dtype=bf16):
    return (lax.broadcasted_iota(jnp.int32, (n, n), 0) == lax.broadcasted_iota(jnp.int32, (n, n), 1)).astype(f32).astype(dtype)


def pool_wide():
    spot = lax.broadcasted_iota(jnp.int32, (144, 768), 1)
    cell = lax.broadcasted_iota(jnp.int32, (144, 768), 0)
    i, j = spot >> 5, spot & 31
    return jnp.where(((i >> 1) * 12 + (j >> 1) == cell) & (j < 24), 0.25, 0.0).astype(bf16)


def pool_pair():
    spot = lax.broadcasted_iota(jnp.int32, (288, 1152), 1)
    cell = lax.broadcasted_iota(jnp.int32, (288, 1152), 0)
    i = (spot * 2731) >> 16
    j = spot - i * 24
    return jnp.where((i >> 1) * 12 + (j >> 1) == cell, 0.25, 0.0).astype(bf16)


def norm_rows(v):
    s = v - jnp.mean(v, axis=1, keepdims=True)
    r = lax.rsqrt(jnp.mean(s * s, axis=1, keepdims=True) + epsilon)
    return s * r, r


def norm_rows_back(dx, xhat, r):
    return r * (dx - jnp.mean(dx, axis=1, keepdims=True) - xhat * jnp.mean(dx * xhat, axis=1, keepdims=True))


def kernel(
    features, slot_live, position, gain_outer, reduce_weight, gain_middle, conv_weight, gain_inner, expand_weight, readout_h, cotangent_h,
    readout_o, gfeat_o, gpos_o, gexp_o, gred_o, gconv_o, gread_o,
    readout_weight, cotangent, RO, GF, SP, WT, WC, CB, WQ, WB, WF, MT, POOL, PLC, XW, XK, ST, SR, QF, QS, QO, QR, RED, HB, GB,
    XM, ZM, RM, XI, ZI, RI, ACT, ACL, PP, POOLED, BEF, GBT, GBR, TE, TR, ES, ER, GP, AT, AR, AS, AZ,
    RSC, GA, RS, FT, TA, PM, PR, PF, CG, CGR, CGS, CGD, CGT, CGZ, CGF, GR, GRR, GRF, ssem, rsem, lsem,
):
    d = lax.axis_index("dp")
    t = lax.axis_index("tensor")
    z = t // 2
    c = t % 2
    sib = 2 * z + 1 - c
    side = z // 2
    is_mid = ((z + 1) // 2) % 2
    near_end, near_mid, far_end, far_mid = 3 * side, 1 + side, 3 - 3 * side, 2 - side
    partner = z + 1 - 2 * (z % 2)
    sends, arrivals = [0], [0]
    pending = []

    def copy(src, dst, dd, tt, arrival):
        cp = pltpu.make_async_remote_copy(
            src_ref=src, dst_ref=dst, send_sem=ssem.at[sends[0]], recv_sem=rsem.at[arrival], device_id=(dd, tt), device_id_type=MESH
        )
        sends[0] += 1
        return cp

    def take(n):
        arrivals[0] += n
        return arrivals[0] - n

    def send(src, dst, dd, tt):
        cp = copy(src, dst, dd, tt, take(1))
        cp.start()
        pending.append(cp)
        return cp

    class Gather:
        def __init__(self, buf, parts):
            self.buf, self.parts, self.rows = buf, parts, buf.shape[1] // parts
            self.base = take(4 * parts)
            self.forwards = []

        def view(self, zz, h):
            return self.buf.at[2 * zz + c, pl.ds(h * self.rows, self.rows)]

        def to(self, block, zz, h):
            return copy(self.view(block, h), self.view(block, h), d, 2 * zz + c, self.base + 4 * h + block)

        def start(self, zz):
            for h in range(self.parts):
                cp = self.to(z, zz, h)
                cp.start()
                pending.append(cp)

        def own(self):
            self.siblings = [send(self.buf.at[t], self.buf.at[t], d, sib)]

        def arrived(self, block, h):
            view = self.view(block, h)
            pltpu.make_async_remote_copy(
                src_ref=view, dst_ref=view, send_sem=ssem.at[0], recv_sem=rsem.at[self.base + 4 * h + block],
                device_id=(d, sib), device_id_type=MESH,
            ).wait_recv()

        def forward(self, block, h):
            cp = self.to(block, near_end, h)
            self.forwards.append(cp)

            @pl.when(is_mid == 1)
            def _():
                self.arrived(block, h)
                cp.start()

        def ready(self, n):
            if n > 0:
                block = (partner, far_mid, far_end)[n - 1]
                for h in range(self.parts):
                    if n == 1:
                        self.arrived(block, h)
                    else:

                        @pl.when(is_mid == 0)
                        def _(h=h):
                            self.arrived(block, h)

                slot = self.buf.at[2 * block + c]
                self.siblings.append(send(slot, slot, d, sib))
            self.siblings[n].wait_recv()

        def drain(self):
            @pl.when(is_mid == 1)
            def _():
                for cp in self.forwards:
                    cp.wait_send()

    order = (
        far_end + is_mid * (near_end - far_end),
        far_mid + is_mid * (far_end - far_mid),
        near_mid + is_mid * (far_mid - near_mid),
    )

    class Summed:
        def __init__(self, out, arrive):
            self.out, self.arrive = out, arrive
            self.base = take(4)
            to = (partner, near_mid + is_mid * (far_end - near_mid), near_mid + is_mid * (far_mid - near_mid))
            slot = (2 * is_mid, 1 + 2 * is_mid, 2 + is_mid)
            self.cps = [copy(out.at[n], arrive.at[slot[n]], d, 2 * to[n] + c, self.base + slot[n]) for n in range(3)]
            pending.extend(self.cps)

        def wait(self, n):
            view = self.arrive.at[n]
            pltpu.make_async_remote_copy(
                src_ref=view, dst_ref=view, send_sem=ssem.at[0], recv_sem=rsem.at[self.base + n], device_id=(d, sib), device_id_type=MESH
            ).wait_recv()

        def start(self, n):
            if n == 0:
                self.cps[0].start()
            else:

                @pl.when(is_mid == 0)
                def _():
                    self.cps[n].start()

        def add(self, n):
            @pl.when(is_mid == 1)
            def _():
                self.wait(n)
                self.out[n + 1] = (self.out[n + 1].astype(f32) + self.arrive[n].astype(f32)).astype(bf16)
                self.cps[n + 1].start()

        def result(self, own):
            self.wait(2)
            self.wait(3)
            return own + self.arrive[2].astype(f32) + self.arrive[3].astype(f32)

    def zpeer(k):
        return 2 * ((z + k) % 4) + c

    def dpeer(k):
        return (d + k) % 4

    operand_cp = [
        pltpu.make_async_copy(readout_h, readout_weight, lsem.at[0]),
        pltpu.make_async_copy(cotangent_h, cotangent, lsem.at[1]),
    ]
    for cp in operand_cp:
        cp.start()
    result_cp = []

    def store(src, dst):
        cp = pltpu.make_async_copy(src, dst, lsem.at[2 + len(result_cp)])
        cp.start()
        result_cp.append(cp)

    barrier = pltpu.get_barrier_semaphore()
    for k in range(1, 8):
        pl.semaphore_signal(barrier, 1, device_id=(d, (t + k) % 8), device_id_type=MESH)
    for k in range(1, 4):
        pl.semaphore_signal(barrier, 1, device_id=(dpeer(k), t), device_id_type=MESH)

    for n in range(9):
        CB[:, 256 * n : 256 * (n + 1)] = conv_weight[n]
    CB[:, 2304:3328] = expand_weight[...]
    eighth = jnp.full((8, 128), 0.125, f32)
    lane = lax.broadcasted_iota(jnp.int32, (32, 128), 1)
    packed = jnp.zeros((32, 128), f32)
    for n, gain in enumerate((gain_middle, gain_inner)):
        column = mm(jnp.broadcast_to(gain[...], (8, 32)), eighth, 0, 0, HIGHEST)
        high, rest = split(column)
        rest = column - high.astype(f32)
        mid, low = split(rest)
        for m, part in enumerate((high, mid, low)):
            packed = jnp.where(lane == 3 * n + m, part.astype(f32), packed)
    CB[:, 3328:3456] = packed.astype(bf16)
    CB[:, 3456:3584] = jnp.zeros((32, 128), bf16)
    POOL[...] = pool_pair()
    pl.semaphore_wait(barrier, 10)

    w_cp = []
    for k in range(1, 8):
        s = (t + k) % 8
        w_cp.append(send(reduce_weight.at[:, pl.ds(pl.multiple_of(256 * (s // 2), 256), 256)], WT.at[pl.ds(pl.multiple_of(32 * t, 32), 32)], d, s))
    WT[pl.ds(pl.multiple_of(32 * t, 32), 32), :] = reduce_weight[:, pl.ds(pl.multiple_of(256 * z, 256), 256)]
    quarter = CB.at[:, pl.ds(pl.multiple_of(896 * d, 128), 896)]
    wq_cp = [send(quarter, WQ.at[z], d, zpeer(k)) for k in range(1, 4)]
    WQ[z] = quarter[...]
    WB[c, d, z] = quarter[...]
    wb_cp = [send(WQ.at[z], WB.at[c, d, z], dpeer(k), t) for k in range(1, 4)]

    go_rows = jnp.broadcast_to(gain_outer[...], (8, 128))
    go = mm(go_rows, eighth, 0, 0, HIGHEST)[:, 0:1]
    pos = position[...]
    pos_pair = mm(eye(128, f32), jnp.concatenate([pos, pos], axis=0), 1, 1, HIGHEST)
    x_cp = []
    for p in (*order, z):
        cols = pl.ds(pl.multiple_of(1152 * p, 128), 1152)
        x = features[:, cols].astype(f32) + pos_pair
        PLC[:, cols] = x
        m = jnp.mean(x, axis=0, keepdims=True)
        x = x - m
        q = jnp.sum(x * x, axis=0, keepdims=True)
        x = (x * go).astype(bf16)
        for par, lo in ((0, 0), (1, 512)):
            XW[par, p] = x[:, lo : lo + 640]
            ST[2 * p + par, 0:1, :] = m[:, lo : lo + 640]
            ST[2 * p + par, 1:2, :] = q[:, lo : lo + 640]
        x_cp.append(send(XW.at[1 - c, p], XK.at[p, pl.ds(pl.multiple_of(128 * c, 128), 128)], d, sib))
        XK[p, pl.ds(pl.multiple_of(128 * c, 128), 128), :] = XW[c, p]

    for cp in w_cp:
        cp.wait_recv()
    WC[...] = mm(eye(256), WT[...], 1, 1).astype(bf16)
    mine = WC[pl.ds(pl.multiple_of(128 * c, 128), 128), :].astype(f32)
    colsum = mm(go_rows, mine, 1, 0, HIGHEST)[0:1]
    for n in range(8):
        ST[n, 2:3, 0:256] = colsum
    st_cp = [send(ST.at[(t + k) % 8], SR.at[t], d, (t + k) % 8) for k in range(1, 8)]
    SR[t] = ST[t]
    reduced_sum = Summed(QS, QR)
    for n, p in enumerate((*order, z)):
        x_cp[n].wait_recv()
        QF[...] = mm(XK[p], WC[...], 0, 0)
        part = QF[pl.ds(pl.multiple_of(64 * c, 64), 576), :]
        if n == 3:
            QO[...] = part
        else:
            QS[n] = part.astype(bf16)
            reduced_sum.start(n)
    for p in range(4):
        high, low = split(PLC[:, 1152 * p : 1152 * (p + 1)])
        PP[t, 288 * p : 288 * (p + 1), :] = (mm(POOL[...], high, 1, 1) + mm(POOL[...], low, 1, 1)).astype(bf16)
    placed_gather = Gather(PP, 1)
    placed_gather.start(far_mid)
    placed_gather.start(partner)
    placed_gather.own()


    for n in range(1, 4):
        wq_cp[n - 1].wait_recv()
        block = (z + 4 - n) % 4
        wb_cp += [send(WQ.at[block], WB.at[c, d, block], dpeer(k), t) for k in range(1, 4)]
        WB[c, d, block] = WQ[block]
    reduced_sum.add(0)
    placed_gather.forward(far_mid, 0)
    reduced_sum.add(1)
    for cp in wb_cp:
        cp.wait_recv()
    ws_cp = send(WB.at[c], WB.at[c], d, sib)
    ws_cp.wait_recv()
    for cc in range(2):
        for zz in range(4):
            for dd in range(4):
                WF[32 * (2 * zz + cc) : 32 * (2 * zz + cc + 1), 896 * dd : 896 * (dd + 1)] = WB[cc, dd, zz]
    lane = lax.broadcasted_iota(jnp.int32, (8, 128), 1)
    row = lax.broadcasted_iota(jnp.int32, (8, 128), 0)
    pick = jnp.where((lane >= 3 * row) & (lane < 3 * row + 3) & (row < 2), 1.0, 0.0).astype(bf16)
    gains = mm(pick, WF[:, 3328:3456], 1, 1)
    gm, gi = gains[0:1], gains[1:2]

    for cp in st_cp:
        cp.wait_recv()
    m_t = SR[:, 0, :]
    q_t = SR[:, 1, :]
    sums = SR[:, 2, 0:256]
    mean = jnp.mean(m_t, axis=0, keepdims=True)
    dm = m_t - mean
    var = (jnp.sum(q_t, axis=0, keepdims=True) + 128.0 * jnp.sum(dm * dm, axis=0, keepdims=True)) * (1.0 / 1024.0)
    rstd = lax.rsqrt(var + epsilon)
    valid = pl.ds(pl.multiple_of(64 * c, 64), 576)
    QF[...] = mm(dm, sums, 0, 0, HIGHEST)
    total = QO[...] + QF[valid, :]
    QF[...] = mm(jnp.broadcast_to(rstd, (8, 640)), jnp.full((8, 256), 0.125, f32), 0, 0, HIGHEST)
    scale = QF[valid, :]
    total = reduced_sum.result(total)
    RED[...] = jnp.zeros((24, 32, 256), f32)
    RED[:, 0:24, :] = (total * scale).reshape(24, 24, 256)

    xm, rm = norm_rows(RED[...].reshape(768, 256))
    zm = xm * gm
    hidden = zm * jax.nn.sigmoid(zm)
    XM[...], ZM[...], RM[...] = xm, zm, jnp.broadcast_to(rm, (768, 128))
    HB[0:32, :] = jnp.zeros((32, 768), bf16)
    HB[800:832, :] = jnp.zeros((32, 768), bf16)
    HB[32:800, 0:256] = pltpu.roll(hidden, 1, 0).astype(bf16)
    HB[32:800, 256:512] = hidden.astype(bf16)
    HB[32:800, 512:768] = pltpu.roll(hidden, 767, 0).astype(bf16)
    conv = mm(HB[0:768, :], WF[:, 0:768], 1, 1)
    conv += mm(HB[32:800, :], WF[:, 768:1536], 1, 1)
    conv += mm(HB[64:832, :], WF[:, 1536:2304], 1, 1)
    xi, ri = norm_rows(conv)
    zi = xi * gi
    activated = (zi * jax.nn.sigmoid(zi)).astype(bf16)
    XI[...], ZI[...], RI[...] = xi, zi, jnp.broadcast_to(ri, (768, 128))
    pool = pool_wide()
    ACT[t] = mm(pool, activated, 1, 0).astype(bf16)
    a_cp = [send(ACT.at[t], ACT.at[t], d, zpeer(k)) for k in range(1, 4)]
    as_cp = [send(ACT.at[t], ACT.at[t], d, sib)]

    placed_gather.forward(far_end, 0)
    for cp in operand_cp:
        cp.wait()
    MT[...] = mm(readout_weight[...], WF[:, 2304:3328], 1, 1).astype(bf16)
    for n, q in enumerate((z, partner, far_mid, far_end)):
        if n == 2:
            for k in range(1, 4):
                a_cp[k - 1].wait_recv()
                slot = 2 * ((z + 4 - k) % 4) + c
                as_cp.append(send(ACT.at[slot], ACT.at[slot], d, sib))
        placed_gather.ready(n)
        both = jnp.concatenate([PP[2 * q], PP[2 * q + 1]], axis=1)
        part = mm(readout_weight[:, pl.ds(pl.multiple_of(256 * q, 256), 256)], both, 1, 1)
        if n == 0:
            BEF[...] = part
        else:
            BEF[...] += part

    for cp in as_cp:
        cp.wait_recv()
    for n in range(8):
        ACL[n] = (ACT[n].astype(f32) * slot_live[n].astype(f32)).astype(bf16)
    act_live = ACL[...].reshape(1152, 256)
    BEF[...] += mm(MT[...], act_live, 1, 1)

    @pl.loop(0, 16)
    def _(u):
        rows = pl.ds(pl.multiple_of(32 * u, 32), 32)
        b = BEF[rows, :]
        bell = jnp.exp(-0.5 * b * b)
        density = bell * 0.3989422804014327
        u = 1.0 / (1.0 + 0.23164189 * jnp.abs(b))
        beyond = u * (0.127414796 + u * (-0.142248368 + u * (0.7107068705 + u * (-0.7265760135 + u * 0.5307027145)))) * bell
        below = jnp.where(b >= 0.0, 1.0 - beyond, beyond)
        RO[rows, :] = (b * below).astype(bf16)
        GBT[rows, :] = (cotangent[rows, :].astype(f32) * (below + b * density)).astype(bf16)

    store(RO, readout_o)
    GBR[...] = jnp.transpose(GBT[...])
    terms = mm(GBR[...], MT[...], 1, 0).astype(bf16).reshape(8, 144, 256)
    for n in range(8):
        AT[n % 2, n // 2] = terms[n]
    at_cp = send(AT.at[1 - c], AR, d, sib)
    pooled_sum = Summed(ES, ER)
    te_cp = []

    def pooled_block(n):
        te_cp[n].wait_recv()
        ES[n] = (TE[c, order[n]].astype(f32) + TR[order[n]].astype(f32)).astype(bf16)
        pooled_sum.start(n)

    for n, q in enumerate((*order, z)):
        block = mm(GBR[...], readout_weight[:, pl.ds(pl.multiple_of(256 * q, 256), 256)], 1, 0).astype(bf16)
        TE[0, q] = block[:, 0:128]
        TE[1, q] = block[:, 128:256]
        te_cp.append(send(TE.at[1 - c, q], TR.at[q], d, sib))
        if n == 0:
            at_cp.wait_recv()
            az_cp = []
            for k in (1, 2, 3):
                p = (z + k) % 4
                AS[k - 1] = (AT[c, p].astype(f32) + AR[p].astype(f32)).astype(bf16)
                az_cp.append(send(AS.at[k - 1], AZ.at[k - 1], d, zpeer(k)))
            grad_act = AT[c, z].astype(f32) + AR[z].astype(f32)
        else:
            pooled_block(n - 1)
    te_cp[3].wait_recv()
    GP[...] = TE[c, z].astype(f32) + TR[z].astype(f32)
    for q in range(4):
        both = jnp.concatenate([PP[2 * q], PP[2 * q + 1]], axis=1).astype(f32)
        POOLED[:, 256 * q : 256 * (q + 1)] = (both + mm(act_live, WF[:, 2304 + 256 * q : 2560 + 256 * q], 1, 0)).astype(bf16)
    for q in range(4):
        GR[q] = mm(GBT[128 * q : 128 * (q + 1), :], POOLED[...], 1, 0).astype(bf16)
    gr_cp = [send(GR.at[(d + k) % 4], GRR.at[d], dpeer(k), t) for k in range(1, 4)]
    GRR[d] = GR[d]

    for cp in az_cp:
        cp.wait_recv()
    for k in range(3):
        grad_act += AZ[k].astype(f32)
    pooled_sum.add(0)
    high, low = split(grad_act * slot_live[t].astype(f32))
    grad_rows = mm(pool, high, 0, 0) + mm(pool, low, 0, 0)
    zi = ZI[...]
    gate = jax.nn.sigmoid(zi)
    dy = grad_rows * (gate * (1.0 + zi * (1.0 - gate)))
    xi = XI[...]
    dyx_inner = dy * xi
    gc = norm_rows_back(dy * gi, xi, RI[:, 0:1]).astype(bf16)
    GB[0:32, :] = jnp.zeros((32, 256), bf16)
    GB[800:832, :] = jnp.zeros((32, 256), bf16)
    GB[32:800, :] = gc
    back = mm(GB[64:832, :], WF[:, 0:768], 1, 0)
    back += mm(GB[32:800, :], WF[:, 768:1536], 1, 0)
    back += mm(GB[0:768, :], WF[:, 1536:2304], 1, 0)
    grad_hidden = pltpu.roll(back[:, 0:256], 767, 0) + back[:, 256:512] + pltpu.roll(back[:, 512:768], 1, 0)
    zm = ZM[...]
    gate = jax.nn.sigmoid(zm)
    inside = (lax.broadcasted_iota(jnp.int32, (768, 256), 0) & 31) < 24
    dy = jnp.where(inside, grad_hidden * (gate * (1.0 + zm * (1.0 - gate))), 0.0)
    xm = XM[...]
    dyx_middle = dy * xm
    gr = norm_rows_back(dy * gm, xm, RM[:, 0:1]).reshape(24, 32, 256)[:, 0:24, :].reshape(576, 256).astype(bf16)
    GA[t] = gr
    grad_gather = Gather(GA, 2)
    grad_gather.start(far_mid)
    wg = jnp.sum(sums, axis=0, keepdims=True)
    grad_rounded = gr.astype(f32)
    s1 = jnp.sum(grad_rounded * wg, axis=1, keepdims=True)
    s2 = jnp.sum(grad_rounded * RED[:, 0:24, :].reshape(576, 256), axis=1, keepdims=True)
    lane = lax.broadcasted_iota(jnp.int32, (576, 128), 1)
    RSC[0:64, :] = jnp.zeros((64, 128), f32)
    RSC[576:640, :] = jnp.zeros((64, 128), f32)
    RSC[valid, :] = jnp.where(lane == 0, s1, s2) * (1.0 / 1024.0)
    row_sums = jnp.transpose(RSC[...])
    RS[t, 0:1, :] = mean
    RS[t, 1:2, :] = rstd
    RS[t, 2:4, :] = row_sums[0:2]
    rs_cp = [send(RS.at[t], RS.at[t], d, (t + k) % 8) for k in range(1, 8)]
    grad_gather.start(partner)
    grad_gather.own()
    pooled_sum.add(1)

    def put(lo, value):
        value = value.astype(bf16)
        for n in range(8):
            CG[n % 2, n // 2, :, lo : lo + value.shape[1]] = value[32 * n : 32 * (n + 1)]

    for a in range(3):
        put(768 * a, mm(gc, HB[32 * a : 32 * a + 768, :], 0, 0))
    ones = jnp.ones((768, 128), bf16)
    for lo, value in ((2304, dyx_inner), (2432, dyx_middle)):
        high, low = split(value)
        put(lo, mm(high, ones, 0, 0) + mm(low, ones, 0, 0))
    cg_cp = send(CG.at[1 - c], CGR, d, sib)

    for cp in gr_cp:
        cp.wait_recv()
    total = GRR[0].astype(f32)
    for n in range(1, 4):
        total += GRR[n].astype(f32)
    GRF[d] = total.astype(bf16)

    cg_cp.wait_recv()
    CGS[...] = (CG[c].astype(f32) + CGR[...].astype(f32)).astype(bf16)
    cgd_cp = []
    for k in range(1, 4):
        dd = dpeer(k)
        cgd_cp.append(send(CGS.at[:, :, pl.ds(pl.multiple_of(640 * dd, 128), 640)], CGD.at[d], dd, t))
    CGD[d] = CGS[:, :, pl.ds(pl.multiple_of(640 * d, 128), 640)]
    grf_cp = [send(GRF.at[d], GRF.at[d], dpeer(k), t) for k in range(1, 4)]

    for h in range(2):
        grad_gather.forward(far_mid, h)
    def turn(n):
        for k in range(1, 8):
            s = (t + k) % 8
            yield send(FT.at[n, pl.ds(pl.multiple_of(32 * s, 32), 32)], TA.at[n, d, t], d, s)
        TA[n, d, t] = FT[n, pl.ds(pl.multiple_of(32 * t, 32), 32), :]

    for cp in rs_cp:
        cp.wait_recv()
    w_own = WC[pl.ds(pl.multiple_of(128 * c, 128), 128), :]
    lane = lax.broadcasted_iota(jnp.int32, (4, 128), 1)
    gain_sum = jnp.zeros((128, 1), f32)
    grad_reduce = jnp.zeros((128, 256), f32)
    for n, p in enumerate((z, partner, far_mid, far_end)):
        if n >= 2:
            grad_gather.forward(far_end, n - 2)
        if n == 3:
            gp = pooled_sum.result(GP[...])
            gp_high, gp_low = split(gp)
            FT[0] = mm(act_live, gp_high, 0, 0).astype(bf16)
            turn_cp = list(turn(0))
            for m in range(4):
                cells = slice(288 * m, 288 * (m + 1))
                SP[:, 1152 * m : 1152 * (m + 1)] = mm(gp_high[cells], POOL[...], 0, 0) + mm(gp_low[cells], POOL[...], 0, 0)
            for cp in cgd_cp:
                cp.wait_recv()
            total = CGD[0].astype(f32)
            for m in range(1, 4):
                total += CGD[m].astype(f32)
            CGT[...] = total.astype(bf16)
            cgz_cp = [send(CGT.at[(z + k) % 4], CGZ.at[z], d, zpeer(k)) for k in range(1, 4)]
            CGZ[z] = CGT[z]
        grad_gather.ready(n)
        cols = pl.ds(pl.multiple_of(1152 * p, 128), 1152)
        even, odd = RS[2 * p], RS[2 * p + 1]
        stats = jnp.concatenate([even[:, 0:512], jnp.where(lane < 64, even[:, 512:640], odd[:, 0:128]), odd[:, 128:640]], axis=1)
        g = GA[pl.ds(2 * p, 2)].reshape(1152, 256)
        xhat = (PLC[:, cols] - stats[0:1]) * stats[1:2]
        grad_reduce += mm((xhat * go).astype(bf16), g, 1, 0)
        if n == 3:
            FT[1] = jnp.transpose(grad_reduce).astype(bf16)
            turn_cp += list(turn(1))
        gn = mm(w_own, g, 1, 1)
        gain_sum += jnp.sum(gn * xhat, axis=1, keepdims=True)
        GF[:, cols] = stats[1:2] * (gn * go - stats[2:3] - xhat * stats[3:4])
    for cp in turn_cp[0:7]:
        cp.wait_recv()
    ta_cp = [send(TA.at[0, d], TA.at[0, d], dpeer(k), t) for k in range(1, 4)]
    place_sum = jnp.zeros((128, 1152), f32)
    for p in range(4):
        cols = slice(1152 * p, 1152 * (p + 1))
        out = GF[:, cols] + SP[:, cols]
        GF[:, cols] = out
        store(GF.at[:, cols], gfeat_o.at[:, cols])
        place_sum += out
    odd = pltpu.roll(place_sum, 576, 1)
    lane = lax.broadcasted_iota(jnp.int32, (128, 640), 1)
    place = jnp.where(lane < 576, place_sum[:, 0:640] + odd[:, 0:640], jnp.broadcast_to(gain_sum, (128, 640))).astype(bf16)
    for q in range(4):
        PM[q] = place[32 * q : 32 * (q + 1)]
    pm_cp = [send(PM.at[dpeer(k)], PR.at[d], dpeer(k), t) for k in range(1, 4)]
    PR[d] = PM[d]

    for cp in turn_cp[7:14]:
        cp.wait_recv()
    ta_cp += [send(TA.at[1, d], TA.at[1, d], dpeer(k), t) for k in range(1, 4)]
    for cp in pm_cp:
        cp.wait_recv()
    total = PR[0].astype(f32)
    for n in range(1, 4):
        total += PR[n].astype(f32)
    PF[d] = total.astype(bf16)
    pf_cp = [send(PF.at[d], PF.at[d], dpeer(k), t) for k in range(1, 4)]
    for cp in cgz_cp:
        cp.wait_recv()
    total = CGZ[0].astype(f32)
    for m in range(1, 4):
        total += CGZ[m].astype(f32)
    CGF[d] = total.astype(bf16)
    cgf_cp = [send(CGF.at[d], CGF.at[d], dpeer(k), t) for k in range(1, 4)]
    for cp in grf_cp:
        cp.wait_recv()
    for q in range(4):
        store(GRF.at[q], gread_o.at[pl.ds(128 * q, 128)])
    for cp in cgf_cp:
        cp.wait_recv()
    for q in range(4):
        gconv_o[:, 640 * q : 640 * (q + 1)] = CGF[q]
    for cp in ta_cp:
        cp.wait_recv()
    for n, out in enumerate((gexp_o, gred_o)):
        for s in range(8):
            total = TA[n, 0, s].astype(f32)
            for m in range(1, 4):
                total += TA[n, m, s].astype(f32)
            out[:, 128 * s : 128 * (s + 1)] = total
    for cp in pf_cp:
        cp.wait_recv()
    gpos_o[...] = jnp.transpose(PF[...].reshape(128, 640).astype(f32))
    for cp in result_cp:
        cp.wait()
    for cp in pending:
        cp.wait_send()
    placed_gather.drain()
    grad_gather.drain()


SCRATCH = (
    ("readout_weight", (512, 1024), bf16), ("cotangent", (512, 1152), bf16), ("RO", (512, 1152), bf16), ("GF", (128, 4608), f32), ("SP", (128, 4608), f32), ("WT", (256, 256), bf16), ("WC", (256, 256), bf16), ("CB", (32, 3584), bf16),
    ("WQ", (4, 32, 896), bf16), ("WB", (2, 4, 4, 32, 896), bf16), ("WF", (256, 3584), bf16), ("MT", (512, 256), bf16),
    ("POOL", (288, 1152), bf16), ("PLC", (128, 4608), f32), ("XW", (2, 4, 128, 640), bf16), ("XK", (4, 256, 640), bf16),
    ("ST", (8, 4, 640), f32), ("SR", (8, 4, 640), f32), ("QF", (640, 256), f32), ("QS", (3, 576, 256), bf16),
    ("QO", (576, 256), f32), ("QR", (4, 576, 256), bf16), ("RED", (24, 32, 256), f32), ("HB", (832, 768), bf16),
    ("GB", (832, 256), bf16), ("XM", (768, 256), f32), ("ZM", (768, 256), f32), ("RM", (768, 128), f32),
    ("XI", (768, 256), f32), ("ZI", (768, 256), f32), ("RI", (768, 128), f32), ("ACT", (8, 144, 256), bf16), ("ACL", (8, 144, 256), bf16),
    ("PP", (8, 1152, 128), bf16), ("POOLED", (1152, 1024), bf16), ("BEF", (512, 1152), f32), ("GBT", (512, 1152), bf16), ("GBR", (1152, 512), bf16),
    ("TE", (2, 4, 1152, 128), bf16), ("TR", (4, 1152, 128), bf16), ("ES", (3, 1152, 128), bf16), ("ER", (4, 1152, 128), bf16),
    ("GP", (1152, 128), f32), ("AT", (2, 4, 144, 256), bf16), ("AR", (4, 144, 256), bf16), ("AS", (3, 144, 256), bf16),
    ("AZ", (3, 144, 256), bf16), ("RSC", (640, 128), f32), ("GA", (8, 576, 256), bf16), ("RS", (8, 4, 640), f32),
    ("FT", (2, 256, 128), bf16), ("TA", (2, 4, 8, 32, 128), bf16), ("PM", (4, 32, 640), bf16),
    ("PR", (4, 32, 640), bf16), ("PF", (4, 32, 640), bf16),
    ("CG", (2, 4, 32, 2560), bf16), ("CGR", (4, 32, 2560), bf16), ("CGS", (4, 32, 2560), bf16), ("CGD", (4, 4, 32, 640), bf16),
    ("CGT", (4, 32, 640), bf16), ("CGZ", (4, 32, 640), bf16), ("CGF", (4, 32, 640), bf16), ("GR", (4, 128, 1024), bf16), ("GRR", (4, 128, 1024), bf16),
    ("GRF", (4, 128, 1024), bf16),
)


def finish(
    readout, gfeat, gpos, gexp, gred, gconv, gread, readout_o, gfeat_o, gpos_o, ggo_o, gred_o, ggm_o, gconv_o, ggi_o, gexp_o, gread_o,
    RO, GF, GB, GC, GR, GP, GQ, GE, GD, sem,
):
    copies = []

    def copy(src, dst):
        cp = pltpu.make_async_copy(src, dst, sem.at[len(copies)])
        copies.append(cp)
        cp.start()
        return cp

    loads = [copy(gread.at[pl.ds(256 * p, 256)], GB.at[pl.ds(256 * p, 256)]) for p in range(2)]
    loads += [copy(gfeat.at[pl.ds(32 * p, 32)], GF.at[pl.ds(32 * p, 32)]) for p in range(4)]
    loads += [copy(readout, RO), copy(gconv, GC), copy(gpos, GP), copy(gexp, GE), copy(gred, GD)]
    stores = []
    for p in range(2):
        rows = pl.ds(256 * p, 256)
        loads[p].wait()
        GR[rows, :] = GB[rows, :].astype(f32)
        stores.append(copy(GR.at[rows], gread_o.at[rows]))
    for p in range(4):
        rows = pl.ds(32 * p, 32)
        loads[2 + p].wait()
        stores.append(copy(GF.at[rows], gfeat_o.at[rows]))
    loads[6].wait()
    stores.append(copy(RO, readout_o))
    loads[7].wait()
    for n in range(9):
        GQ[n] = GC[:, 256 * n : 256 * (n + 1)].astype(f32)
    stores.append(copy(GQ, gconv_o))
    first = (lax.broadcasted_iota(jnp.int32, (8, 128), 1) == 0).astype(f32).astype(bf16)
    ggi_o[...] = mm(first, GC[:, 2304:2432], 1, 1)[0:1]
    ggm_o[...] = mm(first, GC[:, 2432:2560], 1, 1)[0:1]
    loads[8].wait()
    stores.append(copy(GP.at[pl.ds(0, 576)], gpos_o))
    ggo_o[...] = GP[576:577, :]
    loads[9].wait()
    stores.append(copy(GE, gexp_o))
    loads[10].wait()
    stores.append(copy(GD, gred_o))
    for cp in stores:
        cp.wait()


def local_by_image(features, slot_live, position, gain_outer, reduce_weight, gain_middle, conv_weight, gain_inner, expand_weight, readout_weight, cotangent):
    vmem = pl.BlockSpec(memory_space=pltpu.VMEM)
    smem = pl.BlockSpec(memory_space=pltpu.SMEM)
    hbm = pl.BlockSpec(memory_space=pl.ANY)

    def shapes(*pairs):
        return tuple(jax.ShapeDtypeStruct(shape, dtype) for shape, dtype in pairs)

    parts = pl.pallas_call(
        kernel,
        out_shape=shapes(
            ((512, 1152), bf16), ((128, 4608), f32), ((640, 128), f32), ((32, 1024), f32), ((32, 1024), f32), ((32, 2560), bf16), ((512, 1024), bf16)
        ),
        in_specs=[vmem, smem] + [vmem] * 7 + [hbm] * 2,
        out_specs=[hbm, hbm, vmem, vmem, vmem, vmem, hbm],
        scratch_shapes=[pltpu.VMEM(shape, dtype) for _, shape, dtype in SCRATCH]
        + [pltpu.SemaphoreType.DMA((COPIES,)), pltpu.SemaphoreType.DMA((COPIES,)), pltpu.SemaphoreType.DMA((16,))],
        compiler_params=pltpu.CompilerParams(collective_id=0, has_side_effects=True, vmem_limit_bytes=60 * 2**20),
    )(
        features, slot_live, position.reshape(576, 128), gain_outer.reshape(1, 128), reduce_weight.T, gain_middle.reshape(1, 32),
        conv_weight.transpose(0, 1, 3, 2).reshape(9, 32, 256), gain_inner.reshape(1, 32), expand_weight, readout_weight, cotangent,
    )
    readout, gfeat, gpos, ggo, gred, ggm, gconv, ggi, gexp, gread = pl.pallas_call(
        finish,
        out_shape=shapes(
            ((512, 1152), bf16), ((128, 4608), f32), ((576, 128), f32), ((1, 128), f32), ((32, 1024), f32), ((1, 32), f32),
            ((9, 32, 256), f32), ((1, 32), f32), ((32, 1024), f32), ((512, 1024), f32),
        ),
        in_specs=[hbm] * 7,
        out_specs=[hbm, hbm, hbm, vmem, hbm, vmem, hbm, vmem, hbm, hbm],
        scratch_shapes=[
            pltpu.VMEM((512, 1152), bf16), pltpu.VMEM((128, 4608), f32), pltpu.VMEM((512, 1024), bf16), pltpu.VMEM((32, 2560), bf16),
            pltpu.VMEM((512, 1024), f32), pltpu.VMEM((640, 128), f32), pltpu.VMEM((9, 32, 256), f32), pltpu.VMEM((32, 1024), f32),
            pltpu.VMEM((32, 1024), f32), pltpu.SemaphoreType.DMA((24,)),
        ],
        compiler_params=pltpu.CompilerParams(vmem_limit_bytes=60 * 2**20),
    )(*parts)
    return (
        readout, gfeat, gpos.reshape(24, 24, 128), ggo.reshape(128), gred.T, ggm.reshape(32),
        gconv.reshape(3, 3, 32, 256).transpose(0, 1, 3, 2), ggi.reshape(32), gexp, gread,
    )


def row_totals(leading, trailing):
    return lax.psum((leading, trailing), "tensor")


def norm_forward(values, norm_gain, breadth):
    totals, squares = row_totals(jnp.sum(values, axis=1), jnp.sum(values * values, axis=1))
    center = totals / breadth
    spread = squares / breadth - center * center
    scaled = lax.rsqrt(spread + epsilon)[:, None]
    normed = (values - center[:, None]) * scaled
    return (normed, scaled, normed * norm_gain)


def norm_backward(grad_out, normed, scaled, norm_gain, breadth):
    grad_normed = grad_out * norm_gain
    gain_grad = jnp.sum(grad_out * normed, axis=0)
    leading, trailing = row_totals(
        jnp.sum(grad_normed, axis=1), jnp.sum(grad_normed * normed, axis=1)
    )
    grad_in = scaled * (
        grad_normed - leading[:, None] / breadth - normed * (trailing[:, None] / breadth)
    )
    return (grad_in, gain_grad)


def silu_grad(inputs):
    gate_value = jax.nn.sigmoid(inputs)
    return gate_value * (1.0 + inputs * (1.0 - gate_value))


def gelu_grad(inputs):
    below = 0.5 * (1.0 + lax.erf(inputs * 0.7071067811865476))
    density = jnp.exp(-0.5 * inputs * inputs) * 0.3989422804014327
    return below + inputs * density


def contract_rows(left_side, right_side):
    return lax.dot_general(
        left_side, right_side, (((0,), (0,)), ((), ())), preferred_element_type=jnp.float32
    )


def window_of(padded, shift_down, shift_across, grid_side):
    images = padded.shape[0]
    breadth = padded.shape[3]
    return padded[
        :, shift_down : shift_down + grid_side, shift_across : shift_across + grid_side, :
    ].reshape(images * grid_side * grid_side, breadth)


def local_by_hidden(
    features,
    slot_live,
    position,
    gain_outer,
    reduce_weight,
    gain_middle,
    conv_weight,
    gain_inner,
    expand_weight,
    readout_weight,
    cotangent,
):
    grid_side = position.shape[0]
    half_side = grid_side // 2
    channel_share = features.shape[0]
    row_count = features.shape[1]
    images = row_count // (grid_side * grid_side)
    tensor_size = lax.axis_size("tensor")
    channels = channel_share * tensor_size
    hidden_share = reduce_weight.shape[1]
    hidden_width = hidden_share * tensor_size
    pooled_count = images * half_side * half_side
    placed = (
        features.T.astype(jnp.float32).reshape(images, grid_side * grid_side, channel_share)
        + position.reshape(1, grid_side * grid_side, channel_share)
    ).reshape(row_count, channel_share)
    live_rows = jnp.repeat(slot_live.astype(jnp.float32), grid_side * grid_side)[:, None]
    normed_outer, scaled_outer, shaped_outer = norm_forward(placed, gain_outer, channels)
    reduce_in = shaped_outer.astype(jnp.bfloat16)
    reduce_full = lax.all_gather(reduce_in, "tensor", axis=1, tiled=True)
    reduced = jnp.dot(reduce_full, reduce_weight, preferred_element_type=jnp.float32)
    normed_middle, scaled_middle, shaped_middle = norm_forward(reduced, gain_middle, hidden_width)
    hidden = jax.nn.silu(shaped_middle).astype(jnp.bfloat16)
    hidden_full = lax.all_gather(hidden, "tensor", axis=1, tiled=True)
    padded_hidden = jnp.pad(
        hidden_full.reshape(images, grid_side, grid_side, hidden_width),
        ((0, 0), (1, 1), (1, 1), (0, 0)),
    )
    convolved = jnp.zeros((row_count, hidden_share), jnp.float32)
    for offset_tap in range(9):
        shift_down = offset_tap // 3
        shift_across = offset_tap % 3
        convolved = convolved + jnp.dot(
            window_of(padded_hidden, shift_down, shift_across, grid_side),
            conv_weight[shift_down, shift_across],
            preferred_element_type=jnp.float32,
        )
    normed_inner, scaled_inner, shaped_inner = norm_forward(convolved, gain_inner, hidden_width)
    activated = jax.nn.silu(shaped_inner).astype(jnp.bfloat16)
    expand_terms = jnp.dot(activated, expand_weight, preferred_element_type=jnp.float32)
    expanded = lax.psum_scatter(expand_terms, "tensor", scatter_dimension=1, tiled=True)
    mixed = placed + live_rows * expanded
    pooled = jnp.mean(mixed.reshape(images, half_side, 2, half_side, 2, channel_share), axis=(2, 4))
    pooled_low = pooled.reshape(pooled_count, channel_share).astype(jnp.bfloat16)
    pooled_full = lax.all_gather(pooled_low, "tensor", axis=1, tiled=True)
    before = lax.dot_general(
        pooled_full, readout_weight, (((1,), (1,)), ((), ())), preferred_element_type=jnp.float32
    )
    readout = jax.nn.gelu(before, approximate=False).astype(jnp.bfloat16).T
    grad_before = (cotangent.T.astype(jnp.float32) * gelu_grad(before)).astype(jnp.bfloat16)
    grad_readout = contract_rows(grad_before, pooled_full)
    pooled_terms = jnp.dot(grad_before, readout_weight, preferred_element_type=jnp.float32)
    grad_pooled = lax.psum_scatter(pooled_terms, "tensor", scatter_dimension=1, tiled=True)
    spread_grad = jnp.broadcast_to(
        (0.25 * grad_pooled).reshape(images, half_side, 1, half_side, 1, channel_share),
        (images, half_side, 2, half_side, 2, channel_share),
    )
    grad_mixed = spread_grad.reshape(row_count, channel_share)
    grad_branch = (live_rows * grad_mixed).astype(jnp.bfloat16)
    grad_full = lax.all_gather(grad_branch, "tensor", axis=1, tiled=True)
    grad_expand = contract_rows(activated, grad_full)
    grad_activated = jnp.dot(grad_full, expand_weight.T, preferred_element_type=jnp.float32)
    grad_convolved, grad_gain_inner = norm_backward(
        grad_activated * silu_grad(shaped_inner),
        normed_inner,
        scaled_inner,
        gain_inner,
        hidden_width,
    )
    grad_conv_low = grad_convolved.astype(jnp.bfloat16)
    tap_grads = []
    grad_padded = jnp.zeros((images, grid_side + 2, grid_side + 2, hidden_width), jnp.float32)
    for offset_tap in range(9):
        shift_down = offset_tap // 3
        shift_across = offset_tap % 3
        tap_grads.append(
            contract_rows(
                window_of(padded_hidden, shift_down, shift_across, grid_side), grad_conv_low
            )
        )
        tap_back = jnp.dot(
            grad_conv_low,
            conv_weight[shift_down, shift_across].T,
            preferred_element_type=jnp.float32,
        )
        grad_padded = grad_padded + jnp.pad(
            tap_back.reshape(images, grid_side, grid_side, hidden_width),
            ((0, 0), (shift_down, 2 - shift_down), (shift_across, 2 - shift_across), (0, 0)),
        )
    grad_conv = jnp.stack(tap_grads, axis=0).reshape(conv_weight.shape)
    grad_window = grad_padded[:, 1 : grid_side + 1, 1 : grid_side + 1, :].reshape(
        row_count, hidden_width
    )
    grad_hidden = lax.psum_scatter(grad_window, "tensor", scatter_dimension=1, tiled=True)
    grad_reduced, grad_gain_middle = norm_backward(
        grad_hidden * silu_grad(shaped_middle),
        normed_middle,
        scaled_middle,
        gain_middle,
        hidden_width,
    )
    grad_reduced_low = grad_reduced.astype(jnp.bfloat16)
    grad_reduce = contract_rows(reduce_full, grad_reduced_low)
    outer_terms = jnp.dot(grad_reduced_low, reduce_weight.T, preferred_element_type=jnp.float32)
    grad_shaped_outer = lax.psum_scatter(outer_terms, "tensor", scatter_dimension=1, tiled=True)
    grad_inputs, grad_gain_outer = norm_backward(
        grad_shaped_outer, normed_outer, scaled_outer, gain_outer, channels
    )
    grad_rows = grad_mixed + grad_inputs
    grad_place = jnp.sum(grad_rows.reshape(images, grid_side, grid_side, channel_share), axis=0)
    grad_total = grad_rows.T
    summed = (
        lax.psum(grad_place.astype(jnp.bfloat16), "dp").astype(jnp.float32),
        lax.psum(grad_gain_outer.astype(jnp.bfloat16), "dp").astype(jnp.float32),
        lax.psum(grad_reduce.astype(jnp.bfloat16), "dp").astype(jnp.float32),
        lax.psum(grad_gain_middle.astype(jnp.bfloat16), "dp").astype(jnp.float32),
        lax.psum(grad_conv.astype(jnp.bfloat16), "dp").astype(jnp.float32),
        lax.psum(grad_gain_inner.astype(jnp.bfloat16), "dp").astype(jnp.float32),
        lax.psum(grad_expand.astype(jnp.bfloat16), "dp").astype(jnp.float32),
        lax.psum(grad_readout.astype(jnp.bfloat16), "dp").astype(jnp.float32),
    )
    return (
        readout,
        grad_total,
        summed[0],
        summed[1],
        summed[2],
        summed[3],
        summed[4],
        summed[5],
        summed[6],
        summed[7],
    )


def solution(mesh):
    parts, groups = mesh.shape["tensor"], mesh.shape["dp"]
    specs = (P("tensor", "dp"), P("dp"), P(None, None, "tensor"), P("tensor"), P(None, "tensor"), P("tensor"), P(None, None, None, "tensor"), P("tensor"), P("tensor", None), P("tensor", None), P("tensor", "dp"))

    def whole(*arrays):
        by_image = (parts, groups) == (8, 4) and arrays[1].shape[0] == parts * groups
        return jax.shard_map(
            local_by_image if by_image else local_by_hidden, mesh=mesh, in_specs=specs,
            out_specs=(P("tensor", "dp"), P("tensor", "dp"), *specs[2:10]), check_vma=False,
        )(*arrays)

    return whole
```

```python
import jax
import jax.numpy as jnp
from jax import lax
from jax.experimental import pallas as pl
from jax.experimental.pallas import tpu as pltpu
from jax.sharding import PartitionSpec as P

epsilon = 1e-05
bf16 = jnp.bfloat16
f32 = jnp.float32
COPIES = 160

MESH = pl.DeviceIdType.MESH
HIGHEST = lax.Precision.HIGHEST


def mm(a, b, ca, cb, precision=None):
    return lax.dot_general(a, b, (((ca,), (cb,)), ((), ())), precision=precision, preferred_element_type=f32)


def split(x):
    high = x.astype(bf16)
    return high, (x - high.astype(f32)).astype(bf16)


def eye(n, dtype=bf16):
    return (lax.broadcasted_iota(jnp.int32, (n, n), 0) == lax.broadcasted_iota(jnp.int32, (n, n), 1)).astype(f32).astype(dtype)


def pool_wide():
    spot = lax.broadcasted_iota(jnp.int32, (144, 768), 1)
    cell = lax.broadcasted_iota(jnp.int32, (144, 768), 0)
    i, j = spot >> 5, spot & 31
    return jnp.where(((i >> 1) * 12 + (j >> 1) == cell) & (j < 24), 0.25, 0.0).astype(bf16)


def pool_pair():
    spot = lax.broadcasted_iota(jnp.int32, (288, 1152), 1)
    cell = lax.broadcasted_iota(jnp.int32, (288, 1152), 0)
    i = (spot * 2731) >> 16
    j = spot - i * 24
    return jnp.where((i >> 1) * 12 + (j >> 1) == cell, 0.25, 0.0).astype(bf16)


def norm_rows(v):
    s = v - jnp.mean(v, axis=1, keepdims=True)
    r = lax.rsqrt(jnp.mean(s * s, axis=1, keepdims=True) + epsilon)
    return s * r, r


def norm_rows_back(dx, xhat, r):
    return r * (dx - jnp.mean(dx, axis=1, keepdims=True) - xhat * jnp.mean(dx * xhat, axis=1, keepdims=True))


def kernel(
    features_h, slot_live, position_h, gain_outer, reduce_weight, gain_middle, conv_h, gain_inner, expand_h, readout_h, cotangent_h,
    readout_o, gfeat_o, gpos_o, gexp_o, gred_o, gconv_o, gread_o,
    features, position, conv_weight, expand_weight, readout_weight, cotangent, RO, GF, SP, WT, WC, CB, WQ, WB, WF, MT, POOL, PLC, XW, XK, ST, SR, QF, QS, QO, QR, RED, HB, GB,
    XM, ZM, RM, XI, ZI, RI, ACT, ACL, PP, POOLED, BEF, GBT, GBR, TE, TR, ES, ER, GP, AT, AR, AS, AZ,
    RSC, GA, RS, FT, TA, PM, PR, PF, CG, CGR, CGS, CGD, CGT, CGZ, CGF, GR, GRR, GRF, ssem, rsem, lsem,
):
    d = lax.axis_index("dp")
    t = lax.axis_index("tensor")
    z = t // 2
    c = t % 2
    sib = 2 * z + 1 - c
    side = z // 2
    is_mid = ((z + 1) // 2) % 2
    near_end, near_mid, far_end, far_mid = 3 * side, 1 + side, 3 - 3 * side, 2 - side
    partner = z + 1 - 2 * (z % 2)
    sends, arrivals = [0], [0]
    pending = []

    def copy(src, dst, dd, tt, arrival):
        cp = pltpu.make_async_remote_copy(
            src_ref=src, dst_ref=dst, send_sem=ssem.at[sends[0]], recv_sem=rsem.at[arrival], device_id=(dd, tt), device_id_type=MESH
        )
        sends[0] += 1
        return cp

    def take(n):
        arrivals[0] += n
        return arrivals[0] - n

    def send(src, dst, dd, tt):
        cp = copy(src, dst, dd, tt, take(1))
        cp.start()
        pending.append(cp)
        return cp

    class Gather:
        def __init__(self, buf, parts):
            self.buf, self.parts, self.rows = buf, parts, buf.shape[1] // parts
            self.base = take(4 * parts)
            self.forwards = []

        def view(self, zz, h):
            return self.buf.at[2 * zz + c, pl.ds(h * self.rows, self.rows)]

        def to(self, block, zz, h):
            return copy(self.view(block, h), self.view(block, h), d, 2 * zz + c, self.base + 4 * h + block)

        def start(self, zz):
            for h in range(self.parts):
                cp = self.to(z, zz, h)
                cp.start()
                pending.append(cp)

        def own(self):
            self.siblings = [send(self.buf.at[t], self.buf.at[t], d, sib)]

        def arrived(self, block, h):
            view = self.view(block, h)
            pltpu.make_async_remote_copy(
                src_ref=view, dst_ref=view, send_sem=ssem.at[0], recv_sem=rsem.at[self.base + 4 * h + block],
                device_id=(d, sib), device_id_type=MESH,
            ).wait_recv()

        def forward(self, block, h):
            cp = self.to(block, near_end, h)
            self.forwards.append(cp)

            @pl.when(is_mid == 1)
            def _():
                self.arrived(block, h)
                cp.start()

        def pass_on(self, n):
            for h in range(self.parts):
                if n == 3:
                    self.arrived(blocks[n], h)
                else:

                    @pl.when(is_mid == 0)
                    def _(h=h):
                        self.arrived(blocks[n], h)

            slot = self.buf.at[2 * blocks[n] + c]
            self.siblings.append(send(slot, slot, d, sib))

        def ready(self, n):
            self.siblings[n].wait_recv()

        def drain(self):
            @pl.when(is_mid == 1)
            def _():
                for cp in self.forwards:
                    cp.wait_send()

    order = (
        far_end + is_mid * (near_end - far_end),
        far_mid + is_mid * (far_end - far_mid),
        near_mid + is_mid * (far_mid - near_mid),
    )

    blocks = (z, partner + is_mid * (far_mid - partner), far_mid + is_mid * (far_end - far_mid), far_end + is_mid * (partner - far_end))

    class Summed:
        def __init__(self, out, arrive):
            self.out, self.arrive = out, arrive
            self.base = take(4)
            to = (partner, near_mid + is_mid * (far_end - near_mid), near_mid + is_mid * (far_mid - near_mid))
            slot = (2 * is_mid, 1 + 2 * is_mid, 2 + is_mid)
            self.cps = [copy(out.at[n], arrive.at[slot[n]], d, 2 * to[n] + c, self.base + slot[n]) for n in range(3)]
            pending.extend(self.cps)

        def wait(self, n):
            view = self.arrive.at[n]
            pltpu.make_async_remote_copy(
                src_ref=view, dst_ref=view, send_sem=ssem.at[0], recv_sem=rsem.at[self.base + n], device_id=(d, sib), device_id_type=MESH
            ).wait_recv()

        def start(self, n):
            if n == 0:
                self.cps[0].start()
            else:

                @pl.when(is_mid == 0)
                def _():
                    self.cps[n].start()

        def add(self, n):
            @pl.when(is_mid == 1)
            def _():
                self.wait(n)
                self.out[n + 1] = (self.out[n + 1].astype(f32) + self.arrive[n].astype(f32)).astype(bf16)
                self.cps[n + 1].start()

        def result(self, own):
            self.wait(2)
            self.wait(3)
            return own + self.arrive[2].astype(f32) + self.arrive[3].astype(f32)

    def zpeer(k):
        return 2 * ((z + k) % 4) + c

    def dpeer(k):
        return (d + k) % 4

    def load(n, src, dst):
        cp = pltpu.make_async_copy(src, dst, lsem.at[n])
        cp.start()
        return cp

    result_cp = []

    def store(src, dst):
        cp = pltpu.make_async_copy(src, dst, lsem.at[9 + len(result_cp)])
        cp.start()
        result_cp.append(cp)

    barrier = pltpu.get_barrier_semaphore()
    for k in range(1, 8):
        pl.semaphore_signal(barrier, 1, device_id=(d, (t + k) % 8), device_id_type=MESH)
    for k in range(1, 4):
        pl.semaphore_signal(barrier, 1, device_id=(dpeer(k), t), device_id_type=MESH)

    position_cp = load(0, position_h, position)
    feature_cp = []
    for n, p in enumerate((*order, z)):
        cols = pl.ds(pl.multiple_of(1152 * p, 128), 1152)
        feature_cp.append(load(1 + n, features_h.at[:, cols], features.at[:, cols]))
    weight_cp = [load(5, conv_h, conv_weight), load(6, expand_h, expand_weight)]
    operand_cp = [load(7, readout_h, readout_weight), load(8, cotangent_h, cotangent)]
    POOL[...] = pool_pair()
    pl.semaphore_wait(barrier, 10)

    w_cp = []
    for k in range(1, 8):
        s = (t + k) % 8
        w_cp.append(send(reduce_weight.at[:, pl.ds(pl.multiple_of(256 * (s // 2), 256), 256)], WT.at[pl.ds(pl.multiple_of(32 * t, 32), 32)], d, s))
    WT[pl.ds(pl.multiple_of(32 * t, 32), 32), :] = reduce_weight[:, pl.ds(pl.multiple_of(256 * z, 256), 256)]
    position_cp.wait()
    go_rows = jnp.broadcast_to(gain_outer[...], (8, 128))
    eighth = jnp.full((8, 128), 0.125, f32)
    go = mm(go_rows, eighth, 0, 0, HIGHEST)[:, 0:1]
    pos = position[...]
    pos_pair = mm(eye(128, f32), jnp.concatenate([pos, pos], axis=0), 1, 1, HIGHEST)
    x_cp = []
    for n, p in enumerate((*order, z)):
        cols = pl.ds(pl.multiple_of(1152 * p, 128), 1152)
        feature_cp[n].wait()
        x = features[:, cols].astype(f32) + pos_pair
        PLC[:, cols] = x
        m = jnp.mean(x, axis=0, keepdims=True)
        x = x - m
        q = jnp.sum(x * x, axis=0, keepdims=True)
        x = (x * go).astype(bf16)
        for par, lo in ((0, 0), (1, 512)):
            XW[par, p] = x[:, lo : lo + 640]
            ST[2 * p + par, 0:1, :] = m[:, lo : lo + 640]
            ST[2 * p + par, 1:2, :] = q[:, lo : lo + 640]
        x_cp.append(send(XW.at[1 - c, p], XK.at[p, pl.ds(pl.multiple_of(128 * c, 128), 128)], d, sib))
        XK[p, pl.ds(pl.multiple_of(128 * c, 128), 128), :] = XW[c, p]

    for p in range(4):
        high, low = split(PLC[:, 1152 * p : 1152 * (p + 1)])
        PP[t, 288 * p : 288 * (p + 1), :] = (mm(POOL[...], high, 1, 1) + mm(POOL[...], low, 1, 1)).astype(bf16)
    placed_gather = Gather(PP, 1)
    placed_gather.start(far_mid)
    for cp in weight_cp:
        cp.wait()
    for n in range(9):
        CB[:, 256 * n : 256 * (n + 1)] = conv_weight[n]
    CB[:, 2304:3328] = expand_weight[...]
    lane = lax.broadcasted_iota(jnp.int32, (32, 128), 1)
    packed = jnp.zeros((32, 128), f32)
    for n, gain in enumerate((gain_middle, gain_inner)):
        column = mm(jnp.broadcast_to(gain[...], (8, 32)), eighth, 0, 0, HIGHEST)
        high, rest = split(column)
        rest = column - high.astype(f32)
        mid, low = split(rest)
        for m, part in enumerate((high, mid, low)):
            packed = jnp.where(lane == 3 * n + m, part.astype(f32), packed)
    CB[:, 3328:3456] = packed.astype(bf16)
    CB[:, 3456:3584] = jnp.zeros((32, 128), bf16)
    quarter = CB.at[:, pl.ds(pl.multiple_of(896 * d, 128), 896)]
    wq_cp = [send(quarter, WQ.at[z], d, zpeer(k)) for k in range(1, 4)]
    WQ[z] = quarter[...]
    WB[c, d, z] = quarter[...]
    wb_cp = [send(WQ.at[z], WB.at[c, d, z], dpeer(k), t) for k in range(1, 4)]

    for cp in w_cp:
        cp.wait_recv()
    WC[...] = mm(eye(256), WT[...], 1, 1).astype(bf16)
    mine = WC[pl.ds(pl.multiple_of(128 * c, 128), 128), :].astype(f32)
    colsum = mm(go_rows, mine, 1, 0, HIGHEST)[0:1]
    for n in range(8):
        ST[n, 2:3, 0:256] = colsum
    reduced_sum = Summed(QS, QR)
    for n, p in enumerate((*order, z)):
        x_cp[n].wait_recv()
        QF[...] = mm(XK[p], WC[...], 0, 0)
        part = QF[pl.ds(pl.multiple_of(64 * c, 64), 576), :]
        if n == 3:
            QO[...] = part
        else:
            QS[n] = part.astype(bf16)
            reduced_sum.start(n)
        if n == 0:
            st_cp = [send(ST.at[(t + k) % 8], SR.at[t], d, (t + k) % 8) for k in range(1, 8)]
            SR[t] = ST[t]
    placed_gather.start(partner)
    placed_gather.own()


    for n in range(1, 4):
        wq_cp[n - 1].wait_recv()
        block = (z + 4 - n) % 4
        wb_cp += [send(WQ.at[block], WB.at[c, d, block], dpeer(k), t) for k in range(1, 4)]
        WB[c, d, block] = WQ[block]
    reduced_sum.add(0)
    placed_gather.forward(far_mid, 0)
    reduced_sum.add(1)
    ws_cp = [send(WB.at[c, d], WB.at[c, d], d, sib)]
    for k in range(1, 4):
        for n in range(4):
            wb_cp[3 * n + k - 1].wait_recv()
        quarter = (d + 4 - k) % 4
        ws_cp.append(send(WB.at[c, quarter], WB.at[c, quarter], d, sib))
    for cp in ws_cp:
        cp.wait_recv()

    def spread_out(lo, hi):
        for cc in range(2):
            for zz in range(4):
                rows = slice(32 * (2 * zz + cc), 32 * (2 * zz + cc + 1))
                for dd in range(lo // 896, (hi + 895) // 896):
                    x, y = max(lo, 896 * dd), min(hi, 896 * (dd + 1))
                    WF[rows, x:y] = WB[cc, dd, zz, :, x - 896 * dd : y - 896 * dd]

    spread_out(0, 2304)
    spread_out(3328, 3456)
    lane = lax.broadcasted_iota(jnp.int32, (8, 128), 1)
    row = lax.broadcasted_iota(jnp.int32, (8, 128), 0)
    pick = jnp.where((lane >= 3 * row) & (lane < 3 * row + 3) & (row < 2), 1.0, 0.0).astype(bf16)
    gains = mm(pick, WF[:, 3328:3456], 1, 1)
    gm, gi = gains[0:1], gains[1:2]

    for cp in st_cp:
        cp.wait_recv()
    m_t = SR[:, 0, :]
    q_t = SR[:, 1, :]
    sums = SR[:, 2, 0:256]
    mean = jnp.mean(m_t, axis=0, keepdims=True)
    dm = m_t - mean
    var = (jnp.sum(q_t, axis=0, keepdims=True) + 128.0 * jnp.sum(dm * dm, axis=0, keepdims=True)) * (1.0 / 1024.0)
    rstd = lax.rsqrt(var + epsilon)
    valid = pl.ds(pl.multiple_of(64 * c, 64), 576)
    QF[...] = mm(dm, sums, 0, 0, HIGHEST)
    total = QO[...] + QF[valid, :]
    QF[...] = mm(jnp.broadcast_to(rstd, (8, 640)), jnp.full((8, 256), 0.125, f32), 0, 0, HIGHEST)
    scale = QF[valid, :]
    total = reduced_sum.result(total)
    RED[...] = jnp.zeros((24, 32, 256), f32)
    RED[:, 0:24, :] = (total * scale).reshape(24, 24, 256)

    xm, rm = norm_rows(RED[...].reshape(768, 256))
    zm = xm * gm
    hidden = zm * jax.nn.sigmoid(zm)
    XM[...], ZM[...], RM[...] = xm, zm, jnp.broadcast_to(rm, (768, 128))
    HB[0:32, :] = jnp.zeros((32, 768), bf16)
    HB[800:832, :] = jnp.zeros((32, 768), bf16)
    HB[32:800, 0:256] = pltpu.roll(hidden, 1, 0).astype(bf16)
    HB[32:800, 256:512] = hidden.astype(bf16)
    HB[32:800, 512:768] = pltpu.roll(hidden, 767, 0).astype(bf16)
    conv = mm(HB[0:768, :], WF[:, 0:768], 1, 1)
    conv += mm(HB[32:800, :], WF[:, 768:1536], 1, 1)
    conv += mm(HB[64:832, :], WF[:, 1536:2304], 1, 1)
    xi, ri = norm_rows(conv)
    zi = xi * gi
    activated = (zi * jax.nn.sigmoid(zi)).astype(bf16)
    XI[...], ZI[...], RI[...] = xi, zi, jnp.broadcast_to(ri, (768, 128))
    pool = pool_wide()
    ACT[t] = mm(pool, activated, 1, 0).astype(bf16)
    a_cp = [send(ACT.at[t], ACT.at[t], d, zpeer(k)) for k in range(1, 4)]
    as_cp = [send(ACT.at[t], ACT.at[t], d, sib)]

    placed_gather.forward(far_end, 0)
    for cp in operand_cp:
        cp.wait()
    spread_out(2304, 3328)
    MT[...] = mm(readout_weight[...], WF[:, 2304:3328], 1, 1).astype(bf16)
    for n, q in enumerate(blocks):
        if n == 0:
            placed_gather.pass_on(1)
            placed_gather.pass_on(2)
        if n == 3:
            for k in range(1, 4):
                a_cp[k - 1].wait_recv()
                slot = 2 * ((z + 4 - k) % 4) + c
                as_cp.append(send(ACT.at[slot], ACT.at[slot], d, sib))
            placed_gather.pass_on(3)
        placed_gather.ready(n)
        both = jnp.concatenate([PP[2 * q], PP[2 * q + 1]], axis=1)
        part = mm(readout_weight[:, pl.ds(pl.multiple_of(256 * q, 256), 256)], both, 1, 1)
        if n == 0:
            BEF[...] = part
        else:
            BEF[...] += part

    for cp in as_cp:
        cp.wait_recv()
    for n in range(8):
        ACL[n] = (ACT[n].astype(f32) * slot_live[n].astype(f32)).astype(bf16)
    act_live = ACL[...].reshape(1152, 256)
    BEF[...] += mm(MT[...], act_live, 1, 1)

    @pl.loop(0, 16)
    def _(u):
        rows = pl.ds(pl.multiple_of(32 * u, 32), 32)
        b = BEF[rows, :]
        bell = jnp.exp(-0.5 * b * b)
        density = bell * 0.3989422804014327
        u = 1.0 / (1.0 + 0.23164189 * jnp.abs(b))
        beyond = u * (0.127414796 + u * (-0.142248368 + u * (0.7107068705 + u * (-0.7265760135 + u * 0.5307027145)))) * bell
        below = jnp.where(b >= 0.0, 1.0 - beyond, beyond)
        RO[rows, :] = (b * below).astype(bf16)
        GBT[rows, :] = (cotangent[rows, :].astype(f32) * (below + b * density)).astype(bf16)

    store(RO, readout_o)
    GBR[...] = jnp.transpose(GBT[...])
    terms = mm(GBR[...], MT[...], 1, 0).astype(bf16).reshape(8, 144, 256)
    for n in range(8):
        AT[n % 2, n // 2] = terms[n]
    at_cp = send(AT.at[1 - c], AR, d, sib)
    pooled_sum = Summed(ES, ER)
    te_cp = []

    def pooled_block(n):
        te_cp[n].wait_recv()
        ES[n] = (TE[c, order[n]].astype(f32) + TR[order[n]].astype(f32)).astype(bf16)
        if n < 2:
            pooled_sum.start(n)

    for n, q in enumerate((*order, z)):
        block = mm(GBR[...], readout_weight[:, pl.ds(pl.multiple_of(256 * q, 256), 256)], 1, 0).astype(bf16)
        TE[0, q] = block[:, 0:128]
        TE[1, q] = block[:, 128:256]
        te_cp.append(send(TE.at[1 - c, q], TR.at[q], d, sib))
        if n == 0:
            at_cp.wait_recv()
            az_cp = []
            for k in (1, 2, 3):
                p = (z + k) % 4
                AS[k - 1] = (AT[c, p].astype(f32) + AR[p].astype(f32)).astype(bf16)
                az_cp.append(send(AS.at[k - 1], AZ.at[k - 1], d, zpeer(k)))
            grad_act = AT[c, z].astype(f32) + AR[z].astype(f32)
        else:
            pooled_block(n - 1)
    te_cp[3].wait_recv()
    GP[...] = TE[c, z].astype(f32) + TR[z].astype(f32)
    for q in range(4):
        both = jnp.concatenate([PP[2 * q], PP[2 * q + 1]], axis=1).astype(f32)
        POOLED[:, 256 * q : 256 * (q + 1)] = (both + mm(act_live, WF[:, 2304 + 256 * q : 2560 + 256 * q], 1, 0)).astype(bf16)
    for q in range(4):
        GR[q] = mm(GBT[128 * q : 128 * (q + 1), :], POOLED[...], 1, 0).astype(bf16)
    gr_cp = [send(GR.at[(d + k) % 4], GRR.at[d], dpeer(k), t) for k in range(1, 4)]
    GRR[d] = GR[d]

    for cp in az_cp:
        cp.wait_recv()
    for k in range(3):
        grad_act += AZ[k].astype(f32)
    pooled_sum.add(0)
    high, low = split(grad_act * slot_live[t].astype(f32))
    grad_rows = mm(pool, high, 0, 0) + mm(pool, low, 0, 0)
    zi = ZI[...]
    gate = jax.nn.sigmoid(zi)
    dy = grad_rows * (gate * (1.0 + zi * (1.0 - gate)))
    xi = XI[...]
    dyx_inner = dy * xi
    gc = norm_rows_back(dy * gi, xi, RI[:, 0:1]).astype(bf16)
    GB[0:32, :] = jnp.zeros((32, 256), bf16)
    GB[800:832, :] = jnp.zeros((32, 256), bf16)
    GB[32:800, :] = gc
    back = mm(GB[64:832, :], WF[:, 0:768], 1, 0)
    back += mm(GB[32:800, :], WF[:, 768:1536], 1, 0)
    back += mm(GB[0:768, :], WF[:, 1536:2304], 1, 0)
    grad_hidden = pltpu.roll(back[:, 0:256], 767, 0) + back[:, 256:512] + pltpu.roll(back[:, 512:768], 1, 0)
    zm = ZM[...]
    gate = jax.nn.sigmoid(zm)
    inside = (lax.broadcasted_iota(jnp.int32, (768, 256), 0) & 31) < 24
    dy = jnp.where(inside, grad_hidden * (gate * (1.0 + zm * (1.0 - gate))), 0.0)
    xm = XM[...]
    dyx_middle = dy * xm
    gr = norm_rows_back(dy * gm, xm, RM[:, 0:1]).reshape(24, 32, 256)[:, 0:24, :].reshape(576, 256).astype(bf16)
    GA[t] = gr
    grad_gather = Gather(GA, 4)
    grad_gather.start(far_mid)
    wg = jnp.sum(sums, axis=0, keepdims=True)
    grad_rounded = gr.astype(f32)
    s1 = jnp.sum(grad_rounded * wg, axis=1, keepdims=True)
    s2 = jnp.sum(grad_rounded * RED[:, 0:24, :].reshape(576, 256), axis=1, keepdims=True)
    lane = lax.broadcasted_iota(jnp.int32, (576, 128), 1)
    RSC[0:64, :] = jnp.zeros((64, 128), f32)
    RSC[576:640, :] = jnp.zeros((64, 128), f32)
    RSC[valid, :] = jnp.where(lane == 0, s1, s2) * (1.0 / 1024.0)
    row_sums = jnp.transpose(RSC[...])
    RS[t, 0:1, :] = mean
    RS[t, 1:2, :] = rstd
    RS[t, 2:4, :] = row_sums[0:2]
    rs_cp = [send(RS.at[t], RS.at[t], d, (t + k) % 8) for k in range(1, 8)]
    grad_gather.start(partner)
    pooled_sum.start(2)
    grad_gather.own()
    pooled_sum.add(1)

    for cp in gr_cp:
        cp.wait_recv()
    total = GRR[0].astype(f32)
    for n in range(1, 4):
        total += GRR[n].astype(f32)
    GRF[d] = total.astype(bf16)
    grf_cp = [send(GRF.at[d], GRF.at[d], dpeer(k), t) for k in range(1, 4)]

    def put(lo, value):
        value = value.astype(bf16)
        for n in range(8):
            CG[n % 2, n // 2, :, lo : lo + value.shape[1]] = value[32 * n : 32 * (n + 1)]

    for a in range(3):
        put(768 * a, mm(gc, HB[32 * a : 32 * a + 768, :], 0, 0))
    ones = jnp.ones((768, 128), bf16)
    for lo, value in ((2304, dyx_inner), (2432, dyx_middle)):
        high, low = split(value)
        put(lo, mm(high, ones, 0, 0) + mm(low, ones, 0, 0))
    cg_cp = send(CG.at[1 - c], CGR, d, sib)

    cg_cp.wait_recv()
    CGS[...] = (CG[c].astype(f32) + CGR[...].astype(f32)).astype(bf16)
    cgd_cp = []
    for k in range(1, 4):
        dd = dpeer(k)
        cgd_cp.append(send(CGS.at[:, :, pl.ds(pl.multiple_of(640 * dd, 128), 640)], CGD.at[d], dd, t))
    CGD[d] = CGS[:, :, pl.ds(pl.multiple_of(640 * d, 128), 640)]

    for h in range(4):
        grad_gather.forward(far_mid, h)
    def turn(n):
        for k in range(1, 8):
            s = (t + k) % 8
            yield send(FT.at[n, pl.ds(pl.multiple_of(32 * s, 32), 32)], TA.at[n, d, t], d, s)
        TA[n, d, t] = FT[n, pl.ds(pl.multiple_of(32 * t, 32), 32), :]

    for cp in rs_cp:
        cp.wait_recv()
    w_own = WC[pl.ds(pl.multiple_of(128 * c, 128), 128), :]
    lane = lax.broadcasted_iota(jnp.int32, (4, 128), 1)
    gain_sum = jnp.zeros((128, 1), f32)
    grad_reduce = jnp.zeros((128, 256), f32)
    for n, p in enumerate(blocks):
        if n == 0:
            grad_gather.pass_on(1)
        if n == 1:
            for h in range(4):
                grad_gather.forward(far_end, h)
            grad_gather.pass_on(2)
            gp = pooled_sum.result(GP[...])
            gp_high, gp_low = split(gp)
            FT[0] = mm(act_live, gp_high, 0, 0).astype(bf16)
            turn_cp = list(turn(0))
            for m in range(4):
                cells = slice(288 * m, 288 * (m + 1))
                SP[:, 1152 * m : 1152 * (m + 1)] = mm(gp_high[cells], POOL[...], 0, 0) + mm(gp_low[cells], POOL[...], 0, 0)
            for cp in cgd_cp:
                cp.wait_recv()
            total = CGD[0].astype(f32)
            for m in range(1, 4):
                total += CGD[m].astype(f32)
            CGT[...] = total.astype(bf16)
            cgz_cp = [send(CGT.at[(z + k) % 4], CGZ.at[z], d, zpeer(k)) for k in range(1, 4)]
            CGZ[z] = CGT[z]
        if n == 3:
            for cp in turn_cp[0:7]:
                cp.wait_recv()
            ta_cp = [send(TA.at[0, d], TA.at[0, d], dpeer(k), t) for k in range(1, 4)]
            for cp in cgz_cp:
                cp.wait_recv()
            total = CGZ[0].astype(f32)
            for m in range(1, 4):
                total += CGZ[m].astype(f32)
            CGF[d] = total.astype(bf16)
            cgf_cp = [send(CGF.at[d], CGF.at[d], dpeer(k), t) for k in range(1, 4)]
            grad_gather.pass_on(3)
        grad_gather.ready(n)
        cols = pl.ds(pl.multiple_of(1152 * p, 128), 1152)
        even, odd = RS[2 * p], RS[2 * p + 1]
        stats = jnp.concatenate([even[:, 0:512], jnp.where(lane < 64, even[:, 512:640], odd[:, 0:128]), odd[:, 128:640]], axis=1)
        g = GA[pl.ds(2 * p, 2)].reshape(1152, 256)
        xhat = (PLC[:, cols] - stats[0:1]) * stats[1:2]
        grad_reduce += mm((xhat * go).astype(bf16), g, 1, 0)
        if n == 3:
            FT[1] = jnp.transpose(grad_reduce).astype(bf16)
            turn_cp += list(turn(1))
        gn = mm(w_own, g, 1, 1)
        gain_sum += jnp.sum(gn * xhat, axis=1, keepdims=True)
        GF[:, cols] = stats[1:2] * (gn * go - stats[2:3] - xhat * stats[3:4])
    place_sum = jnp.zeros((128, 1152), f32)
    for p in range(4):
        cols = slice(1152 * p, 1152 * (p + 1))
        out = GF[:, cols] + SP[:, cols]
        GF[:, cols] = out
        store(GF.at[:, cols], gfeat_o.at[:, cols])
        place_sum += out
    odd = pltpu.roll(place_sum, 576, 1)
    lane = lax.broadcasted_iota(jnp.int32, (128, 640), 1)
    place = jnp.where(lane < 576, place_sum[:, 0:640] + odd[:, 0:640], jnp.broadcast_to(gain_sum, (128, 640))).astype(bf16)
    for q in range(4):
        PM[q] = place[32 * q : 32 * (q + 1)]
    pm_cp = [send(PM.at[dpeer(k)], PR.at[d], dpeer(k), t) for k in range(1, 4)]
    PR[d] = PM[d]

    for cp in turn_cp[7:14]:
        cp.wait_recv()
    ta_cp += [send(TA.at[1, d], TA.at[1, d], dpeer(k), t) for k in range(1, 4)]
    for cp in pm_cp:
        cp.wait_recv()
    total = PR[0].astype(f32)
    for n in range(1, 4):
        total += PR[n].astype(f32)
    PF[d] = total.astype(bf16)
    pf_cp = [send(PF.at[d], PF.at[d], dpeer(k), t) for k in range(1, 4)]
    for cp in grf_cp:
        cp.wait_recv()
    for q in range(4):
        store(GRF.at[q], gread_o.at[pl.ds(128 * q, 128)])
    for cp in cgf_cp:
        cp.wait_recv()
    for q in range(4):
        gconv_o[:, 640 * q : 640 * (q + 1)] = CGF[q]
    for cp in ta_cp:
        cp.wait_recv()
    for n, out in enumerate((gexp_o, gred_o)):
        for s in range(8):
            total = TA[n, 0, s].astype(f32)
            for m in range(1, 4):
                total += TA[n, m, s].astype(f32)
            out[:, 128 * s : 128 * (s + 1)] = total
    for cp in pf_cp:
        cp.wait_recv()
    gpos_o[...] = jnp.transpose(PF[...].reshape(128, 640).astype(f32))
    for cp in result_cp:
        cp.wait()
    for cp in pending:
        cp.wait_send()
    placed_gather.drain()
    grad_gather.drain()


SCRATCH = (
    ("features", (128, 4608), bf16), ("position", (576, 128), f32), ("conv_weight", (9, 32, 256), bf16), ("expand_weight", (32, 1024), bf16), ("readout_weight", (512, 1024), bf16), ("cotangent", (512, 1152), bf16), ("RO", (512, 1152), bf16), ("GF", (128, 4608), f32), ("SP", (128, 4608), f32), ("WT", (256, 256), bf16), ("WC", (256, 256), bf16), ("CB", (32, 3584), bf16),
    ("WQ", (4, 32, 896), bf16), ("WB", (2, 4, 4, 32, 896), bf16), ("WF", (256, 3584), bf16), ("MT", (512, 256), bf16),
    ("POOL", (288, 1152), bf16), ("PLC", (128, 4608), f32), ("XW", (2, 4, 128, 640), bf16), ("XK", (4, 256, 640), bf16),
    ("ST", (8, 4, 640), f32), ("SR", (8, 4, 640), f32), ("QF", (640, 256), f32), ("QS", (3, 576, 256), bf16),
    ("QO", (576, 256), f32), ("QR", (4, 576, 256), bf16), ("RED", (24, 32, 256), f32), ("HB", (832, 768), bf16),
    ("GB", (832, 256), bf16), ("XM", (768, 256), f32), ("ZM", (768, 256), f32), ("RM", (768, 128), f32),
    ("XI", (768, 256), f32), ("ZI", (768, 256), f32), ("RI", (768, 128), f32), ("ACT", (8, 144, 256), bf16), ("ACL", (8, 144, 256), bf16),
    ("PP", (8, 1152, 128), bf16), ("POOLED", (1152, 1024), bf16), ("BEF", (512, 1152), f32), ("GBT", (512, 1152), bf16), ("GBR", (1152, 512), bf16),
    ("TE", (2, 4, 1152, 128), bf16), ("TR", (4, 1152, 128), bf16), ("ES", (3, 1152, 128), bf16), ("ER", (4, 1152, 128), bf16),
    ("GP", (1152, 128), f32), ("AT", (2, 4, 144, 256), bf16), ("AR", (4, 144, 256), bf16), ("AS", (3, 144, 256), bf16),
    ("AZ", (3, 144, 256), bf16), ("RSC", (640, 128), f32), ("GA", (8, 576, 256), bf16), ("RS", (8, 4, 640), f32),
    ("FT", (2, 256, 128), bf16), ("TA", (2, 4, 8, 32, 128), bf16), ("PM", (4, 32, 640), bf16),
    ("PR", (4, 32, 640), bf16), ("PF", (4, 32, 640), bf16),
    ("CG", (2, 4, 32, 2560), bf16), ("CGR", (4, 32, 2560), bf16), ("CGS", (4, 32, 2560), bf16), ("CGD", (4, 4, 32, 640), bf16),
    ("CGT", (4, 32, 640), bf16), ("CGZ", (4, 32, 640), bf16), ("CGF", (4, 32, 640), bf16), ("GR", (4, 128, 1024), bf16), ("GRR", (4, 128, 1024), bf16),
    ("GRF", (4, 128, 1024), bf16),
)


def finish(
    readout, gfeat, gpos, gexp, gred, gconv, gread, readout_o, gfeat_o, gpos_o, ggo_o, gred_o, ggm_o, gconv_o, ggi_o, gexp_o, gread_o,
    RO, GF, GB, GC, GR, GP, GQ, GE, GD, sem,
):
    copies = []

    def copy(src, dst):
        cp = pltpu.make_async_copy(src, dst, sem.at[len(copies)])
        copies.append(cp)
        cp.start()
        return cp

    loads = [copy(gread.at[pl.ds(256 * p, 256)], GB.at[pl.ds(256 * p, 256)]) for p in range(2)]
    loads += [copy(gfeat.at[pl.ds(32 * p, 32)], GF.at[pl.ds(32 * p, 32)]) for p in range(4)]
    loads += [copy(readout, RO), copy(gconv, GC), copy(gpos, GP), copy(gexp, GE), copy(gred, GD)]
    stores = []
    for p in range(2):
        rows = pl.ds(256 * p, 256)
        loads[p].wait()
        GR[rows, :] = GB[rows, :].astype(f32)
        stores.append(copy(GR.at[rows], gread_o.at[rows]))
    for p in range(4):
        rows = pl.ds(32 * p, 32)
        loads[2 + p].wait()
        stores.append(copy(GF.at[rows], gfeat_o.at[rows]))
    loads[6].wait()
    stores.append(copy(RO, readout_o))
    loads[7].wait()
    for n in range(9):
        GQ[n] = GC[:, 256 * n : 256 * (n + 1)].astype(f32)
    stores.append(copy(GQ, gconv_o))
    first = (lax.broadcasted_iota(jnp.int32, (8, 128), 1) == 0).astype(f32).astype(bf16)
    ggi_o[...] = mm(first, GC[:, 2304:2432], 1, 1)[0:1]
    ggm_o[...] = mm(first, GC[:, 2432:2560], 1, 1)[0:1]
    loads[8].wait()
    stores.append(copy(GP.at[pl.ds(0, 576)], gpos_o))
    ggo_o[...] = GP[576:577, :]
    loads[9].wait()
    stores.append(copy(GE, gexp_o))
    loads[10].wait()
    stores.append(copy(GD, gred_o))
    for cp in stores:
        cp.wait()


def local_by_image(features, slot_live, position, gain_outer, reduce_weight, gain_middle, conv_weight, gain_inner, expand_weight, readout_weight, cotangent):
    vmem = pl.BlockSpec(memory_space=pltpu.VMEM)
    smem = pl.BlockSpec(memory_space=pltpu.SMEM)
    hbm = pl.BlockSpec(memory_space=pl.ANY)

    def shapes(*pairs):
        return tuple(jax.ShapeDtypeStruct(shape, dtype) for shape, dtype in pairs)

    parts = pl.pallas_call(
        kernel,
        out_shape=shapes(
            ((512, 1152), bf16), ((128, 4608), f32), ((640, 128), f32), ((32, 1024), f32), ((32, 1024), f32), ((32, 2560), bf16), ((512, 1024), bf16)
        ),
        in_specs=[hbm, smem, hbm, vmem, vmem, vmem, hbm, vmem, hbm, hbm, hbm],
        out_specs=[hbm, hbm, vmem, vmem, vmem, vmem, hbm],
        scratch_shapes=[pltpu.VMEM(shape, dtype) for _, shape, dtype in SCRATCH]
        + [pltpu.SemaphoreType.DMA((COPIES,)), pltpu.SemaphoreType.DMA((COPIES,)), pltpu.SemaphoreType.DMA((24,))],
        compiler_params=pltpu.CompilerParams(collective_id=0, has_side_effects=True, vmem_limit_bytes=60 * 2**20),
    )(
        features, slot_live, position.reshape(576, 128), gain_outer.reshape(1, 128), reduce_weight.T, gain_middle.reshape(1, 32),
        conv_weight.transpose(0, 1, 3, 2).reshape(9, 32, 256), gain_inner.reshape(1, 32), expand_weight, readout_weight, cotangent,
    )
    readout, gfeat, gpos, ggo, gred, ggm, gconv, ggi, gexp, gread = pl.pallas_call(
        finish,
        out_shape=shapes(
            ((512, 1152), bf16), ((128, 4608), f32), ((576, 128), f32), ((1, 128), f32), ((32, 1024), f32), ((1, 32), f32),
            ((9, 32, 256), f32), ((1, 32), f32), ((32, 1024), f32), ((512, 1024), f32),
        ),
        in_specs=[hbm] * 7,
        out_specs=[hbm, hbm, hbm, vmem, hbm, vmem, hbm, vmem, hbm, hbm],
        scratch_shapes=[
            pltpu.VMEM((512, 1152), bf16), pltpu.VMEM((128, 4608), f32), pltpu.VMEM((512, 1024), bf16), pltpu.VMEM((32, 2560), bf16),
            pltpu.VMEM((512, 1024), f32), pltpu.VMEM((640, 128), f32), pltpu.VMEM((9, 32, 256), f32), pltpu.VMEM((32, 1024), f32),
            pltpu.VMEM((32, 1024), f32), pltpu.SemaphoreType.DMA((24,)),
        ],
        compiler_params=pltpu.CompilerParams(vmem_limit_bytes=60 * 2**20),
    )(*parts)
    return (
        readout, gfeat, gpos.reshape(24, 24, 128), ggo.reshape(128), gred.T, ggm.reshape(32),
        gconv.reshape(3, 3, 32, 256).transpose(0, 1, 3, 2), ggi.reshape(32), gexp, gread,
    )


def row_totals(leading, trailing):
    return lax.psum((leading, trailing), "tensor")


def norm_forward(values, norm_gain, breadth):
    totals, squares = row_totals(jnp.sum(values, axis=1), jnp.sum(values * values, axis=1))
    center = totals / breadth
    spread = squares / breadth - center * center
    scaled = lax.rsqrt(spread + epsilon)[:, None]
    normed = (values - center[:, None]) * scaled
    return (normed, scaled, normed * norm_gain)


def norm_backward(grad_out, normed, scaled, norm_gain, breadth):
    grad_normed = grad_out * norm_gain
    gain_grad = jnp.sum(grad_out * normed, axis=0)
    leading, trailing = row_totals(
        jnp.sum(grad_normed, axis=1), jnp.sum(grad_normed * normed, axis=1)
    )
    grad_in = scaled * (
        grad_normed - leading[:, None] / breadth - normed * (trailing[:, None] / breadth)
    )
    return (grad_in, gain_grad)


def silu_grad(inputs):
    gate_value = jax.nn.sigmoid(inputs)
    return gate_value * (1.0 + inputs * (1.0 - gate_value))


def gelu_grad(inputs):
    below = 0.5 * (1.0 + lax.erf(inputs * 0.7071067811865476))
    density = jnp.exp(-0.5 * inputs * inputs) * 0.3989422804014327
    return below + inputs * density


def contract_rows(left_side, right_side):
    return lax.dot_general(
        left_side, right_side, (((0,), (0,)), ((), ())), preferred_element_type=jnp.float32
    )


def window_of(padded, shift_down, shift_across, grid_side):
    images = padded.shape[0]
    breadth = padded.shape[3]
    return padded[
        :, shift_down : shift_down + grid_side, shift_across : shift_across + grid_side, :
    ].reshape(images * grid_side * grid_side, breadth)


def local_by_hidden(
    features,
    slot_live,
    position,
    gain_outer,
    reduce_weight,
    gain_middle,
    conv_weight,
    gain_inner,
    expand_weight,
    readout_weight,
    cotangent,
):
    grid_side = position.shape[0]
    half_side = grid_side // 2
    channel_share = features.shape[0]
    row_count = features.shape[1]
    images = row_count // (grid_side * grid_side)
    tensor_size = lax.axis_size("tensor")
    channels = channel_share * tensor_size
    hidden_share = reduce_weight.shape[1]
    hidden_width = hidden_share * tensor_size
    pooled_count = images * half_side * half_side
    placed = (
        features.T.astype(jnp.float32).reshape(images, grid_side * grid_side, channel_share)
        + position.reshape(1, grid_side * grid_side, channel_share)
    ).reshape(row_count, channel_share)
    live_rows = jnp.repeat(slot_live.astype(jnp.float32), grid_side * grid_side)[:, None]
    normed_outer, scaled_outer, shaped_outer = norm_forward(placed, gain_outer, channels)
    reduce_in = shaped_outer.astype(jnp.bfloat16)
    reduce_full = lax.all_gather(reduce_in, "tensor", axis=1, tiled=True)
    reduced = jnp.dot(reduce_full, reduce_weight, preferred_element_type=jnp.float32)
    normed_middle, scaled_middle, shaped_middle = norm_forward(reduced, gain_middle, hidden_width)
    hidden = jax.nn.silu(shaped_middle).astype(jnp.bfloat16)
    hidden_full = lax.all_gather(hidden, "tensor", axis=1, tiled=True)
    padded_hidden = jnp.pad(
        hidden_full.reshape(images, grid_side, grid_side, hidden_width),
        ((0, 0), (1, 1), (1, 1), (0, 0)),
    )
    convolved = jnp.zeros((row_count, hidden_share), jnp.float32)
    for offset_tap in range(9):
        shift_down = offset_tap // 3
        shift_across = offset_tap % 3
        convolved = convolved + jnp.dot(
            window_of(padded_hidden, shift_down, shift_across, grid_side),
            conv_weight[shift_down, shift_across],
            preferred_element_type=jnp.float32,
        )
    normed_inner, scaled_inner, shaped_inner = norm_forward(convolved, gain_inner, hidden_width)
    activated = jax.nn.silu(shaped_inner).astype(jnp.bfloat16)
    expand_terms = jnp.dot(activated, expand_weight, preferred_element_type=jnp.float32)
    expanded = lax.psum_scatter(expand_terms, "tensor", scatter_dimension=1, tiled=True)
    mixed = placed + live_rows * expanded
    pooled = jnp.mean(mixed.reshape(images, half_side, 2, half_side, 2, channel_share), axis=(2, 4))
    pooled_low = pooled.reshape(pooled_count, channel_share).astype(jnp.bfloat16)
    pooled_full = lax.all_gather(pooled_low, "tensor", axis=1, tiled=True)
    before = lax.dot_general(
        pooled_full, readout_weight, (((1,), (1,)), ((), ())), preferred_element_type=jnp.float32
    )
    readout = jax.nn.gelu(before, approximate=False).astype(jnp.bfloat16).T
    grad_before = (cotangent.T.astype(jnp.float32) * gelu_grad(before)).astype(jnp.bfloat16)
    grad_readout = contract_rows(grad_before, pooled_full)
    pooled_terms = jnp.dot(grad_before, readout_weight, preferred_element_type=jnp.float32)
    grad_pooled = lax.psum_scatter(pooled_terms, "tensor", scatter_dimension=1, tiled=True)
    spread_grad = jnp.broadcast_to(
        (0.25 * grad_pooled).reshape(images, half_side, 1, half_side, 1, channel_share),
        (images, half_side, 2, half_side, 2, channel_share),
    )
    grad_mixed = spread_grad.reshape(row_count, channel_share)
    grad_branch = (live_rows * grad_mixed).astype(jnp.bfloat16)
    grad_full = lax.all_gather(grad_branch, "tensor", axis=1, tiled=True)
    grad_expand = contract_rows(activated, grad_full)
    grad_activated = jnp.dot(grad_full, expand_weight.T, preferred_element_type=jnp.float32)
    grad_convolved, grad_gain_inner = norm_backward(
        grad_activated * silu_grad(shaped_inner),
        normed_inner,
        scaled_inner,
        gain_inner,
        hidden_width,
    )
    grad_conv_low = grad_convolved.astype(jnp.bfloat16)
    tap_grads = []
    grad_padded = jnp.zeros((images, grid_side + 2, grid_side + 2, hidden_width), jnp.float32)
    for offset_tap in range(9):
        shift_down = offset_tap // 3
        shift_across = offset_tap % 3
        tap_grads.append(
            contract_rows(
                window_of(padded_hidden, shift_down, shift_across, grid_side), grad_conv_low
            )
        )
        tap_back = jnp.dot(
            grad_conv_low,
            conv_weight[shift_down, shift_across].T,
            preferred_element_type=jnp.float32,
        )
        grad_padded = grad_padded + jnp.pad(
            tap_back.reshape(images, grid_side, grid_side, hidden_width),
            ((0, 0), (shift_down, 2 - shift_down), (shift_across, 2 - shift_across), (0, 0)),
        )
    grad_conv = jnp.stack(tap_grads, axis=0).reshape(conv_weight.shape)
    grad_window = grad_padded[:, 1 : grid_side + 1, 1 : grid_side + 1, :].reshape(
        row_count, hidden_width
    )
    grad_hidden = lax.psum_scatter(grad_window, "tensor", scatter_dimension=1, tiled=True)
    grad_reduced, grad_gain_middle = norm_backward(
        grad_hidden * silu_grad(shaped_middle),
        normed_middle,
        scaled_middle,
        gain_middle,
        hidden_width,
    )
    grad_reduced_low = grad_reduced.astype(jnp.bfloat16)
    grad_reduce = contract_rows(reduce_full, grad_reduced_low)
    outer_terms = jnp.dot(grad_reduced_low, reduce_weight.T, preferred_element_type=jnp.float32)
    grad_shaped_outer = lax.psum_scatter(outer_terms, "tensor", scatter_dimension=1, tiled=True)
    grad_inputs, grad_gain_outer = norm_backward(
        grad_shaped_outer, normed_outer, scaled_outer, gain_outer, channels
    )
    grad_rows = grad_mixed + grad_inputs
    grad_place = jnp.sum(grad_rows.reshape(images, grid_side, grid_side, channel_share), axis=0)
    grad_total = grad_rows.T
    summed = (
        lax.psum(grad_place.astype(jnp.bfloat16), "dp").astype(jnp.float32),
        lax.psum(grad_gain_outer.astype(jnp.bfloat16), "dp").astype(jnp.float32),
        lax.psum(grad_reduce.astype(jnp.bfloat16), "dp").astype(jnp.float32),
        lax.psum(grad_gain_middle.astype(jnp.bfloat16), "dp").astype(jnp.float32),
        lax.psum(grad_conv.astype(jnp.bfloat16), "dp").astype(jnp.float32),
        lax.psum(grad_gain_inner.astype(jnp.bfloat16), "dp").astype(jnp.float32),
        lax.psum(grad_expand.astype(jnp.bfloat16), "dp").astype(jnp.float32),
        lax.psum(grad_readout.astype(jnp.bfloat16), "dp").astype(jnp.float32),
    )
    return (
        readout,
        grad_total,
        summed[0],
        summed[1],
        summed[2],
        summed[3],
        summed[4],
        summed[5],
        summed[6],
        summed[7],
    )


def solution(mesh):
    parts, groups = mesh.shape["tensor"], mesh.shape["dp"]
    specs = (P("tensor", "dp"), P("dp"), P(None, None, "tensor"), P("tensor"), P(None, "tensor"), P("tensor"), P(None, None, None, "tensor"), P("tensor"), P("tensor", None), P("tensor", None), P("tensor", "dp"))

    def whole(*arrays):
        by_image = (parts, groups) == (8, 4) and arrays[1].shape[0] == parts * groups
        return jax.shard_map(
            local_by_image if by_image else local_by_hidden, mesh=mesh, in_specs=specs,
            out_specs=(P("tensor", "dp"), P("tensor", "dp"), *specs[2:10]), check_vma=False,
        )(*arrays)

    return whole
```

```python
import jax
import jax.numpy as jnp
from jax import lax
from jax.experimental import pallas as pl
from jax.experimental.pallas import tpu as pltpu
from jax.sharding import PartitionSpec as P

epsilon = 1e-05
bf16 = jnp.bfloat16
f32 = jnp.float32
COPIES = 160

MESH = pl.DeviceIdType.MESH
HIGHEST = lax.Precision.HIGHEST


def mm(a, b, ca, cb, precision=None):
    return lax.dot_general(a, b, (((ca,), (cb,)), ((), ())), precision=precision, preferred_element_type=f32)


def split(x):
    high = x.astype(bf16)
    return high, (x - high.astype(f32)).astype(bf16)


def eye(n, dtype=bf16):
    return (lax.broadcasted_iota(jnp.int32, (n, n), 0) == lax.broadcasted_iota(jnp.int32, (n, n), 1)).astype(f32).astype(dtype)


def pool_wide():
    spot = lax.broadcasted_iota(jnp.int32, (144, 768), 1)
    cell = lax.broadcasted_iota(jnp.int32, (144, 768), 0)
    i, j = spot >> 5, spot & 31
    return jnp.where(((i >> 1) * 12 + (j >> 1) == cell) & (j < 24), 0.25, 0.0).astype(bf16)


def pool_pair():
    spot = lax.broadcasted_iota(jnp.int32, (288, 1152), 1)
    cell = lax.broadcasted_iota(jnp.int32, (288, 1152), 0)
    i = (spot * 2731) >> 16
    j = spot - i * 24
    return jnp.where((i >> 1) * 12 + (j >> 1) == cell, 0.25, 0.0).astype(bf16)


def norm_rows(v):
    s = v - jnp.mean(v, axis=1, keepdims=True)
    r = lax.rsqrt(jnp.mean(s * s, axis=1, keepdims=True) + epsilon)
    return s * r, r


def norm_rows_back(dx, xhat, r):
    return r * (dx - jnp.mean(dx, axis=1, keepdims=True) - xhat * jnp.mean(dx * xhat, axis=1, keepdims=True))


def kernel(
    features_h, slot_live, position_h, gain_outer, reduce_weight, gain_middle, conv_h, gain_inner, expand_h, readout_h, cotangent_h,
    readout_o, gfeat_o, gpos_o, gexp_o, gred_o, gconv_o, gread_o,
    features, position, conv_weight, expand_weight, readout_weight, cotangent, RO, GF, SP, WT, WC, CB, WQ, WB, WF, MT, POOL, PLC, XW, XK, ST, SR, QF, QS, QO, QR, RED, HB, GB,
    XM, ZM, RM, XI, ZI, RI, ACT, ACL, PP, POOLED, BEF, GBT, GBR, TE, TR, ES, ER, GP, AT, AR, AS, AZ,
    RSC, GA, RS, FT, TA, PM, PR, PF, CG, CGR, CGS, CGD, CGT, CGZ, CGF, GR, GRR, GRF, ssem, rsem, lsem,
):
    d = lax.axis_index("dp")
    t = lax.axis_index("tensor")
    z = t // 2
    c = t % 2
    sib = 2 * z + 1 - c
    side = z // 2
    is_mid = ((z + 1) // 2) % 2
    near_end, near_mid, far_end, far_mid = 3 * side, 1 + side, 3 - 3 * side, 2 - side
    partner = z + 1 - 2 * (z % 2)
    sends, arrivals = [0], [0]
    pending = []

    def copy(src, dst, dd, tt, arrival):
        cp = pltpu.make_async_remote_copy(
            src_ref=src, dst_ref=dst, send_sem=ssem.at[sends[0]], recv_sem=rsem.at[arrival], device_id=(dd, tt), device_id_type=MESH
        )
        sends[0] += 1
        return cp

    def take(n):
        arrivals[0] += n
        return arrivals[0] - n

    def send(src, dst, dd, tt):
        cp = copy(src, dst, dd, tt, take(1))
        cp.start()
        pending.append(cp)
        return cp

    class Gather:
        def __init__(self, buf, parts):
            self.buf, self.parts, self.rows = buf, parts, buf.shape[1] // parts
            self.base = take(4 * parts)
            self.forwards = []

        def view(self, zz, h):
            return self.buf.at[2 * zz + c, pl.ds(h * self.rows, self.rows)]

        def to(self, block, zz, h):
            return copy(self.view(block, h), self.view(block, h), d, 2 * zz + c, self.base + 4 * h + block)

        def start(self, zz):
            for h in range(self.parts):
                cp = self.to(z, zz, h)
                cp.start()
                pending.append(cp)

        def own(self):
            self.siblings = [send(self.buf.at[t], self.buf.at[t], d, sib)]

        def arrived(self, block, h):
            view = self.view(block, h)
            pltpu.make_async_remote_copy(
                src_ref=view, dst_ref=view, send_sem=ssem.at[0], recv_sem=rsem.at[self.base + 4 * h + block],
                device_id=(d, sib), device_id_type=MESH,
            ).wait_recv()

        def forward(self, block, h):
            cp = self.to(block, near_end, h)
            self.forwards.append(cp)

            @pl.when(is_mid == 1)
            def _():
                self.arrived(block, h)
                cp.start()

        def pass_on(self, n):
            for h in range(self.parts):
                if n == 3:
                    self.arrived(blocks[n], h)
                else:

                    @pl.when(is_mid == 0)
                    def _(h=h):
                        self.arrived(blocks[n], h)

            slot = self.buf.at[2 * blocks[n] + c]
            self.siblings.append(send(slot, slot, d, sib))

        def ready(self, n):
            self.siblings[n].wait_recv()

        def drain(self):
            @pl.when(is_mid == 1)
            def _():
                for cp in self.forwards:
                    cp.wait_send()

    order = (
        far_end + is_mid * (near_end - far_end),
        far_mid + is_mid * (far_end - far_mid),
        near_mid + is_mid * (far_mid - near_mid),
    )

    blocks = (z, partner + is_mid * (far_mid - partner), far_mid + is_mid * (far_end - far_mid), far_end + is_mid * (partner - far_end))

    class Summed:
        def __init__(self, out, arrive):
            self.out, self.arrive = out, arrive
            self.base = take(4)
            to = (partner, near_mid + is_mid * (far_end - near_mid), near_mid + is_mid * (far_mid - near_mid))
            slot = (2 * is_mid, 1 + 2 * is_mid, 2 + is_mid)
            self.cps = [copy(out.at[n], arrive.at[slot[n]], d, 2 * to[n] + c, self.base + slot[n]) for n in range(3)]
            pending.extend(self.cps)

        def wait(self, n):
            view = self.arrive.at[n]
            pltpu.make_async_remote_copy(
                src_ref=view, dst_ref=view, send_sem=ssem.at[0], recv_sem=rsem.at[self.base + n], device_id=(d, sib), device_id_type=MESH
            ).wait_recv()

        def start(self, n):
            if n == 0:
                self.cps[0].start()
            else:

                @pl.when(is_mid == 0)
                def _():
                    self.cps[n].start()

        def add(self, n):
            @pl.when(is_mid == 1)
            def _():
                self.wait(n)
                self.out[n + 1] = (self.out[n + 1].astype(f32) + self.arrive[n].astype(f32)).astype(bf16)
                self.cps[n + 1].start()

        def result(self, own):
            self.wait(2)
            self.wait(3)
            return own + self.arrive[2].astype(f32) + self.arrive[3].astype(f32)

    def zpeer(k):
        return 2 * ((z + k) % 4) + c

    def dpeer(k):
        return (d + k) % 4

    def load(n, src, dst):
        cp = pltpu.make_async_copy(src, dst, lsem.at[n])
        cp.start()
        return cp

    result_cp = []

    def store(src, dst):
        cp = pltpu.make_async_copy(src, dst, lsem.at[9 + len(result_cp)])
        cp.start()
        result_cp.append(cp)

    barrier = pltpu.get_barrier_semaphore()
    for k in range(1, 8):
        pl.semaphore_signal(barrier, 1, device_id=(d, (t + k) % 8), device_id_type=MESH)
    for k in range(1, 4):
        pl.semaphore_signal(barrier, 1, device_id=(dpeer(k), t), device_id_type=MESH)

    position_cp = load(0, position_h, position)
    feature_cp = []
    for n, p in enumerate((*order, z)):
        cols = pl.ds(pl.multiple_of(1152 * p, 128), 1152)
        feature_cp.append(load(1 + n, features_h.at[:, cols], features.at[:, cols]))
    weight_cp = [load(5, conv_h, conv_weight), load(6, expand_h, expand_weight)]
    operand_cp = [load(7, readout_h, readout_weight), load(8, cotangent_h, cotangent)]
    POOL[...] = pool_pair()
    pl.semaphore_wait(barrier, 10)

    w_cp = []
    for k in range(1, 8):
        s = (t + k) % 8
        w_cp.append(send(reduce_weight.at[:, pl.ds(pl.multiple_of(256 * (s // 2), 256), 256)], WT.at[pl.ds(pl.multiple_of(32 * t, 32), 32)], d, s))
    WT[pl.ds(pl.multiple_of(32 * t, 32), 32), :] = reduce_weight[:, pl.ds(pl.multiple_of(256 * z, 256), 256)]
    position_cp.wait()
    go_rows = jnp.broadcast_to(gain_outer[...], (8, 128))
    eighth = jnp.full((8, 128), 0.125, f32)
    go = mm(go_rows, eighth, 0, 0, HIGHEST)[:, 0:1]
    pos = position[...]
    pos_pair = mm(eye(128, f32), jnp.concatenate([pos, pos], axis=0), 1, 1, HIGHEST)
    x_cp = []
    for n, p in enumerate((*order, z)):
        cols = pl.ds(pl.multiple_of(1152 * p, 128), 1152)
        feature_cp[n].wait()
        x = features[:, cols].astype(f32) + pos_pair
        PLC[:, cols] = x
        m = jnp.mean(x, axis=0, keepdims=True)
        x = x - m
        q = jnp.sum(x * x, axis=0, keepdims=True)
        x = (x * go).astype(bf16)
        for par, lo in ((0, 0), (1, 512)):
            XW[par, p] = x[:, lo : lo + 640]
            ST[2 * p + par, 0:1, :] = m[:, lo : lo + 640]
            ST[2 * p + par, 1:2, :] = q[:, lo : lo + 640]
        x_cp.append(send(XW.at[1 - c, p], XK.at[p, pl.ds(pl.multiple_of(128 * c, 128), 128)], d, sib))
        XK[p, pl.ds(pl.multiple_of(128 * c, 128), 128), :] = XW[c, p]

    for cp in weight_cp:
        cp.wait()
    for n in range(9):
        CB[:, 256 * n : 256 * (n + 1)] = conv_weight[n]
    CB[:, 2304:3328] = expand_weight[...]
    lane = lax.broadcasted_iota(jnp.int32, (32, 128), 1)
    packed = jnp.zeros((32, 128), f32)
    for n, gain in enumerate((gain_middle, gain_inner)):
        column = mm(jnp.broadcast_to(gain[...], (8, 32)), eighth, 0, 0, HIGHEST)
        high, rest = split(column)
        rest = column - high.astype(f32)
        mid, low = split(rest)
        for m, part in enumerate((high, mid, low)):
            packed = jnp.where(lane == 3 * n + m, part.astype(f32), packed)
    CB[:, 3328:3456] = packed.astype(bf16)
    CB[:, 3456:3584] = jnp.zeros((32, 128), bf16)
    quarter = CB.at[:, pl.ds(pl.multiple_of(896 * d, 128), 896)]
    wq_cp = [send(quarter, WQ.at[z], d, zpeer(k)) for k in range(1, 4)]
    WQ[z] = quarter[...]
    WB[c, d, z] = quarter[...]
    wb_cp = [send(WQ.at[z], WB.at[c, d, z], dpeer(k), t) for k in range(1, 4)]

    for p in range(4):
        high, low = split(PLC[:, 1152 * p : 1152 * (p + 1)])
        PP[t, 288 * p : 288 * (p + 1), :] = (mm(POOL[...], high, 1, 1) + mm(POOL[...], low, 1, 1)).astype(bf16)
    placed_gather = Gather(PP, 1)
    for cp in w_cp:
        cp.wait_recv()
    WC[...] = mm(eye(256), WT[...], 1, 1).astype(bf16)
    mine = WC[pl.ds(pl.multiple_of(128 * c, 128), 128), :].astype(f32)
    colsum = mm(go_rows, mine, 1, 0, HIGHEST)[0:1]
    for n in range(8):
        ST[n, 2:3, 0:256] = colsum
    reduced_sum = Summed(QS, QR)
    for n, p in enumerate((*order, z)):
        x_cp[n].wait_recv()
        QF[...] = mm(XK[p], WC[...], 0, 0)
        part = QF[pl.ds(pl.multiple_of(64 * c, 64), 576), :]
        if n == 3:
            QO[...] = part
        else:
            QS[n] = part.astype(bf16)
            reduced_sum.start(n)
        if n == 0:
            st_cp = [send(ST.at[(t + k) % 8], SR.at[t], d, (t + k) % 8) for k in range(1, 8)]
            SR[t] = ST[t]
    placed_gather.start(far_mid)
    placed_gather.start(partner)
    placed_gather.own()


    for n in range(1, 4):
        wq_cp[n - 1].wait_recv()
        block = (z + 4 - n) % 4
        wb_cp += [send(WQ.at[block], WB.at[c, d, block], dpeer(k), t) for k in range(1, 4)]
        WB[c, d, block] = WQ[block]
    reduced_sum.add(0)
    placed_gather.forward(far_mid, 0)
    reduced_sum.add(1)
    ws_cp = [send(WB.at[c, d], WB.at[c, d], d, sib)]
    for k in range(1, 4):
        for n in range(4):
            wb_cp[3 * n + k - 1].wait_recv()
        quarter = (d + 4 - k) % 4
        ws_cp.append(send(WB.at[c, quarter], WB.at[c, quarter], d, sib))
    for cp in ws_cp:
        cp.wait_recv()

    def spread_out(lo, hi):
        for cc in range(2):
            for zz in range(4):
                rows = slice(32 * (2 * zz + cc), 32 * (2 * zz + cc + 1))
                for dd in range(lo // 896, (hi + 895) // 896):
                    x, y = max(lo, 896 * dd), min(hi, 896 * (dd + 1))
                    WF[rows, x:y] = WB[cc, dd, zz, :, x - 896 * dd : y - 896 * dd]

    spread_out(0, 2304)
    spread_out(3328, 3456)
    lane = lax.broadcasted_iota(jnp.int32, (8, 128), 1)
    row = lax.broadcasted_iota(jnp.int32, (8, 128), 0)
    pick = jnp.where((lane >= 3 * row) & (lane < 3 * row + 3) & (row < 2), 1.0, 0.0).astype(bf16)
    gains = mm(pick, WF[:, 3328:3456], 1, 1)
    gm, gi = gains[0:1], gains[1:2]

    for cp in st_cp:
        cp.wait_recv()
    m_t = SR[:, 0, :]
    q_t = SR[:, 1, :]
    sums = SR[:, 2, 0:256]
    mean = jnp.mean(m_t, axis=0, keepdims=True)
    dm = m_t - mean
    var = (jnp.sum(q_t, axis=0, keepdims=True) + 128.0 * jnp.sum(dm * dm, axis=0, keepdims=True)) * (1.0 / 1024.0)
    rstd = lax.rsqrt(var + epsilon)
    valid = pl.ds(pl.multiple_of(64 * c, 64), 576)
    QF[...] = mm(dm, sums, 0, 0, HIGHEST)
    total = QO[...] + QF[valid, :]
    QF[...] = mm(jnp.broadcast_to(rstd, (8, 640)), jnp.full((8, 256), 0.125, f32), 0, 0, HIGHEST)
    scale = QF[valid, :]
    total = reduced_sum.result(total)
    RED[...] = jnp.zeros((24, 32, 256), f32)
    RED[:, 0:24, :] = (total * scale).reshape(24, 24, 256)

    xm, rm = norm_rows(RED[...].reshape(768, 256))
    zm = xm * gm
    hidden = zm * jax.nn.sigmoid(zm)
    XM[...], ZM[...], RM[...] = xm, zm, jnp.broadcast_to(rm, (768, 128))
    HB[0:32, :] = jnp.zeros((32, 768), bf16)
    HB[800:832, :] = jnp.zeros((32, 768), bf16)
    HB[32:800, 0:256] = pltpu.roll(hidden, 1, 0).astype(bf16)
    HB[32:800, 256:512] = hidden.astype(bf16)
    HB[32:800, 512:768] = pltpu.roll(hidden, 767, 0).astype(bf16)
    conv = mm(HB[0:768, :], WF[:, 0:768], 1, 1)
    conv += mm(HB[32:800, :], WF[:, 768:1536], 1, 1)
    conv += mm(HB[64:832, :], WF[:, 1536:2304], 1, 1)
    xi, ri = norm_rows(conv)
    zi = xi * gi
    activated = (zi * jax.nn.sigmoid(zi)).astype(bf16)
    XI[...], ZI[...], RI[...] = xi, zi, jnp.broadcast_to(ri, (768, 128))
    pool = pool_wide()
    ACT[t] = mm(pool, activated, 1, 0).astype(bf16)
    a_cp = [send(ACT.at[t], ACT.at[t], d, zpeer(k)) for k in range(1, 4)]
    as_cp = [send(ACT.at[t], ACT.at[t], d, sib)]

    placed_gather.forward(far_end, 0)
    for cp in operand_cp:
        cp.wait()
    spread_out(2304, 3328)
    MT[...] = mm(readout_weight[...], WF[:, 2304:3328], 1, 1).astype(bf16)
    for n, q in enumerate(blocks):
        if n == 0:
            placed_gather.pass_on(1)
            placed_gather.pass_on(2)
        if n == 3:
            for k in range(1, 4):
                a_cp[k - 1].wait_recv()
                slot = 2 * ((z + 4 - k) % 4) + c
                as_cp.append(send(ACT.at[slot], ACT.at[slot], d, sib))
            placed_gather.pass_on(3)
        placed_gather.ready(n)
        both = jnp.concatenate([PP[2 * q], PP[2 * q + 1]], axis=1)
        part = mm(readout_weight[:, pl.ds(pl.multiple_of(256 * q, 256), 256)], both, 1, 1)
        if n == 0:
            BEF[...] = part
        else:
            BEF[...] += part

    for cp in as_cp:
        cp.wait_recv()
    for n in range(8):
        ACL[n] = (ACT[n].astype(f32) * slot_live[n].astype(f32)).astype(bf16)
    act_live = ACL[...].reshape(1152, 256)
    BEF[...] += mm(MT[...], act_live, 1, 1)

    @pl.loop(0, 16)
    def _(u):
        rows = pl.ds(pl.multiple_of(32 * u, 32), 32)
        b = BEF[rows, :]
        bell = jnp.exp(-0.5 * b * b)
        density = bell * 0.3989422804014327
        u = 1.0 / (1.0 + 0.23164189 * jnp.abs(b))
        beyond = u * (0.127414796 + u * (-0.142248368 + u * (0.7107068705 + u * (-0.7265760135 + u * 0.5307027145)))) * bell
        below = jnp.where(b >= 0.0, 1.0 - beyond, beyond)
        RO[rows, :] = (b * below).astype(bf16)
        GBT[rows, :] = (cotangent[rows, :].astype(f32) * (below + b * density)).astype(bf16)

    store(RO, readout_o)
    GBR[...] = jnp.transpose(GBT[...])
    terms = mm(GBR[...], MT[...], 1, 0).astype(bf16).reshape(8, 144, 256)
    for n in range(8):
        AT[n % 2, n // 2] = terms[n]
    at_cp = send(AT.at[1 - c], AR, d, sib)
    pooled_sum = Summed(ES, ER)
    te_cp = []

    def pooled_block(n):
        te_cp[n].wait_recv()
        ES[n] = (TE[c, order[n]].astype(f32) + TR[order[n]].astype(f32)).astype(bf16)
        if n < 2:
            pooled_sum.start(n)

    for n, q in enumerate((*order, z)):
        block = mm(GBR[...], readout_weight[:, pl.ds(pl.multiple_of(256 * q, 256), 256)], 1, 0).astype(bf16)
        TE[0, q] = block[:, 0:128]
        TE[1, q] = block[:, 128:256]
        te_cp.append(send(TE.at[1 - c, q], TR.at[q], d, sib))
        if n == 0:
            at_cp.wait_recv()
            az_cp = []
            for k in (1, 2, 3):
                p = (z + k) % 4
                AS[k - 1] = (AT[c, p].astype(f32) + AR[p].astype(f32)).astype(bf16)
                az_cp.append(send(AS.at[k - 1], AZ.at[k - 1], d, zpeer(k)))
            grad_act = AT[c, z].astype(f32) + AR[z].astype(f32)
        else:
            pooled_block(n - 1)
    te_cp[3].wait_recv()
    GP[...] = TE[c, z].astype(f32) + TR[z].astype(f32)
    for q in range(4):
        both = jnp.concatenate([PP[2 * q], PP[2 * q + 1]], axis=1).astype(f32)
        POOLED[:, 256 * q : 256 * (q + 1)] = (both + mm(act_live, WF[:, 2304 + 256 * q : 2560 + 256 * q], 1, 0)).astype(bf16)
    for q in range(4):
        GR[q] = mm(GBT[128 * q : 128 * (q + 1), :], POOLED[...], 1, 0).astype(bf16)
    gr_cp = [send(GR.at[(d + k) % 4], GRR.at[d], dpeer(k), t) for k in range(1, 4)]
    GRR[d] = GR[d]

    for cp in az_cp:
        cp.wait_recv()
    for k in range(3):
        grad_act += AZ[k].astype(f32)
    pooled_sum.add(0)
    high, low = split(grad_act * slot_live[t].astype(f32))
    grad_rows = mm(pool, high, 0, 0) + mm(pool, low, 0, 0)
    zi = ZI[...]
    gate = jax.nn.sigmoid(zi)
    dy = grad_rows * (gate * (1.0 + zi * (1.0 - gate)))
    xi = XI[...]
    dyx_inner = dy * xi
    gc = norm_rows_back(dy * gi, xi, RI[:, 0:1]).astype(bf16)
    GB[0:32, :] = jnp.zeros((32, 256), bf16)
    GB[800:832, :] = jnp.zeros((32, 256), bf16)
    GB[32:800, :] = gc
    back = mm(GB[64:832, :], WF[:, 0:768], 1, 0)
    back += mm(GB[32:800, :], WF[:, 768:1536], 1, 0)
    back += mm(GB[0:768, :], WF[:, 1536:2304], 1, 0)
    grad_hidden = pltpu.roll(back[:, 0:256], 767, 0) + back[:, 256:512] + pltpu.roll(back[:, 512:768], 1, 0)
    zm = ZM[...]
    gate = jax.nn.sigmoid(zm)
    inside = (lax.broadcasted_iota(jnp.int32, (768, 256), 0) & 31) < 24
    dy = jnp.where(inside, grad_hidden * (gate * (1.0 + zm * (1.0 - gate))), 0.0)
    xm = XM[...]
    dyx_middle = dy * xm
    gr = norm_rows_back(dy * gm, xm, RM[:, 0:1]).reshape(24, 32, 256)[:, 0:24, :].reshape(576, 256).astype(bf16)
    GA[t] = gr
    wg = jnp.sum(sums, axis=0, keepdims=True)
    grad_rounded = gr.astype(f32)
    s1 = jnp.sum(grad_rounded * wg, axis=1, keepdims=True)
    s2 = jnp.sum(grad_rounded * RED[:, 0:24, :].reshape(576, 256), axis=1, keepdims=True)
    lane = lax.broadcasted_iota(jnp.int32, (576, 128), 1)
    RSC[0:64, :] = jnp.zeros((64, 128), f32)
    RSC[576:640, :] = jnp.zeros((64, 128), f32)
    RSC[valid, :] = jnp.where(lane == 0, s1, s2) * (1.0 / 1024.0)
    row_sums = jnp.transpose(RSC[...])
    RS[t, 0:1, :] = mean
    RS[t, 1:2, :] = rstd
    RS[t, 2:4, :] = row_sums[0:2]
    rs_cp = [send(RS.at[t], RS.at[t], d, (t + k) % 8) for k in range(1, 8)]
    grad_gather = Gather(GA, 4)
    grad_gather.start(far_mid)
    grad_gather.start(partner)
    pooled_sum.start(2)
    grad_gather.own()
    pooled_sum.add(1)

    for cp in gr_cp:
        cp.wait_recv()
    total = GRR[0].astype(f32)
    for n in range(1, 4):
        total += GRR[n].astype(f32)
    GRF[d] = total.astype(bf16)
    grf_cp = [send(GRF.at[d], GRF.at[d], dpeer(k), t) for k in range(1, 4)]

    def put(lo, value):
        value = value.astype(bf16)
        for n in range(8):
            CG[n % 2, n // 2, :, lo : lo + value.shape[1]] = value[32 * n : 32 * (n + 1)]

    for a in range(3):
        put(768 * a, mm(gc, HB[32 * a : 32 * a + 768, :], 0, 0))
    ones = jnp.ones((768, 128), bf16)
    for lo, value in ((2304, dyx_inner), (2432, dyx_middle)):
        high, low = split(value)
        put(lo, mm(high, ones, 0, 0) + mm(low, ones, 0, 0))
    cg_cp = send(CG.at[1 - c], CGR, d, sib)

    cg_cp.wait_recv()
    CGS[...] = (CG[c].astype(f32) + CGR[...].astype(f32)).astype(bf16)
    cgd_cp = []
    for k in range(1, 4):
        dd = dpeer(k)
        cgd_cp.append(send(CGS.at[:, :, pl.ds(pl.multiple_of(640 * dd, 128), 640)], CGD.at[d], dd, t))
    CGD[d] = CGS[:, :, pl.ds(pl.multiple_of(640 * d, 128), 640)]

    for h in range(4):
        grad_gather.forward(far_mid, h)
    def turn(n):
        for k in range(1, 8):
            s = (t + k) % 8
            yield send(FT.at[n, pl.ds(pl.multiple_of(32 * s, 32), 32)], TA.at[n, d, t], d, s)
        TA[n, d, t] = FT[n, pl.ds(pl.multiple_of(32 * t, 32), 32), :]

    for cp in rs_cp:
        cp.wait_recv()
    w_own = WC[pl.ds(pl.multiple_of(128 * c, 128), 128), :]
    lane = lax.broadcasted_iota(jnp.int32, (4, 128), 1)
    gain_sum = jnp.zeros((128, 1), f32)
    grad_reduce = jnp.zeros((128, 256), f32)
    for n, p in enumerate(blocks):
        if n == 0:
            grad_gather.pass_on(1)
        if n == 1:
            for h in range(4):
                grad_gather.forward(far_end, h)
            grad_gather.pass_on(2)
            gp = pooled_sum.result(GP[...])
            gp_high, gp_low = split(gp)
            FT[0] = mm(act_live, gp_high, 0, 0).astype(bf16)
            turn_cp = list(turn(0))
            for m in range(4):
                cells = slice(288 * m, 288 * (m + 1))
                SP[:, 1152 * m : 1152 * (m + 1)] = mm(gp_high[cells], POOL[...], 0, 0) + mm(gp_low[cells], POOL[...], 0, 0)
            for cp in cgd_cp:
                cp.wait_recv()
            total = CGD[0].astype(f32)
            for m in range(1, 4):
                total += CGD[m].astype(f32)
            CGT[...] = total.astype(bf16)
            cgz_cp = [send(CGT.at[(z + k) % 4], CGZ.at[z], d, zpeer(k)) for k in range(1, 4)]
            CGZ[z] = CGT[z]
        if n == 3:
            for cp in turn_cp[0:7]:
                cp.wait_recv()
            ta_cp = [send(TA.at[0, d], TA.at[0, d], dpeer(k), t) for k in range(1, 4)]
            for cp in cgz_cp:
                cp.wait_recv()
            total = CGZ[0].astype(f32)
            for m in range(1, 4):
                total += CGZ[m].astype(f32)
            CGF[d] = total.astype(bf16)
            cgf_cp = [send(CGF.at[d], CGF.at[d], dpeer(k), t) for k in range(1, 4)]
            grad_gather.pass_on(3)
        grad_gather.ready(n)
        cols = pl.ds(pl.multiple_of(1152 * p, 128), 1152)
        even, odd = RS[2 * p], RS[2 * p + 1]
        stats = jnp.concatenate([even[:, 0:512], jnp.where(lane < 64, even[:, 512:640], odd[:, 0:128]), odd[:, 128:640]], axis=1)
        g = GA[pl.ds(2 * p, 2)].reshape(1152, 256)
        xhat = (PLC[:, cols] - stats[0:1]) * stats[1:2]
        grad_reduce += mm((xhat * go).astype(bf16), g, 1, 0)
        if n == 3:
            FT[1] = jnp.transpose(grad_reduce).astype(bf16)
            turn_cp += list(turn(1))
        gn = mm(w_own, g, 1, 1)
        gain_sum += jnp.sum(gn * xhat, axis=1, keepdims=True)
        GF[:, cols] = stats[1:2] * (gn * go - stats[2:3] - xhat * stats[3:4])
    place_sum = jnp.zeros((128, 1152), f32)
    for p in range(4):
        cols = slice(1152 * p, 1152 * (p + 1))
        out = GF[:, cols] + SP[:, cols]
        GF[:, cols] = out
        store(GF.at[:, cols], gfeat_o.at[:, cols])
        place_sum += out
    odd = pltpu.roll(place_sum, 576, 1)
    lane = lax.broadcasted_iota(jnp.int32, (128, 640), 1)
    place = jnp.where(lane < 576, place_sum[:, 0:640] + odd[:, 0:640], jnp.broadcast_to(gain_sum, (128, 640))).astype(bf16)
    for q in range(4):
        PM[q] = place[32 * q : 32 * (q + 1)]
    pm_cp = [send(PM.at[dpeer(k)], PR.at[d], dpeer(k), t) for k in range(1, 4)]
    PR[d] = PM[d]

    for cp in turn_cp[7:14]:
        cp.wait_recv()
    ta_cp += [send(TA.at[1, d], TA.at[1, d], dpeer(k), t) for k in range(1, 4)]
    for cp in pm_cp:
        cp.wait_recv()
    total = PR[0].astype(f32)
    for n in range(1, 4):
        total += PR[n].astype(f32)
    PF[d] = total.astype(bf16)
    pf_cp = [send(PF.at[d], PF.at[d], dpeer(k), t) for k in range(1, 4)]
    for cp in grf_cp:
        cp.wait_recv()
    for q in range(4):
        store(GRF.at[q], gread_o.at[pl.ds(128 * q, 128)])
    for cp in cgf_cp:
        cp.wait_recv()
    for q in range(4):
        gconv_o[:, 640 * q : 640 * (q + 1)] = CGF[q]
    for cp in ta_cp:
        cp.wait_recv()
    for n, out in enumerate((gexp_o, gred_o)):
        for s in range(8):
            total = TA[n, 0, s].astype(f32)
            for m in range(1, 4):
                total += TA[n, m, s].astype(f32)
            out[:, 128 * s : 128 * (s + 1)] = total
    for cp in pf_cp:
        cp.wait_recv()
    gpos_o[...] = jnp.transpose(PF[...].reshape(128, 640).astype(f32))
    for cp in result_cp:
        cp.wait()
    for cp in pending:
        cp.wait_send()
    placed_gather.drain()
    grad_gather.drain()


SCRATCH = (
    ("features", (128, 4608), bf16), ("position", (576, 128), f32), ("conv_weight", (9, 32, 256), bf16), ("expand_weight", (32, 1024), bf16), ("readout_weight", (512, 1024), bf16), ("cotangent", (512, 1152), bf16), ("RO", (512, 1152), bf16), ("GF", (128, 4608), f32), ("SP", (128, 4608), f32), ("WT", (256, 256), bf16), ("WC", (256, 256), bf16), ("CB", (32, 3584), bf16),
    ("WQ", (4, 32, 896), bf16), ("WB", (2, 4, 4, 32, 896), bf16), ("WF", (256, 3584), bf16), ("MT", (512, 256), bf16),
    ("POOL", (288, 1152), bf16), ("PLC", (128, 4608), f32), ("XW", (2, 4, 128, 640), bf16), ("XK", (4, 256, 640), bf16),
    ("ST", (8, 4, 640), f32), ("SR", (8, 4, 640), f32), ("QF", (640, 256), f32), ("QS", (3, 576, 256), bf16),
    ("QO", (576, 256), f32), ("QR", (4, 576, 256), bf16), ("RED", (24, 32, 256), f32), ("HB", (832, 768), bf16),
    ("GB", (832, 256), bf16), ("XM", (768, 256), f32), ("ZM", (768, 256), f32), ("RM", (768, 128), f32),
    ("XI", (768, 256), f32), ("ZI", (768, 256), f32), ("RI", (768, 128), f32), ("ACT", (8, 144, 256), bf16), ("ACL", (8, 144, 256), bf16),
    ("PP", (8, 1152, 128), bf16), ("POOLED", (1152, 1024), bf16), ("BEF", (512, 1152), f32), ("GBT", (512, 1152), bf16), ("GBR", (1152, 512), bf16),
    ("TE", (2, 4, 1152, 128), bf16), ("TR", (4, 1152, 128), bf16), ("ES", (3, 1152, 128), bf16), ("ER", (4, 1152, 128), bf16),
    ("GP", (1152, 128), f32), ("AT", (2, 4, 144, 256), bf16), ("AR", (4, 144, 256), bf16), ("AS", (3, 144, 256), bf16),
    ("AZ", (3, 144, 256), bf16), ("RSC", (640, 128), f32), ("GA", (8, 576, 256), bf16), ("RS", (8, 4, 640), f32),
    ("FT", (2, 256, 128), bf16), ("TA", (2, 4, 8, 32, 128), bf16), ("PM", (4, 32, 640), bf16),
    ("PR", (4, 32, 640), bf16), ("PF", (4, 32, 640), bf16),
    ("CG", (2, 4, 32, 2560), bf16), ("CGR", (4, 32, 2560), bf16), ("CGS", (4, 32, 2560), bf16), ("CGD", (4, 4, 32, 640), bf16),
    ("CGT", (4, 32, 640), bf16), ("CGZ", (4, 32, 640), bf16), ("CGF", (4, 32, 640), bf16), ("GR", (4, 128, 1024), bf16), ("GRR", (4, 128, 1024), bf16),
    ("GRF", (4, 128, 1024), bf16),
)


def finish(
    readout, gfeat, gpos, gexp, gred, gconv, gread, readout_o, gfeat_o, gpos_o, ggo_o, gred_o, ggm_o, gconv_o, ggi_o, gexp_o, gread_o,
    RO, GF, GB, GC, GR, GP, GQ, GE, GD, sem,
):
    copies = []

    def copy(src, dst):
        cp = pltpu.make_async_copy(src, dst, sem.at[len(copies)])
        copies.append(cp)
        cp.start()
        return cp

    loads = [copy(gread.at[pl.ds(256 * p, 256)], GB.at[pl.ds(256 * p, 256)]) for p in range(2)]
    loads += [copy(gfeat.at[pl.ds(32 * p, 32)], GF.at[pl.ds(32 * p, 32)]) for p in range(4)]
    loads += [copy(readout, RO), copy(gconv, GC), copy(gpos, GP), copy(gexp, GE), copy(gred, GD)]
    stores = []
    for p in range(2):
        rows = pl.ds(256 * p, 256)
        loads[p].wait()
        GR[rows, :] = GB[rows, :].astype(f32)
        stores.append(copy(GR.at[rows], gread_o.at[rows]))
    for p in range(4):
        rows = pl.ds(32 * p, 32)
        loads[2 + p].wait()
        stores.append(copy(GF.at[rows], gfeat_o.at[rows]))
    loads[6].wait()
    stores.append(copy(RO, readout_o))
    loads[7].wait()
    for n in range(9):
        GQ[n] = GC[:, 256 * n : 256 * (n + 1)].astype(f32)
    stores.append(copy(GQ, gconv_o))
    first = (lax.broadcasted_iota(jnp.int32, (8, 128), 1) == 0).astype(f32).astype(bf16)
    ggi_o[...] = mm(first, GC[:, 2304:2432], 1, 1)[0:1]
    ggm_o[...] = mm(first, GC[:, 2432:2560], 1, 1)[0:1]
    loads[8].wait()
    stores.append(copy(GP.at[pl.ds(0, 576)], gpos_o))
    ggo_o[...] = GP[576:577, :]
    loads[9].wait()
    stores.append(copy(GE, gexp_o))
    loads[10].wait()
    stores.append(copy(GD, gred_o))
    for cp in stores:
        cp.wait()


def local_by_image(features, slot_live, position, gain_outer, reduce_weight, gain_middle, conv_weight, gain_inner, expand_weight, readout_weight, cotangent):
    vmem = pl.BlockSpec(memory_space=pltpu.VMEM)
    smem = pl.BlockSpec(memory_space=pltpu.SMEM)
    hbm = pl.BlockSpec(memory_space=pl.ANY)

    def shapes(*pairs):
        return tuple(jax.ShapeDtypeStruct(shape, dtype) for shape, dtype in pairs)

    parts = pl.pallas_call(
        kernel,
        out_shape=shapes(
            ((512, 1152), bf16), ((128, 4608), f32), ((640, 128), f32), ((32, 1024), f32), ((32, 1024), f32), ((32, 2560), bf16), ((512, 1024), bf16)
        ),
        in_specs=[hbm, smem, hbm, vmem, vmem, vmem, hbm, vmem, hbm, hbm, hbm],
        out_specs=[hbm, hbm, vmem, vmem, vmem, vmem, hbm],
        scratch_shapes=[pltpu.VMEM(shape, dtype) for _, shape, dtype in SCRATCH]
        + [pltpu.SemaphoreType.DMA((COPIES,)), pltpu.SemaphoreType.DMA((COPIES,)), pltpu.SemaphoreType.DMA((24,))],
        compiler_params=pltpu.CompilerParams(collective_id=0, has_side_effects=True, vmem_limit_bytes=60 * 2**20),
    )(
        features, slot_live, position.reshape(576, 128), gain_outer.reshape(1, 128), reduce_weight.T, gain_middle.reshape(1, 32),
        conv_weight.transpose(0, 1, 3, 2).reshape(9, 32, 256), gain_inner.reshape(1, 32), expand_weight, readout_weight, cotangent,
    )
    readout, gfeat, gpos, ggo, gred, ggm, gconv, ggi, gexp, gread = pl.pallas_call(
        finish,
        out_shape=shapes(
            ((512, 1152), bf16), ((128, 4608), f32), ((576, 128), f32), ((1, 128), f32), ((32, 1024), f32), ((1, 32), f32),
            ((9, 32, 256), f32), ((1, 32), f32), ((32, 1024), f32), ((512, 1024), f32),
        ),
        in_specs=[hbm] * 7,
        out_specs=[hbm, hbm, hbm, vmem, hbm, vmem, hbm, vmem, hbm, hbm],
        scratch_shapes=[
            pltpu.VMEM((512, 1152), bf16), pltpu.VMEM((128, 4608), f32), pltpu.VMEM((512, 1024), bf16), pltpu.VMEM((32, 2560), bf16),
            pltpu.VMEM((512, 1024), f32), pltpu.VMEM((640, 128), f32), pltpu.VMEM((9, 32, 256), f32), pltpu.VMEM((32, 1024), f32),
            pltpu.VMEM((32, 1024), f32), pltpu.SemaphoreType.DMA((24,)),
        ],
        compiler_params=pltpu.CompilerParams(vmem_limit_bytes=60 * 2**20),
    )(*parts)
    return (
        readout, gfeat, gpos.reshape(24, 24, 128), ggo.reshape(128), gred.T, ggm.reshape(32),
        gconv.reshape(3, 3, 32, 256).transpose(0, 1, 3, 2), ggi.reshape(32), gexp, gread,
    )


def row_totals(leading, trailing):
    return lax.psum((leading, trailing), "tensor")


def norm_forward(values, norm_gain, breadth):
    totals, squares = row_totals(jnp.sum(values, axis=1), jnp.sum(values * values, axis=1))
    center = totals / breadth
    spread = squares / breadth - center * center
    scaled = lax.rsqrt(spread + epsilon)[:, None]
    normed = (values - center[:, None]) * scaled
    return (normed, scaled, normed * norm_gain)


def norm_backward(grad_out, normed, scaled, norm_gain, breadth):
    grad_normed = grad_out * norm_gain
    gain_grad = jnp.sum(grad_out * normed, axis=0)
    leading, trailing = row_totals(
        jnp.sum(grad_normed, axis=1), jnp.sum(grad_normed * normed, axis=1)
    )
    grad_in = scaled * (
        grad_normed - leading[:, None] / breadth - normed * (trailing[:, None] / breadth)
    )
    return (grad_in, gain_grad)


def silu_grad(inputs):
    gate_value = jax.nn.sigmoid(inputs)
    return gate_value * (1.0 + inputs * (1.0 - gate_value))


def gelu_grad(inputs):
    below = 0.5 * (1.0 + lax.erf(inputs * 0.7071067811865476))
    density = jnp.exp(-0.5 * inputs * inputs) * 0.3989422804014327
    return below + inputs * density


def contract_rows(left_side, right_side):
    return lax.dot_general(
        left_side, right_side, (((0,), (0,)), ((), ())), preferred_element_type=jnp.float32
    )


def window_of(padded, shift_down, shift_across, grid_side):
    images = padded.shape[0]
    breadth = padded.shape[3]
    return padded[
        :, shift_down : shift_down + grid_side, shift_across : shift_across + grid_side, :
    ].reshape(images * grid_side * grid_side, breadth)


def local_by_hidden(
    features,
    slot_live,
    position,
    gain_outer,
    reduce_weight,
    gain_middle,
    conv_weight,
    gain_inner,
    expand_weight,
    readout_weight,
    cotangent,
):
    grid_side = position.shape[0]
    half_side = grid_side // 2
    channel_share = features.shape[0]
    row_count = features.shape[1]
    images = row_count // (grid_side * grid_side)
    tensor_size = lax.axis_size("tensor")
    channels = channel_share * tensor_size
    hidden_share = reduce_weight.shape[1]
    hidden_width = hidden_share * tensor_size
    pooled_count = images * half_side * half_side
    placed = (
        features.T.astype(jnp.float32).reshape(images, grid_side * grid_side, channel_share)
        + position.reshape(1, grid_side * grid_side, channel_share)
    ).reshape(row_count, channel_share)
    live_rows = jnp.repeat(slot_live.astype(jnp.float32), grid_side * grid_side)[:, None]
    normed_outer, scaled_outer, shaped_outer = norm_forward(placed, gain_outer, channels)
    reduce_in = shaped_outer.astype(jnp.bfloat16)
    reduce_full = lax.all_gather(reduce_in, "tensor", axis=1, tiled=True)
    reduced = jnp.dot(reduce_full, reduce_weight, preferred_element_type=jnp.float32)
    normed_middle, scaled_middle, shaped_middle = norm_forward(reduced, gain_middle, hidden_width)
    hidden = jax.nn.silu(shaped_middle).astype(jnp.bfloat16)
    hidden_full = lax.all_gather(hidden, "tensor", axis=1, tiled=True)
    padded_hidden = jnp.pad(
        hidden_full.reshape(images, grid_side, grid_side, hidden_width),
        ((0, 0), (1, 1), (1, 1), (0, 0)),
    )
    convolved = jnp.zeros((row_count, hidden_share), jnp.float32)
    for offset_tap in range(9):
        shift_down = offset_tap // 3
        shift_across = offset_tap % 3
        convolved = convolved + jnp.dot(
            window_of(padded_hidden, shift_down, shift_across, grid_side),
            conv_weight[shift_down, shift_across],
            preferred_element_type=jnp.float32,
        )
    normed_inner, scaled_inner, shaped_inner = norm_forward(convolved, gain_inner, hidden_width)
    activated = jax.nn.silu(shaped_inner).astype(jnp.bfloat16)
    expand_terms = jnp.dot(activated, expand_weight, preferred_element_type=jnp.float32)
    expanded = lax.psum_scatter(expand_terms, "tensor", scatter_dimension=1, tiled=True)
    mixed = placed + live_rows * expanded
    pooled = jnp.mean(mixed.reshape(images, half_side, 2, half_side, 2, channel_share), axis=(2, 4))
    pooled_low = pooled.reshape(pooled_count, channel_share).astype(jnp.bfloat16)
    pooled_full = lax.all_gather(pooled_low, "tensor", axis=1, tiled=True)
    before = lax.dot_general(
        pooled_full, readout_weight, (((1,), (1,)), ((), ())), preferred_element_type=jnp.float32
    )
    readout = jax.nn.gelu(before, approximate=False).astype(jnp.bfloat16).T
    grad_before = (cotangent.T.astype(jnp.float32) * gelu_grad(before)).astype(jnp.bfloat16)
    grad_readout = contract_rows(grad_before, pooled_full)
    pooled_terms = jnp.dot(grad_before, readout_weight, preferred_element_type=jnp.float32)
    grad_pooled = lax.psum_scatter(pooled_terms, "tensor", scatter_dimension=1, tiled=True)
    spread_grad = jnp.broadcast_to(
        (0.25 * grad_pooled).reshape(images, half_side, 1, half_side, 1, channel_share),
        (images, half_side, 2, half_side, 2, channel_share),
    )
    grad_mixed = spread_grad.reshape(row_count, channel_share)
    grad_branch = (live_rows * grad_mixed).astype(jnp.bfloat16)
    grad_full = lax.all_gather(grad_branch, "tensor", axis=1, tiled=True)
    grad_expand = contract_rows(activated, grad_full)
    grad_activated = jnp.dot(grad_full, expand_weight.T, preferred_element_type=jnp.float32)
    grad_convolved, grad_gain_inner = norm_backward(
        grad_activated * silu_grad(shaped_inner),
        normed_inner,
        scaled_inner,
        gain_inner,
        hidden_width,
    )
    grad_conv_low = grad_convolved.astype(jnp.bfloat16)
    tap_grads = []
    grad_padded = jnp.zeros((images, grid_side + 2, grid_side + 2, hidden_width), jnp.float32)
    for offset_tap in range(9):
        shift_down = offset_tap // 3
        shift_across = offset_tap % 3
        tap_grads.append(
            contract_rows(
                window_of(padded_hidden, shift_down, shift_across, grid_side), grad_conv_low
            )
        )
        tap_back = jnp.dot(
            grad_conv_low,
            conv_weight[shift_down, shift_across].T,
            preferred_element_type=jnp.float32,
        )
        grad_padded = grad_padded + jnp.pad(
            tap_back.reshape(images, grid_side, grid_side, hidden_width),
            ((0, 0), (shift_down, 2 - shift_down), (shift_across, 2 - shift_across), (0, 0)),
        )
    grad_conv = jnp.stack(tap_grads, axis=0).reshape(conv_weight.shape)
    grad_window = grad_padded[:, 1 : grid_side + 1, 1 : grid_side + 1, :].reshape(
        row_count, hidden_width
    )
    grad_hidden = lax.psum_scatter(grad_window, "tensor", scatter_dimension=1, tiled=True)
    grad_reduced, grad_gain_middle = norm_backward(
        grad_hidden * silu_grad(shaped_middle),
        normed_middle,
        scaled_middle,
        gain_middle,
        hidden_width,
    )
    grad_reduced_low = grad_reduced.astype(jnp.bfloat16)
    grad_reduce = contract_rows(reduce_full, grad_reduced_low)
    outer_terms = jnp.dot(grad_reduced_low, reduce_weight.T, preferred_element_type=jnp.float32)
    grad_shaped_outer = lax.psum_scatter(outer_terms, "tensor", scatter_dimension=1, tiled=True)
    grad_inputs, grad_gain_outer = norm_backward(
        grad_shaped_outer, normed_outer, scaled_outer, gain_outer, channels
    )
    grad_rows = grad_mixed + grad_inputs
    grad_place = jnp.sum(grad_rows.reshape(images, grid_side, grid_side, channel_share), axis=0)
    grad_total = grad_rows.T
    summed = (
        lax.psum(grad_place.astype(jnp.bfloat16), "dp").astype(jnp.float32),
        lax.psum(grad_gain_outer.astype(jnp.bfloat16), "dp").astype(jnp.float32),
        lax.psum(grad_reduce.astype(jnp.bfloat16), "dp").astype(jnp.float32),
        lax.psum(grad_gain_middle.astype(jnp.bfloat16), "dp").astype(jnp.float32),
        lax.psum(grad_conv.astype(jnp.bfloat16), "dp").astype(jnp.float32),
        lax.psum(grad_gain_inner.astype(jnp.bfloat16), "dp").astype(jnp.float32),
        lax.psum(grad_expand.astype(jnp.bfloat16), "dp").astype(jnp.float32),
        lax.psum(grad_readout.astype(jnp.bfloat16), "dp").astype(jnp.float32),
    )
    return (
        readout,
        grad_total,
        summed[0],
        summed[1],
        summed[2],
        summed[3],
        summed[4],
        summed[5],
        summed[6],
        summed[7],
    )


def solution(mesh):
    parts, groups = mesh.shape["tensor"], mesh.shape["dp"]
    specs = (P("tensor", "dp"), P("dp"), P(None, None, "tensor"), P("tensor"), P(None, "tensor"), P("tensor"), P(None, None, None, "tensor"), P("tensor"), P("tensor", None), P("tensor", None), P("tensor", "dp"))

    def whole(*arrays):
        by_image = (parts, groups) == (8, 4) and arrays[1].shape[0] == parts * groups
        return jax.shard_map(
            local_by_image if by_image else local_by_hidden, mesh=mesh, in_specs=specs,
            out_specs=(P("tensor", "dp"), P("tensor", "dp"), *specs[2:10]), check_vma=False,
        )(*arrays)

    return whole
```

```python
import jax
import jax.numpy as jnp
from jax import lax
from jax.experimental import pallas as pl
from jax.experimental.pallas import tpu as pltpu
from jax.sharding import PartitionSpec as P

epsilon = 1e-05
bf16 = jnp.bfloat16
f32 = jnp.float32
COPIES = 160

MESH = pl.DeviceIdType.MESH
HIGHEST = lax.Precision.HIGHEST


def mm(a, b, ca, cb, precision=None):
    return lax.dot_general(a, b, (((ca,), (cb,)), ((), ())), precision=precision, preferred_element_type=f32)


def split(x):
    high = x.astype(bf16)
    return high, (x - high.astype(f32)).astype(bf16)


def eye(n, dtype=bf16):
    return (lax.broadcasted_iota(jnp.int32, (n, n), 0) == lax.broadcasted_iota(jnp.int32, (n, n), 1)).astype(f32).astype(dtype)


def pool_wide():
    spot = lax.broadcasted_iota(jnp.int32, (144, 768), 1)
    cell = lax.broadcasted_iota(jnp.int32, (144, 768), 0)
    i, j = spot >> 5, spot & 31
    return jnp.where(((i >> 1) * 12 + (j >> 1) == cell) & (j < 24), 0.25, 0.0).astype(bf16)


def pool_pair():
    spot = lax.broadcasted_iota(jnp.int32, (288, 1152), 1)
    cell = lax.broadcasted_iota(jnp.int32, (288, 1152), 0)
    i = (spot * 2731) >> 16
    j = spot - i * 24
    return jnp.where((i >> 1) * 12 + (j >> 1) == cell, 0.25, 0.0).astype(bf16)


def norm_rows(v):
    s = v - jnp.mean(v, axis=1, keepdims=True)
    r = lax.rsqrt(jnp.mean(s * s, axis=1, keepdims=True) + epsilon)
    return s * r, r


def norm_rows_back(dx, xhat, r):
    return r * (dx - jnp.mean(dx, axis=1, keepdims=True) - xhat * jnp.mean(dx * xhat, axis=1, keepdims=True))


def kernel(
    features_h, slot_live, position_h, gain_outer, reduce_weight, gain_middle, conv_h, gain_inner, expand_h, readout_h, cotangent_h,
    readout_o, gfeat_o, gpos_o, gexp_o, gred_o, gconv_o, gread_o,
    features, position, conv_weight, expand_weight, readout_weight, cotangent, RO, GF, SP, WT, WC, CB, WQ, WB, WF, MT, POOL, PLC, XW, XK, ST, SR, QF, QS, QO, QR, RED, HB, GB,
    XM, ZM, RM, XI, ZI, RI, ACT, ACL, PP, POOLED, BEF, GBT, GBR, TE, TR, ES, ER, GP, AT, AR, AS, AZ,
    RSC, GA, RS, FT, TA, PM, PR, PF, CG, CGR, CGS, CGD, CGT, CGZ, CGF, GR, GRR, GRF, ssem, rsem, lsem,
):
    d = lax.axis_index("dp")
    t = lax.axis_index("tensor")
    z = t // 2
    c = t % 2
    sib = 2 * z + 1 - c
    side = z // 2
    is_mid = ((z + 1) // 2) % 2
    near_end, near_mid, far_end, far_mid = 3 * side, 1 + side, 3 - 3 * side, 2 - side
    partner = z + 1 - 2 * (z % 2)
    sends, arrivals = [0], [0]
    pending = []

    def copy(src, dst, dd, tt, arrival):
        cp = pltpu.make_async_remote_copy(
            src_ref=src, dst_ref=dst, send_sem=ssem.at[sends[0]], recv_sem=rsem.at[arrival], device_id=(dd, tt), device_id_type=MESH
        )
        sends[0] += 1
        return cp

    def take(n):
        arrivals[0] += n
        return arrivals[0] - n

    def send(src, dst, dd, tt):
        cp = copy(src, dst, dd, tt, take(1))
        cp.start()
        pending.append(cp)
        return cp

    class Gather:
        def __init__(self, buf, parts):
            self.buf, self.parts, self.rows = buf, parts, buf.shape[1] // parts
            self.base = take(4 * parts)
            self.forwards = []

        def view(self, zz, h):
            return self.buf.at[2 * zz + c, pl.ds(h * self.rows, self.rows)]

        def to(self, block, zz, h):
            return copy(self.view(block, h), self.view(block, h), d, 2 * zz + c, self.base + 4 * h + block)

        def start(self, zz):
            for h in range(self.parts):
                cp = self.to(z, zz, h)
                cp.start()
                pending.append(cp)

        def own(self):
            self.siblings = [send(self.buf.at[t], self.buf.at[t], d, sib)]

        def arrived(self, block, h):
            view = self.view(block, h)
            pltpu.make_async_remote_copy(
                src_ref=view, dst_ref=view, send_sem=ssem.at[0], recv_sem=rsem.at[self.base + 4 * h + block],
                device_id=(d, sib), device_id_type=MESH,
            ).wait_recv()

        def forward(self, block, h):
            cp = self.to(block, near_end, h)
            self.forwards.append(cp)

            @pl.when(is_mid == 1)
            def _():
                self.arrived(block, h)
                cp.start()

        def pass_on(self, n):
            for h in range(self.parts):
                if n == 3:
                    self.arrived(blocks[n], h)
                else:

                    @pl.when(is_mid == 0)
                    def _(h=h):
                        self.arrived(blocks[n], h)

            slot = self.buf.at[2 * blocks[n] + c]
            self.siblings.append(send(slot, slot, d, sib))

        def ready(self, n):
            self.siblings[n].wait_recv()

        def drain(self):
            @pl.when(is_mid == 1)
            def _():
                for cp in self.forwards:
                    cp.wait_send()

    order = (
        far_end + is_mid * (near_end - far_end),
        far_mid + is_mid * (far_end - far_mid),
        near_mid + is_mid * (far_mid - near_mid),
    )

    blocks = (z, partner + is_mid * (far_mid - partner), far_mid + is_mid * (far_end - far_mid), far_end + is_mid * (partner - far_end))

    class Summed:
        def __init__(self, out, arrive):
            self.out, self.arrive = out, arrive
            self.base = take(4)
            to = (partner, near_mid + is_mid * (far_end - near_mid), near_mid + is_mid * (far_mid - near_mid))
            slot = (2 * is_mid, 1 + 2 * is_mid, 2 + is_mid)
            self.cps = [copy(out.at[n], arrive.at[slot[n]], d, 2 * to[n] + c, self.base + slot[n]) for n in range(3)]
            pending.extend(self.cps)

        def wait(self, n):
            view = self.arrive.at[n]
            pltpu.make_async_remote_copy(
                src_ref=view, dst_ref=view, send_sem=ssem.at[0], recv_sem=rsem.at[self.base + n], device_id=(d, sib), device_id_type=MESH
            ).wait_recv()

        def start(self, n):
            if n == 0:
                self.cps[0].start()
            else:

                @pl.when(is_mid == 0)
                def _():
                    self.cps[n].start()

        def add(self, n):
            @pl.when(is_mid == 1)
            def _():
                self.wait(n)
                self.out[n + 1] = (self.out[n + 1].astype(f32) + self.arrive[n].astype(f32)).astype(bf16)
                self.cps[n + 1].start()

        def result(self, own):
            self.wait(2)
            self.wait(3)
            return own + self.arrive[2].astype(f32) + self.arrive[3].astype(f32)

    def zpeer(k):
        return 2 * ((z + k) % 4) + c

    def dpeer(k):
        return (d + k) % 4

    def load(n, src, dst):
        cp = pltpu.make_async_copy(src, dst, lsem.at[n])
        cp.start()
        return cp

    result_cp = []

    def store(src, dst):
        cp = pltpu.make_async_copy(src, dst, lsem.at[9 + len(result_cp)])
        cp.start()
        result_cp.append(cp)

    barrier = pltpu.get_barrier_semaphore()
    for k in range(1, 8):
        pl.semaphore_signal(barrier, 1, device_id=(d, (t + k) % 8), device_id_type=MESH)
    for k in range(1, 4):
        pl.semaphore_signal(barrier, 1, device_id=(dpeer(k), t), device_id_type=MESH)

    position_cp = load(0, position_h, position)
    feature_cp = []
    for n, p in enumerate((*order, z)):
        cols = pl.ds(pl.multiple_of(1152 * p, 128), 1152)
        feature_cp.append(load(1 + n, features_h.at[:, cols], features.at[:, cols]))
    weight_cp = [load(5, conv_h, conv_weight), load(6, expand_h, expand_weight)]
    operand_cp = [load(7, readout_h, readout_weight), load(8, cotangent_h, cotangent)]
    POOL[...] = pool_pair()
    pl.semaphore_wait(barrier, 10)

    w_cp = []
    for k in range(1, 8):
        s = (t + k) % 8
        w_cp.append(send(reduce_weight.at[:, pl.ds(pl.multiple_of(256 * (s // 2), 256), 256)], WT.at[pl.ds(pl.multiple_of(32 * t, 32), 32)], d, s))
    WT[pl.ds(pl.multiple_of(32 * t, 32), 32), :] = reduce_weight[:, pl.ds(pl.multiple_of(256 * z, 256), 256)]
    position_cp.wait()
    go_rows = jnp.broadcast_to(gain_outer[...], (8, 128))
    eighth = jnp.full((8, 128), 0.125, f32)
    go = mm(go_rows, eighth, 0, 0, HIGHEST)[:, 0:1]
    pos = position[...]
    pos_pair = mm(eye(128, f32), jnp.concatenate([pos, pos], axis=0), 1, 1, HIGHEST)
    x_cp = []
    for n, p in enumerate((*order, z)):
        cols = pl.ds(pl.multiple_of(1152 * p, 128), 1152)
        feature_cp[n].wait()
        x = features[:, cols].astype(f32) + pos_pair
        PLC[:, cols] = x
        m = jnp.mean(x, axis=0, keepdims=True)
        x = x - m
        q = jnp.sum(x * x, axis=0, keepdims=True)
        x = (x * go).astype(bf16)
        for par, lo in ((0, 0), (1, 512)):
            XW[par, p] = x[:, lo : lo + 640]
            ST[2 * p + par, 0:1, :] = m[:, lo : lo + 640]
            ST[2 * p + par, 1:2, :] = q[:, lo : lo + 640]
        x_cp.append(send(XW.at[1 - c, p], XK.at[p, pl.ds(pl.multiple_of(128 * c, 128), 128)], d, sib))
        XK[p, pl.ds(pl.multiple_of(128 * c, 128), 128), :] = XW[c, p]

    for cp in weight_cp:
        cp.wait()
    for n in range(9):
        CB[:, 256 * n : 256 * (n + 1)] = conv_weight[n]
    CB[:, 2304:3328] = expand_weight[...]
    lane = lax.broadcasted_iota(jnp.int32, (32, 128), 1)
    packed = jnp.zeros((32, 128), f32)
    for n, gain in enumerate((gain_middle, gain_inner)):
        column = mm(jnp.broadcast_to(gain[...], (8, 32)), eighth, 0, 0, HIGHEST)
        high, rest = split(column)
        rest = column - high.astype(f32)
        mid, low = split(rest)
        for m, part in enumerate((high, mid, low)):
            packed = jnp.where(lane == 3 * n + m, part.astype(f32), packed)
    CB[:, 3328:3456] = packed.astype(bf16)
    CB[:, 3456:3584] = jnp.zeros((32, 128), bf16)
    quarter = CB.at[:, pl.ds(pl.multiple_of(896 * d, 128), 896)]
    wq_cp = [send(quarter, WQ.at[z], d, zpeer(k)) for k in range(1, 4)]
    WQ[z] = quarter[...]
    WB[c, d, z] = quarter[...]
    wb_cp = [send(WQ.at[z], WB.at[c, d, z], dpeer(k), t) for k in range(1, 4)]

    for p in range(4):
        high, low = split(PLC[:, 1152 * p : 1152 * (p + 1)])
        PP[t, 288 * p : 288 * (p + 1), :] = (mm(POOL[...], high, 1, 1) + mm(POOL[...], low, 1, 1)).astype(bf16)
    placed_gather = Gather(PP, 1)
    for cp in w_cp:
        cp.wait_recv()
    WC[...] = mm(eye(256), WT[...], 1, 1).astype(bf16)
    mine = WC[pl.ds(pl.multiple_of(128 * c, 128), 128), :].astype(f32)
    colsum = mm(go_rows, mine, 1, 0, HIGHEST)[0:1]
    for n in range(8):
        ST[n, 2:3, 0:256] = colsum
    reduced_sum = Summed(QS, QR)
    for n, p in enumerate((*order, z)):
        x_cp[n].wait_recv()
        QF[...] = mm(XK[p], WC[...], 0, 0)
        part = QF[pl.ds(pl.multiple_of(64 * c, 64), 576), :]
        if n == 3:
            QO[...] = part
        else:
            QS[n] = part.astype(bf16)
            reduced_sum.start(n)
        if n == 0:
            st_cp = [send(ST.at[(t + k) % 8], SR.at[t], d, (t + k) % 8) for k in range(1, 8)]
            SR[t] = ST[t]
    placed_gather.start(far_mid)
    placed_gather.start(partner)
    placed_gather.own()


    for n in range(1, 4):
        wq_cp[n - 1].wait_recv()
        block = (z + 4 - n) % 4
        wb_cp += [send(WQ.at[block], WB.at[c, d, block], dpeer(k), t) for k in range(1, 4)]
        WB[c, d, block] = WQ[block]
    reduced_sum.add(0)
    placed_gather.forward(far_mid, 0)
    ws_cp = [send(WB.at[c, d], WB.at[c, d], d, sib)]
    for k in range(1, 4):
        for n in range(4):
            wb_cp[3 * n + k - 1].wait_recv()
        quarter = (d + 4 - k) % 4
        ws_cp.append(send(WB.at[c, quarter], WB.at[c, quarter], d, sib))
    reduced_sum.add(1)
    for cp in ws_cp:
        cp.wait_recv()

    def spread_out(lo, hi):
        for cc in range(2):
            for zz in range(4):
                rows = slice(32 * (2 * zz + cc), 32 * (2 * zz + cc + 1))
                for dd in range(lo // 896, (hi + 895) // 896):
                    x, y = max(lo, 896 * dd), min(hi, 896 * (dd + 1))
                    WF[rows, x:y] = WB[cc, dd, zz, :, x - 896 * dd : y - 896 * dd]

    spread_out(0, 2304)
    spread_out(3328, 3456)
    lane = lax.broadcasted_iota(jnp.int32, (8, 128), 1)
    row = lax.broadcasted_iota(jnp.int32, (8, 128), 0)
    pick = jnp.where((lane >= 3 * row) & (lane < 3 * row + 3) & (row < 2), 1.0, 0.0).astype(bf16)
    gains = mm(pick, WF[:, 3328:3456], 1, 1)
    gm, gi = gains[0:1], gains[1:2]

    for cp in st_cp:
        cp.wait_recv()
    m_t = SR[:, 0, :]
    q_t = SR[:, 1, :]
    sums = SR[:, 2, 0:256]
    mean = jnp.mean(m_t, axis=0, keepdims=True)
    dm = m_t - mean
    var = (jnp.sum(q_t, axis=0, keepdims=True) + 128.0 * jnp.sum(dm * dm, axis=0, keepdims=True)) * (1.0 / 1024.0)
    rstd = lax.rsqrt(var + epsilon)
    valid = pl.ds(pl.multiple_of(64 * c, 64), 576)
    QF[...] = mm(dm, sums, 0, 0, HIGHEST)
    total = QO[...] + QF[valid, :]
    QF[...] = mm(jnp.broadcast_to(rstd, (8, 640)), jnp.full((8, 256), 0.125, f32), 0, 0, HIGHEST)
    scale = QF[valid, :]
    total = reduced_sum.result(total)
    RED[...] = jnp.zeros((24, 32, 256), f32)
    RED[:, 0:24, :] = (total * scale).reshape(24, 24, 256)

    xm, rm = norm_rows(RED[...].reshape(768, 256))
    zm = xm * gm
    hidden = zm * jax.nn.sigmoid(zm)
    XM[...], ZM[...], RM[...] = xm, zm, jnp.broadcast_to(rm, (768, 128))
    HB[0:32, :] = jnp.zeros((32, 768), bf16)
    HB[800:832, :] = jnp.zeros((32, 768), bf16)
    HB[32:800, 0:256] = pltpu.roll(hidden, 1, 0).astype(bf16)
    HB[32:800, 256:512] = hidden.astype(bf16)
    HB[32:800, 512:768] = pltpu.roll(hidden, 767, 0).astype(bf16)
    conv = mm(HB[0:768, :], WF[:, 0:768], 1, 1)
    conv += mm(HB[32:800, :], WF[:, 768:1536], 1, 1)
    conv += mm(HB[64:832, :], WF[:, 1536:2304], 1, 1)
    xi, ri = norm_rows(conv)
    zi = xi * gi
    activated = (zi * jax.nn.sigmoid(zi)).astype(bf16)
    XI[...], ZI[...], RI[...] = xi, zi, jnp.broadcast_to(ri, (768, 128))
    pool = pool_wide()
    ACT[t] = mm(pool, activated, 1, 0).astype(bf16)
    a_cp = [send(ACT.at[t], ACT.at[t], d, zpeer(k)) for k in range(1, 4)]
    as_cp = [send(ACT.at[t], ACT.at[t], d, sib)]

    placed_gather.forward(far_end, 0)
    for cp in operand_cp:
        cp.wait()
    spread_out(2304, 3328)
    MT[...] = mm(readout_weight[...], WF[:, 2304:3328], 1, 1).astype(bf16)
    for n, q in enumerate(blocks):
        if n == 0:
            placed_gather.pass_on(1)
            placed_gather.pass_on(2)
        if n == 3:
            for k in range(1, 4):
                a_cp[k - 1].wait_recv()
                slot = 2 * ((z + 4 - k) % 4) + c
                as_cp.append(send(ACT.at[slot], ACT.at[slot], d, sib))
            placed_gather.pass_on(3)
        placed_gather.ready(n)
        both = jnp.concatenate([PP[2 * q], PP[2 * q + 1]], axis=1)
        part = mm(readout_weight[:, pl.ds(pl.multiple_of(256 * q, 256), 256)], both, 1, 1)
        if n == 0:
            BEF[...] = part
        else:
            BEF[...] += part

    for cp in as_cp:
        cp.wait_recv()
    for n in range(8):
        ACL[n] = (ACT[n].astype(f32) * slot_live[n].astype(f32)).astype(bf16)
    act_live = ACL[...].reshape(1152, 256)
    BEF[...] += mm(MT[...], act_live, 1, 1)

    @pl.loop(0, 16)
    def _(u):
        rows = pl.ds(pl.multiple_of(32 * u, 32), 32)
        b = BEF[rows, :]
        bell = jnp.exp(-0.5 * b * b)
        density = bell * 0.3989422804014327
        u = 1.0 / (1.0 + 0.23164189 * jnp.abs(b))
        beyond = u * (0.127414796 + u * (-0.142248368 + u * (0.7107068705 + u * (-0.7265760135 + u * 0.5307027145)))) * bell
        below = jnp.where(b >= 0.0, 1.0 - beyond, beyond)
        RO[rows, :] = (b * below).astype(bf16)
        GBT[rows, :] = (cotangent[rows, :].astype(f32) * (below + b * density)).astype(bf16)

    store(RO, readout_o)
    GBR[...] = jnp.transpose(GBT[...])
    terms = mm(GBR[...], MT[...], 1, 0).astype(bf16).reshape(8, 144, 256)
    for n in range(8):
        AT[n % 2, n // 2] = terms[n]
    at_cp = send(AT.at[1 - c], AR, d, sib)
    pooled_sum = Summed(ES, ER)
    te_cp = []

    def pooled_block(n):
        te_cp[n].wait_recv()
        ES[n] = (TE[c, order[n]].astype(f32) + TR[order[n]].astype(f32)).astype(bf16)
        if n < 2:
            pooled_sum.start(n)

    for n, q in enumerate((*order, z)):
        block = mm(GBR[...], readout_weight[:, pl.ds(pl.multiple_of(256 * q, 256), 256)], 1, 0).astype(bf16)
        TE[0, q] = block[:, 0:128]
        TE[1, q] = block[:, 128:256]
        te_cp.append(send(TE.at[1 - c, q], TR.at[q], d, sib))
        if n == 0:
            at_cp.wait_recv()
            az_cp = []
            for k in (1, 2, 3):
                p = (z + k) % 4
                AS[k - 1] = (AT[c, p].astype(f32) + AR[p].astype(f32)).astype(bf16)
                az_cp.append(send(AS.at[k - 1], AZ.at[k - 1], d, zpeer(k)))
            grad_act = AT[c, z].astype(f32) + AR[z].astype(f32)
        else:
            pooled_block(n - 1)
    te_cp[3].wait_recv()
    GP[...] = TE[c, z].astype(f32) + TR[z].astype(f32)
    for q in range(4):
        both = jnp.concatenate([PP[2 * q], PP[2 * q + 1]], axis=1).astype(f32)
        POOLED[:, 256 * q : 256 * (q + 1)] = (both + mm(act_live, WF[:, 2304 + 256 * q : 2560 + 256 * q], 1, 0)).astype(bf16)
    for q in range(4):
        GR[q] = mm(GBT[128 * q : 128 * (q + 1), :], POOLED[...], 1, 0).astype(bf16)
    gr_cp = [send(GR.at[(d + k) % 4], GRR.at[d], dpeer(k), t) for k in range(1, 4)]
    GRR[d] = GR[d]

    for cp in az_cp:
        cp.wait_recv()
    for k in range(3):
        grad_act += AZ[k].astype(f32)
    pooled_sum.add(0)
    high, low = split(grad_act * slot_live[t].astype(f32))
    grad_rows = mm(pool, high, 0, 0) + mm(pool, low, 0, 0)
    zi = ZI[...]
    gate = jax.nn.sigmoid(zi)
    dy = grad_rows * (gate * (1.0 + zi * (1.0 - gate)))
    xi = XI[...]
    dyx_inner = dy * xi
    gc = norm_rows_back(dy * gi, xi, RI[:, 0:1]).astype(bf16)
    GB[0:32, :] = jnp.zeros((32, 256), bf16)
    GB[800:832, :] = jnp.zeros((32, 256), bf16)
    GB[32:800, :] = gc
    back = mm(GB[64:832, :], WF[:, 0:768], 1, 0)
    back += mm(GB[32:800, :], WF[:, 768:1536], 1, 0)
    back += mm(GB[0:768, :], WF[:, 1536:2304], 1, 0)
    grad_hidden = pltpu.roll(back[:, 0:256], 767, 0) + back[:, 256:512] + pltpu.roll(back[:, 512:768], 1, 0)
    zm = ZM[...]
    gate = jax.nn.sigmoid(zm)
    inside = (lax.broadcasted_iota(jnp.int32, (768, 256), 0) & 31) < 24
    dy = jnp.where(inside, grad_hidden * (gate * (1.0 + zm * (1.0 - gate))), 0.0)
    xm = XM[...]
    dyx_middle = dy * xm
    gr = norm_rows_back(dy * gm, xm, RM[:, 0:1]).reshape(24, 32, 256)[:, 0:24, :].reshape(576, 256).astype(bf16)
    GA[t] = gr
    wg = jnp.sum(sums, axis=0, keepdims=True)
    grad_rounded = gr.astype(f32)
    s1 = jnp.sum(grad_rounded * wg, axis=1, keepdims=True)
    s2 = jnp.sum(grad_rounded * RED[:, 0:24, :].reshape(576, 256), axis=1, keepdims=True)
    lane = lax.broadcasted_iota(jnp.int32, (576, 128), 1)
    RSC[0:64, :] = jnp.zeros((64, 128), f32)
    RSC[576:640, :] = jnp.zeros((64, 128), f32)
    RSC[valid, :] = jnp.where(lane == 0, s1, s2) * (1.0 / 1024.0)
    row_sums = jnp.transpose(RSC[...])
    RS[t, 0:1, :] = mean
    RS[t, 1:2, :] = rstd
    RS[t, 2:4, :] = row_sums[0:2]
    rs_cp = [send(RS.at[t], RS.at[t], d, (t + k) % 8) for k in range(1, 8)]
    grad_gather = Gather(GA, 4)
    grad_gather.start(far_mid)
    grad_gather.start(partner)
    pooled_sum.start(2)
    grad_gather.own()
    pooled_sum.add(1)

    for cp in gr_cp:
        cp.wait_recv()
    total = GRR[0].astype(f32)
    for n in range(1, 4):
        total += GRR[n].astype(f32)
    GRF[d] = total.astype(bf16)
    grf_cp = [send(GRF.at[d], GRF.at[d], dpeer(k), t) for k in range(1, 4)]

    def put(lo, value):
        value = value.astype(bf16)
        for n in range(8):
            CG[n % 2, n // 2, :, lo : lo + value.shape[1]] = value[32 * n : 32 * (n + 1)]

    for a in range(3):
        put(768 * a, mm(gc, HB[32 * a : 32 * a + 768, :], 0, 0))
    ones = jnp.ones((768, 128), bf16)
    for lo, value in ((2304, dyx_inner), (2432, dyx_middle)):
        high, low = split(value)
        put(lo, mm(high, ones, 0, 0) + mm(low, ones, 0, 0))
    cg_cp = send(CG.at[1 - c], CGR, d, sib)

    cg_cp.wait_recv()
    CGS[...] = (CG[c].astype(f32) + CGR[...].astype(f32)).astype(bf16)
    cgd_cp = []
    for k in range(1, 4):
        dd = dpeer(k)
        cgd_cp.append(send(CGS.at[:, :, pl.ds(pl.multiple_of(640 * dd, 128), 640)], CGD.at[d], dd, t))
    CGD[d] = CGS[:, :, pl.ds(pl.multiple_of(640 * d, 128), 640)]

    for h in range(4):
        grad_gather.forward(far_mid, h)
    def turn(n):
        for k in range(1, 8):
            s = (t + k) % 8
            yield send(FT.at[n, pl.ds(pl.multiple_of(32 * s, 32), 32)], TA.at[n, d, t], d, s)
        TA[n, d, t] = FT[n, pl.ds(pl.multiple_of(32 * t, 32), 32), :]

    for cp in rs_cp:
        cp.wait_recv()
    w_own = WC[pl.ds(pl.multiple_of(128 * c, 128), 128), :]
    lane = lax.broadcasted_iota(jnp.int32, (4, 128), 1)
    gain_sum = jnp.zeros((128, 1), f32)
    grad_reduce = jnp.zeros((128, 256), f32)
    for n, p in enumerate(blocks):
        if n == 0:
            grad_gather.pass_on(1)
        if n == 1:
            for h in range(4):
                grad_gather.forward(far_end, h)
            grad_gather.pass_on(2)
            gp = pooled_sum.result(GP[...])
            gp_high, gp_low = split(gp)
            FT[0] = mm(act_live, gp_high, 0, 0).astype(bf16)
            turn_cp = list(turn(0))
            for m in range(4):
                cells = slice(288 * m, 288 * (m + 1))
                SP[:, 1152 * m : 1152 * (m + 1)] = mm(gp_high[cells], POOL[...], 0, 0) + mm(gp_low[cells], POOL[...], 0, 0)
            for cp in cgd_cp:
                cp.wait_recv()
            total = CGD[0].astype(f32)
            for m in range(1, 4):
                total += CGD[m].astype(f32)
            CGT[...] = total.astype(bf16)
            cgz_cp = [send(CGT.at[(z + k) % 4], CGZ.at[z], d, zpeer(k)) for k in range(1, 4)]
            CGZ[z] = CGT[z]
        if n == 3:
            for cp in turn_cp[0:7]:
                cp.wait_recv()
            ta_cp = [send(TA.at[0, d], TA.at[0, d], dpeer(k), t) for k in range(1, 4)]
            for cp in cgz_cp:
                cp.wait_recv()
            total = CGZ[0].astype(f32)
            for m in range(1, 4):
                total += CGZ[m].astype(f32)
            CGF[d] = total.astype(bf16)
            cgf_cp = [send(CGF.at[d], CGF.at[d], dpeer(k), t) for k in range(1, 4)]
            grad_gather.pass_on(3)
        grad_gather.ready(n)
        cols = pl.ds(pl.multiple_of(1152 * p, 128), 1152)
        even, odd = RS[2 * p], RS[2 * p + 1]
        stats = jnp.concatenate([even[:, 0:512], jnp.where(lane < 64, even[:, 512:640], odd[:, 0:128]), odd[:, 128:640]], axis=1)
        g = GA[pl.ds(2 * p, 2)].reshape(1152, 256)
        xhat = (PLC[:, cols] - stats[0:1]) * stats[1:2]
        grad_reduce += mm((xhat * go).astype(bf16), g, 1, 0)
        if n == 3:
            FT[1] = jnp.transpose(grad_reduce).astype(bf16)
            turn_cp += list(turn(1))
        gn = mm(w_own, g, 1, 1)
        gain_sum += jnp.sum(gn * xhat, axis=1, keepdims=True)
        GF[:, cols] = stats[1:2] * (gn * go - stats[2:3] - xhat * stats[3:4])
    place_sum = jnp.zeros((128, 1152), f32)
    for p in range(4):
        cols = slice(1152 * p, 1152 * (p + 1))
        out = GF[:, cols] + SP[:, cols]
        GF[:, cols] = out
        store(GF.at[:, cols], gfeat_o.at[:, cols])
        place_sum += out
    odd = pltpu.roll(place_sum, 576, 1)
    lane = lax.broadcasted_iota(jnp.int32, (128, 640), 1)
    place = jnp.where(lane < 576, place_sum[:, 0:640] + odd[:, 0:640], jnp.broadcast_to(gain_sum, (128, 640))).astype(bf16)
    for q in range(4):
        PM[q] = place[32 * q : 32 * (q + 1)]
    pm_cp = [send(PM.at[dpeer(k)], PR.at[d], dpeer(k), t) for k in range(1, 4)]
    PR[d] = PM[d]

    for cp in turn_cp[7:14]:
        cp.wait_recv()
    ta_cp += [send(TA.at[1, d], TA.at[1, d], dpeer(k), t) for k in range(1, 4)]
    for cp in pm_cp:
        cp.wait_recv()
    total = PR[0].astype(f32)
    for n in range(1, 4):
        total += PR[n].astype(f32)
    PF[d] = total.astype(bf16)
    pf_cp = [send(PF.at[d], PF.at[d], dpeer(k), t) for k in range(1, 4)]
    for cp in grf_cp:
        cp.wait_recv()
    for q in range(4):
        store(GRF.at[q], gread_o.at[pl.ds(128 * q, 128)])
    for cp in cgf_cp:
        cp.wait_recv()
    for q in range(4):
        gconv_o[:, 640 * q : 640 * (q + 1)] = CGF[q]
    for cp in ta_cp:
        cp.wait_recv()
    for n, out in enumerate((gexp_o, gred_o)):
        for s in range(8):
            total = TA[n, 0, s].astype(f32)
            for m in range(1, 4):
                total += TA[n, m, s].astype(f32)
            out[:, 128 * s : 128 * (s + 1)] = total
    for cp in pf_cp:
        cp.wait_recv()
    gpos_o[...] = jnp.transpose(PF[...].reshape(128, 640).astype(f32))
    for cp in result_cp:
        cp.wait()
    for cp in pending:
        cp.wait_send()
    placed_gather.drain()
    grad_gather.drain()


SCRATCH = (
    ("features", (128, 4608), bf16), ("position", (576, 128), f32), ("conv_weight", (9, 32, 256), bf16), ("expand_weight", (32, 1024), bf16), ("readout_weight", (512, 1024), bf16), ("cotangent", (512, 1152), bf16), ("RO", (512, 1152), bf16), ("GF", (128, 4608), f32), ("SP", (128, 4608), f32), ("WT", (256, 256), bf16), ("WC", (256, 256), bf16), ("CB", (32, 3584), bf16),
    ("WQ", (4, 32, 896), bf16), ("WB", (2, 4, 4, 32, 896), bf16), ("WF", (256, 3584), bf16), ("MT", (512, 256), bf16),
    ("POOL", (288, 1152), bf16), ("PLC", (128, 4608), f32), ("XW", (2, 4, 128, 640), bf16), ("XK", (4, 256, 640), bf16),
    ("ST", (8, 4, 640), f32), ("SR", (8, 4, 640), f32), ("QF", (640, 256), f32), ("QS", (3, 576, 256), bf16),
    ("QO", (576, 256), f32), ("QR", (4, 576, 256), bf16), ("RED", (24, 32, 256), f32), ("HB", (832, 768), bf16),
    ("GB", (832, 256), bf16), ("XM", (768, 256), f32), ("ZM", (768, 256), f32), ("RM", (768, 128), f32),
    ("XI", (768, 256), f32), ("ZI", (768, 256), f32), ("RI", (768, 128), f32), ("ACT", (8, 144, 256), bf16), ("ACL", (8, 144, 256), bf16),
    ("PP", (8, 1152, 128), bf16), ("POOLED", (1152, 1024), bf16), ("BEF", (512, 1152), f32), ("GBT", (512, 1152), bf16), ("GBR", (1152, 512), bf16),
    ("TE", (2, 4, 1152, 128), bf16), ("TR", (4, 1152, 128), bf16), ("ES", (3, 1152, 128), bf16), ("ER", (4, 1152, 128), bf16),
    ("GP", (1152, 128), f32), ("AT", (2, 4, 144, 256), bf16), ("AR", (4, 144, 256), bf16), ("AS", (3, 144, 256), bf16),
    ("AZ", (3, 144, 256), bf16), ("RSC", (640, 128), f32), ("GA", (8, 576, 256), bf16), ("RS", (8, 4, 640), f32),
    ("FT", (2, 256, 128), bf16), ("TA", (2, 4, 8, 32, 128), bf16), ("PM", (4, 32, 640), bf16),
    ("PR", (4, 32, 640), bf16), ("PF", (4, 32, 640), bf16),
    ("CG", (2, 4, 32, 2560), bf16), ("CGR", (4, 32, 2560), bf16), ("CGS", (4, 32, 2560), bf16), ("CGD", (4, 4, 32, 640), bf16),
    ("CGT", (4, 32, 640), bf16), ("CGZ", (4, 32, 640), bf16), ("CGF", (4, 32, 640), bf16), ("GR", (4, 128, 1024), bf16), ("GRR", (4, 128, 1024), bf16),
    ("GRF", (4, 128, 1024), bf16),
)


def finish(
    readout, gfeat, gpos, gexp, gred, gconv, gread, readout_o, gfeat_o, gpos_o, ggo_o, gred_o, ggm_o, gconv_o, ggi_o, gexp_o, gread_o,
    RO, GF, GB, GC, GR, GP, GQ, GE, GD, sem,
):
    copies = []

    def copy(src, dst):
        cp = pltpu.make_async_copy(src, dst, sem.at[len(copies)])
        copies.append(cp)
        cp.start()
        return cp

    loads = [copy(gread.at[pl.ds(256 * p, 256)], GB.at[pl.ds(256 * p, 256)]) for p in range(2)]
    loads += [copy(gfeat.at[pl.ds(32 * p, 32)], GF.at[pl.ds(32 * p, 32)]) for p in range(4)]
    loads += [copy(readout, RO), copy(gconv, GC), copy(gpos, GP), copy(gexp, GE), copy(gred, GD)]
    stores = []
    for p in range(2):
        rows = pl.ds(256 * p, 256)
        loads[p].wait()
        GR[rows, :] = GB[rows, :].astype(f32)
        stores.append(copy(GR.at[rows], gread_o.at[rows]))
    for p in range(4):
        rows = pl.ds(32 * p, 32)
        loads[2 + p].wait()
        stores.append(copy(GF.at[rows], gfeat_o.at[rows]))
    loads[6].wait()
    stores.append(copy(RO, readout_o))
    loads[7].wait()
    for n in range(9):
        GQ[n] = GC[:, 256 * n : 256 * (n + 1)].astype(f32)
    stores.append(copy(GQ, gconv_o))
    first = (lax.broadcasted_iota(jnp.int32, (8, 128), 1) == 0).astype(f32).astype(bf16)
    ggi_o[...] = mm(first, GC[:, 2304:2432], 1, 1)[0:1]
    ggm_o[...] = mm(first, GC[:, 2432:2560], 1, 1)[0:1]
    loads[8].wait()
    stores.append(copy(GP.at[pl.ds(0, 576)], gpos_o))
    ggo_o[...] = GP[576:577, :]
    loads[9].wait()
    stores.append(copy(GE, gexp_o))
    loads[10].wait()
    stores.append(copy(GD, gred_o))
    for cp in stores:
        cp.wait()


def local_by_image(features, slot_live, position, gain_outer, reduce_weight, gain_middle, conv_weight, gain_inner, expand_weight, readout_weight, cotangent):
    vmem = pl.BlockSpec(memory_space=pltpu.VMEM)
    smem = pl.BlockSpec(memory_space=pltpu.SMEM)
    hbm = pl.BlockSpec(memory_space=pl.ANY)

    def shapes(*pairs):
        return tuple(jax.ShapeDtypeStruct(shape, dtype) for shape, dtype in pairs)

    parts = pl.pallas_call(
        kernel,
        out_shape=shapes(
            ((512, 1152), bf16), ((128, 4608), f32), ((640, 128), f32), ((32, 1024), f32), ((32, 1024), f32), ((32, 2560), bf16), ((512, 1024), bf16)
        ),
        in_specs=[hbm, smem, hbm, vmem, vmem, vmem, hbm, vmem, hbm, hbm, hbm],
        out_specs=[hbm, hbm, vmem, vmem, vmem, vmem, hbm],
        scratch_shapes=[pltpu.VMEM(shape, dtype) for _, shape, dtype in SCRATCH]
        + [pltpu.SemaphoreType.DMA((COPIES,)), pltpu.SemaphoreType.DMA((COPIES,)), pltpu.SemaphoreType.DMA((24,))],
        compiler_params=pltpu.CompilerParams(collective_id=0, has_side_effects=True, vmem_limit_bytes=60 * 2**20),
    )(
        features, slot_live, position.reshape(576, 128), gain_outer.reshape(1, 128), reduce_weight.T, gain_middle.reshape(1, 32),
        conv_weight.transpose(0, 1, 3, 2).reshape(9, 32, 256), gain_inner.reshape(1, 32), expand_weight, readout_weight, cotangent,
    )
    readout, gfeat, gpos, ggo, gred, ggm, gconv, ggi, gexp, gread = pl.pallas_call(
        finish,
        out_shape=shapes(
            ((512, 1152), bf16), ((128, 4608), f32), ((576, 128), f32), ((1, 128), f32), ((32, 1024), f32), ((1, 32), f32),
            ((9, 32, 256), f32), ((1, 32), f32), ((32, 1024), f32), ((512, 1024), f32),
        ),
        in_specs=[hbm] * 7,
        out_specs=[hbm, hbm, hbm, vmem, hbm, vmem, hbm, vmem, hbm, hbm],
        scratch_shapes=[
            pltpu.VMEM((512, 1152), bf16), pltpu.VMEM((128, 4608), f32), pltpu.VMEM((512, 1024), bf16), pltpu.VMEM((32, 2560), bf16),
            pltpu.VMEM((512, 1024), f32), pltpu.VMEM((640, 128), f32), pltpu.VMEM((9, 32, 256), f32), pltpu.VMEM((32, 1024), f32),
            pltpu.VMEM((32, 1024), f32), pltpu.SemaphoreType.DMA((24,)),
        ],
        compiler_params=pltpu.CompilerParams(vmem_limit_bytes=60 * 2**20),
    )(*parts)
    return (
        readout, gfeat, gpos.reshape(24, 24, 128), ggo.reshape(128), gred.T, ggm.reshape(32),
        gconv.reshape(3, 3, 32, 256).transpose(0, 1, 3, 2), ggi.reshape(32), gexp, gread,
    )


def row_totals(leading, trailing):
    return lax.psum((leading, trailing), "tensor")


def norm_forward(values, norm_gain, breadth):
    totals, squares = row_totals(jnp.sum(values, axis=1), jnp.sum(values * values, axis=1))
    center = totals / breadth
    spread = squares / breadth - center * center
    scaled = lax.rsqrt(spread + epsilon)[:, None]
    normed = (values - center[:, None]) * scaled
    return (normed, scaled, normed * norm_gain)


def norm_backward(grad_out, normed, scaled, norm_gain, breadth):
    grad_normed = grad_out * norm_gain
    gain_grad = jnp.sum(grad_out * normed, axis=0)
    leading, trailing = row_totals(
        jnp.sum(grad_normed, axis=1), jnp.sum(grad_normed * normed, axis=1)
    )
    grad_in = scaled * (
        grad_normed - leading[:, None] / breadth - normed * (trailing[:, None] / breadth)
    )
    return (grad_in, gain_grad)


def silu_grad(inputs):
    gate_value = jax.nn.sigmoid(inputs)
    return gate_value * (1.0 + inputs * (1.0 - gate_value))


def gelu_grad(inputs):
    below = 0.5 * (1.0 + lax.erf(inputs * 0.7071067811865476))
    density = jnp.exp(-0.5 * inputs * inputs) * 0.3989422804014327
    return below + inputs * density


def contract_rows(left_side, right_side):
    return lax.dot_general(
        left_side, right_side, (((0,), (0,)), ((), ())), preferred_element_type=jnp.float32
    )


def window_of(padded, shift_down, shift_across, grid_side):
    images = padded.shape[0]
    breadth = padded.shape[3]
    return padded[
        :, shift_down : shift_down + grid_side, shift_across : shift_across + grid_side, :
    ].reshape(images * grid_side * grid_side, breadth)


def local_by_hidden(
    features,
    slot_live,
    position,
    gain_outer,
    reduce_weight,
    gain_middle,
    conv_weight,
    gain_inner,
    expand_weight,
    readout_weight,
    cotangent,
):
    grid_side = position.shape[0]
    half_side = grid_side // 2
    channel_share = features.shape[0]
    row_count = features.shape[1]
    images = row_count // (grid_side * grid_side)
    tensor_size = lax.axis_size("tensor")
    channels = channel_share * tensor_size
    hidden_share = reduce_weight.shape[1]
    hidden_width = hidden_share * tensor_size
    pooled_count = images * half_side * half_side
    placed = (
        features.T.astype(jnp.float32).reshape(images, grid_side * grid_side, channel_share)
        + position.reshape(1, grid_side * grid_side, channel_share)
    ).reshape(row_count, channel_share)
    live_rows = jnp.repeat(slot_live.astype(jnp.float32), grid_side * grid_side)[:, None]
    normed_outer, scaled_outer, shaped_outer = norm_forward(placed, gain_outer, channels)
    reduce_in = shaped_outer.astype(jnp.bfloat16)
    reduce_full = lax.all_gather(reduce_in, "tensor", axis=1, tiled=True)
    reduced = jnp.dot(reduce_full, reduce_weight, preferred_element_type=jnp.float32)
    normed_middle, scaled_middle, shaped_middle = norm_forward(reduced, gain_middle, hidden_width)
    hidden = jax.nn.silu(shaped_middle).astype(jnp.bfloat16)
    hidden_full = lax.all_gather(hidden, "tensor", axis=1, tiled=True)
    padded_hidden = jnp.pad(
        hidden_full.reshape(images, grid_side, grid_side, hidden_width),
        ((0, 0), (1, 1), (1, 1), (0, 0)),
    )
    convolved = jnp.zeros((row_count, hidden_share), jnp.float32)
    for offset_tap in range(9):
        shift_down = offset_tap // 3
        shift_across = offset_tap % 3
        convolved = convolved + jnp.dot(
            window_of(padded_hidden, shift_down, shift_across, grid_side),
            conv_weight[shift_down, shift_across],
            preferred_element_type=jnp.float32,
        )
    normed_inner, scaled_inner, shaped_inner = norm_forward(convolved, gain_inner, hidden_width)
    activated = jax.nn.silu(shaped_inner).astype(jnp.bfloat16)
    expand_terms = jnp.dot(activated, expand_weight, preferred_element_type=jnp.float32)
    expanded = lax.psum_scatter(expand_terms, "tensor", scatter_dimension=1, tiled=True)
    mixed = placed + live_rows * expanded
    pooled = jnp.mean(mixed.reshape(images, half_side, 2, half_side, 2, channel_share), axis=(2, 4))
    pooled_low = pooled.reshape(pooled_count, channel_share).astype(jnp.bfloat16)
    pooled_full = lax.all_gather(pooled_low, "tensor", axis=1, tiled=True)
    before = lax.dot_general(
        pooled_full, readout_weight, (((1,), (1,)), ((), ())), preferred_element_type=jnp.float32
    )
    readout = jax.nn.gelu(before, approximate=False).astype(jnp.bfloat16).T
    grad_before = (cotangent.T.astype(jnp.float32) * gelu_grad(before)).astype(jnp.bfloat16)
    grad_readout = contract_rows(grad_before, pooled_full)
    pooled_terms = jnp.dot(grad_before, readout_weight, preferred_element_type=jnp.float32)
    grad_pooled = lax.psum_scatter(pooled_terms, "tensor", scatter_dimension=1, tiled=True)
    spread_grad = jnp.broadcast_to(
        (0.25 * grad_pooled).reshape(images, half_side, 1, half_side, 1, channel_share),
        (images, half_side, 2, half_side, 2, channel_share),
    )
    grad_mixed = spread_grad.reshape(row_count, channel_share)
    grad_branch = (live_rows * grad_mixed).astype(jnp.bfloat16)
    grad_full = lax.all_gather(grad_branch, "tensor", axis=1, tiled=True)
    grad_expand = contract_rows(activated, grad_full)
    grad_activated = jnp.dot(grad_full, expand_weight.T, preferred_element_type=jnp.float32)
    grad_convolved, grad_gain_inner = norm_backward(
        grad_activated * silu_grad(shaped_inner),
        normed_inner,
        scaled_inner,
        gain_inner,
        hidden_width,
    )
    grad_conv_low = grad_convolved.astype(jnp.bfloat16)
    tap_grads = []
    grad_padded = jnp.zeros((images, grid_side + 2, grid_side + 2, hidden_width), jnp.float32)
    for offset_tap in range(9):
        shift_down = offset_tap // 3
        shift_across = offset_tap % 3
        tap_grads.append(
            contract_rows(
                window_of(padded_hidden, shift_down, shift_across, grid_side), grad_conv_low
            )
        )
        tap_back = jnp.dot(
            grad_conv_low,
            conv_weight[shift_down, shift_across].T,
            preferred_element_type=jnp.float32,
        )
        grad_padded = grad_padded + jnp.pad(
            tap_back.reshape(images, grid_side, grid_side, hidden_width),
            ((0, 0), (shift_down, 2 - shift_down), (shift_across, 2 - shift_across), (0, 0)),
        )
    grad_conv = jnp.stack(tap_grads, axis=0).reshape(conv_weight.shape)
    grad_window = grad_padded[:, 1 : grid_side + 1, 1 : grid_side + 1, :].reshape(
        row_count, hidden_width
    )
    grad_hidden = lax.psum_scatter(grad_window, "tensor", scatter_dimension=1, tiled=True)
    grad_reduced, grad_gain_middle = norm_backward(
        grad_hidden * silu_grad(shaped_middle),
        normed_middle,
        scaled_middle,
        gain_middle,
        hidden_width,
    )
    grad_reduced_low = grad_reduced.astype(jnp.bfloat16)
    grad_reduce = contract_rows(reduce_full, grad_reduced_low)
    outer_terms = jnp.dot(grad_reduced_low, reduce_weight.T, preferred_element_type=jnp.float32)
    grad_shaped_outer = lax.psum_scatter(outer_terms, "tensor", scatter_dimension=1, tiled=True)
    grad_inputs, grad_gain_outer = norm_backward(
        grad_shaped_outer, normed_outer, scaled_outer, gain_outer, channels
    )
    grad_rows = grad_mixed + grad_inputs
    grad_place = jnp.sum(grad_rows.reshape(images, grid_side, grid_side, channel_share), axis=0)
    grad_total = grad_rows.T
    summed = (
        lax.psum(grad_place.astype(jnp.bfloat16), "dp").astype(jnp.float32),
        lax.psum(grad_gain_outer.astype(jnp.bfloat16), "dp").astype(jnp.float32),
        lax.psum(grad_reduce.astype(jnp.bfloat16), "dp").astype(jnp.float32),
        lax.psum(grad_gain_middle.astype(jnp.bfloat16), "dp").astype(jnp.float32),
        lax.psum(grad_conv.astype(jnp.bfloat16), "dp").astype(jnp.float32),
        lax.psum(grad_gain_inner.astype(jnp.bfloat16), "dp").astype(jnp.float32),
        lax.psum(grad_expand.astype(jnp.bfloat16), "dp").astype(jnp.float32),
        lax.psum(grad_readout.astype(jnp.bfloat16), "dp").astype(jnp.float32),
    )
    return (
        readout,
        grad_total,
        summed[0],
        summed[1],
        summed[2],
        summed[3],
        summed[4],
        summed[5],
        summed[6],
        summed[7],
    )


def solution(mesh):
    parts, groups = mesh.shape["tensor"], mesh.shape["dp"]
    specs = (P("tensor", "dp"), P("dp"), P(None, None, "tensor"), P("tensor"), P(None, "tensor"), P("tensor"), P(None, None, None, "tensor"), P("tensor"), P("tensor", None), P("tensor", None), P("tensor", "dp"))

    def whole(*arrays):
        by_image = (parts, groups) == (8, 4) and arrays[1].shape[0] == parts * groups
        return jax.shard_map(
            local_by_image if by_image else local_by_hidden, mesh=mesh, in_specs=specs,
            out_specs=(P("tensor", "dp"), P("tensor", "dp"), *specs[2:10]), check_vma=False,
        )(*arrays)

    return whole
```
